128 devices in a mesh: member: 8 (over x_lo, z), space: 16 (over y, x_hi, core).
Axes of the slice: x: 4 (x_hi: 2, x_lo: 2; x = x_hi * 2 + x_lo), y: 4, z: 4, core: 2. Of those that a mesh axis runs over, the one named last changes fastest.
Arguments:
- initial_ensemble: float32 [64, 6, 128, 512], P('member', None, 'space'), may hold values from -6 to 6
- obs_value: float32 [16, 2048], P('space'), may hold values from -6 to 6
- obs_error: float32 [16, 2048], P('space'), may hold values from 0.25 to 4
- obs_location: int32 [16, 2048], P('space'), may hold values from 0 to 24575, as said below
- patch_obs: int32 [16, 512, 64], P('space', 'member'), may hold values from 0 to 2047, as said below
- cotangent: float32 [64, 6, 128, 512], P('member', None, 'space'), may hold values from -6 to 6
Outputs:
- analysis: float32 [64, 6, 128, 512], P('member', None, 'space')
- gradient: float32 [64, 6, 128, 512], P('member', None, 'space')
The draws below stay inside these ranges and needn't reach their ends.
Inputs may be any that keep to these rules, and one draw needn't show every extreme that they name: `obs_location`: observation j of a tile lies in column (j * 512) // 2048; observation 0 lies at cell 0 and observation 2048 - 1 at cell 6 * 8 * 512 - 1. `patch_obs`: entry q of patch p is (((8 c + 3) * 2048) // 1024 + e) mod 2048 with c = p // 4 and -(32) <= e <= 32; entries may repeat.
All inputs are finite; a program needn't handle non-finite values.
Results may differ from the reference program's by a relative error of at most 0.0003.
Values sent between devices are 32-bit elements; how exact they have to be, the bound alone decides.
No kernel may reach another device: no remote copies, remote signals or barrier semaphores. Data moves between devices by JAX's collectives and lax.ppermute only.
A program may use at most 192 MiB of HBM per device.

```python
import math
import jax
import jax.numpy as jnp
from jax import lax

FIELDS = 3
LEV = 2
STACK_QUANTITIES = 6
MEM_DEV = 8
SAMPLE_TOTAL = 64
SUBDOMAIN_HEIGHT = 8
MESH_WIDTH = 512
SUBDOMAIN_TOTAL = 16
MESH_HEIGHT = 128
NOBS = 2048
POBS = 64
PATCHES = 512
LOC_R = 8
NS_ITERS = 4
STEPS = 1


def draw_obs_location(key, part):
    key_var, key_row, key_col = jax.random.split(key, 3)
    obs_ids = jnp.arange(NOBS, dtype=jnp.int32)[None, :]
    variable = jax.random.randint(key_var, (SUBDOMAIN_TOTAL, NOBS), 0, STACK_QUANTITIES)
    row_pick = jax.random.randint(key_row, (SUBDOMAIN_TOTAL, NOBS), 0, SUBDOMAIN_HEIGHT)
    jitter = jax.random.randint(key_col, (SUBDOMAIN_TOTAL, NOBS), 0, max(MESH_WIDTH // NOBS, 1))
    column = obs_ids * MESH_WIDTH // NOBS + jitter
    flat_cell = variable * (SUBDOMAIN_HEIGHT * MESH_WIDTH) + row_pick * MESH_WIDTH + column
    flat_cell = jnp.where(obs_ids == 0, 0, flat_cell)
    flat_cell = jnp.where(obs_ids == NOBS - 1, STACK_QUANTITIES * SUBDOMAIN_HEIGHT * MESH_WIDTH - 1, flat_cell)
    return flat_cell.astype(jnp.int32)


def draw_patch_obs(key, part):
    patch_ids = jnp.arange(PATCHES, dtype=jnp.int32)[None, :, None]
    column_pair = patch_ids // (SUBDOMAIN_HEIGHT // 2)
    centre_obs = (8 * column_pair + 3) * NOBS // (2 * MESH_WIDTH)
    offsets = jax.random.randint(key, (SUBDOMAIN_TOTAL, PATCHES, POBS), -(POBS // 2), POBS // 2 + 1)
    return ((centre_obs + offsets) % NOBS).astype(jnp.int32)


def steps_of(key, extent, pieces, smallest, high):
    def one(axis_at, blocks):
        steps = jax.random.uniform(jax.random.fold_in(jax.random.fold_in(key, 6), axis_at), (blocks,), jnp.float32, smallest / len(pieces), high / len(pieces))
        return jnp.repeat(jnp.exp(steps), extent[axis_at] // blocks).reshape((-1,) + (1,) * (len(extent) - axis_at - 1))

    gain = one(*pieces[0])
    for cut in pieces[1:]:
        gain = gain * one(*cut)
    return gain


def centred(own_key, extent, scale, reach, pieces=(), kind=jnp.bfloat16):
    array = jax.random.normal(own_key, extent, jnp.float32) * scale
    if len(pieces) > 0:
        array = steps_of(own_key, extent, pieces, -0.22, 0.18) * array
    return jnp.clip(array, min=-reach, max=reach).astype(kind)


def setup_inputs(seed: int = 0) -> dict:
    splits = jax.random.split(jax.random.key(seed), 7)
    initial_ensemble = centred(splits[0], (SAMPLE_TOTAL, STACK_QUANTITIES, MESH_HEIGHT, MESH_WIDTH), 1.0, 6.0, ((0, 8), (2, 16)), jnp.float32)
    obs_value = centred(splits[1], (SUBDOMAIN_TOTAL, NOBS), 1.0, 6.0, ((0, 16),), jnp.float32)
    obs_error = jnp.clip(jnp.exp(math.log(4.0) - 2.7725887 * jax.random.uniform(splits[2], (SUBDOMAIN_TOTAL, NOBS), jnp.float32) ** steps_of(splits[2], (SUBDOMAIN_TOTAL, NOBS), ((0, 16),), -0.2, 0.2)), 0.25, 4.0)
    obs_location = draw_obs_location(jax.random.fold_in(splits[6], 71), 0)
    patch_obs = draw_patch_obs(jax.random.fold_in(splits[6], 71), 0)
    cotangent = centred(splits[5], (SAMPLE_TOTAL, STACK_QUANTITIES, MESH_HEIGHT, MESH_WIDTH), 1.0, 6.0, ((0, 8), (2, 16)), jnp.float32)
    return dict(initial_ensemble=initial_ensemble, obs_value=obs_value, obs_error=obs_error, obs_location=obs_location, patch_obs=patch_obs, cotangent=cotangent)


time_step = 0.2
coriolis = 0.5
stratification = 1.0
mixing = 0.3
highest = lax.Precision.HIGHEST

def row_diff(padded):
    return (padded[..., :-4, :] - 8.0 * padded[..., 1:-3, :] + 8.0 * padded[..., 3:-1, :] - padded[..., 4:, :]) / 12.0

def col_diff(field):
    return (jnp.roll(field, 2, axis=-1) - 8.0 * jnp.roll(field, 1, axis=-1) + 8.0 * jnp.roll(field, -1, axis=-1) - jnp.roll(field, -2, axis=-1)) / 12.0

def tendency(padded):
    members = padded.shape[0]
    layered = padded.reshape(members, FIELDS, LEV, padded.shape[2], padded.shape[3])
    interior = layered[:, :, :, 2:-2, :]
    along_rows = row_diff(layered)
    along_cols = col_diff(interior)
    speed_u = interior[:, 0]
    speed_v = interior[:, 1]
    carried = speed_u[:, None] * along_rows + speed_v[:, None] * along_cols
    rate_u = -carried[:, 0] + coriolis * speed_v - along_rows[:, 2]
    rate_v = -carried[:, 1] - coriolis * speed_u - along_cols[:, 2]
    rate_b = -carried[:, 2] - stratification * (along_rows[:, 0] + along_cols[:, 1])
    rates = jnp.stack([rate_u, rate_v, rate_b], axis=1)
    above = jnp.concatenate([interior[:, :, 1:], interior[:, :, -1:]], axis=2)
    below = jnp.concatenate([interior[:, :, :1], interior[:, :, :-1]], axis=2)
    rates = rates + mixing * (above - 2.0 * interior + below)
    return rates.reshape(members, FIELDS * LEV, interior.shape[3], interior.shape[4])

def wrap_rows(grid):
    return jnp.concatenate([grid[:, :, -2:], grid, grid[:, :, :2]], axis=2)

def propagate_dynamics(group):
    for step_count in range(STEPS):
        first_rate = tendency(wrap_rows(group))
        middle = group + time_step * first_rate
        second_rate = tendency(wrap_rows(middle))
        group = group + 0.5 * time_step * (first_rate + second_rate)
    return group

def analyse(ensemble, obs_ens, obs_values, obs_errors, obs_cells, patch_lists, first_col):
    members = ensemble.shape[0]
    variables = ensemble.shape[1]
    tile_rows = ensemble.shape[2]
    columns = ensemble.shape[3]
    half_rows = tile_rows // 2
    quads = columns // 4
    patch_count = half_rows * quads
    patch_ids = jnp.arange(patch_count, dtype=jnp.int32)
    patch_col = patch_ids // half_rows
    patch_row = patch_ids % half_rows
    picked = obs_ens[:, patch_lists]
    mean_obs = lax.optimization_barrier(jnp.mean(picked, axis=0))
    spread = picked - mean_obs
    innovation = obs_values[patch_lists] - mean_obs
    located = obs_cells[patch_lists]
    obs_row = located // MESH_WIDTH % SUBDOMAIN_HEIGHT
    obs_col = located % MESH_WIDTH
    row_gap = (obs_row - 2 * patch_row[:, None]).astype(jnp.float32) - 0.5
    col_shift = obs_col - 4 * (patch_col[:, None] + first_col // 4)
    col_shift = (col_shift + MESH_WIDTH // 2) % MESH_WIDTH - MESH_WIDTH // 2
    col_gap = col_shift.astype(jnp.float32) - 1.5
    weight = jnp.exp(-(row_gap * row_gap + col_gap * col_gap) / (2.0 * LOC_R * LOC_R)) / obs_errors[patch_lists]
    scaled = spread * weight
    identity = jnp.eye(members, dtype=jnp.float32)
    gram = (members - 1.0) * identity + jnp.einsum('kpq,jpq->pkj', scaled, spread, precision=highest)
    scale = jnp.sqrt(lax.optimization_barrier(jnp.sum(gram * gram, axis=(1, 2))))
    root_iter = gram / scale[:, None, None]
    inverse_root = jnp.broadcast_to(identity, gram.shape)
    for sweep in range(NS_ITERS):
        factor = 1.5 * identity - 0.5 * jnp.einsum('pij,pjk->pik', inverse_root, root_iter, precision=highest)
        root_iter = jnp.einsum('pij,pjk->pik', root_iter, factor, precision=highest)
        inverse_root = jnp.einsum('pij,pjk->pik', factor, inverse_root, precision=highest)
    forcing = jnp.einsum('kpq,pq->pk', scaled, innovation, precision=highest)
    half_way = jnp.einsum('pij,pj->pi', inverse_root, forcing, precision=highest)
    mean_weight = jnp.einsum('pij,pj->pi', inverse_root, half_way, precision=highest) / scale[:, None]
    weights = jnp.sqrt(members - 1.0) * inverse_root / jnp.sqrt(scale)[:, None, None] + mean_weight[:, :, None]
    patch_cells = ensemble.reshape(members, variables, half_rows, 2, quads, 4).transpose(4, 2, 0, 1, 3, 5)
    patch_cells = patch_cells.reshape(patch_count, members, variables * 8)
    centre = lax.optimization_barrier(jnp.mean(patch_cells, axis=1, keepdims=True))
    anomaly = patch_cells - centre
    updated = centre + jnp.einsum('pkc,pkj->pjc', anomaly, weights, precision=highest)
    updated = updated.reshape(quads, half_rows, members, variables, 2, 4).transpose(2, 3, 1, 4, 0, 5)
    return updated.reshape(members, variables, tile_rows, columns)

def reference(initial_ensemble, obs_value, obs_error, obs_location, patch_obs, cotangent):

    def whole(initial):
        subdomain_batches = initial.reshape(SAMPLE_TOTAL // MEM_DEV, MEM_DEV, STACK_QUANTITIES, MESH_HEIGHT, MESH_WIDTH)
        predicted_samples = lax.map(jax.checkpoint(propagate_dynamics), subdomain_batches).reshape(SAMPLE_TOTAL, STACK_QUANTITIES, MESH_HEIGHT, MESH_WIDTH)
        subdomain_slices = predicted_samples.reshape(SAMPLE_TOTAL, STACK_QUANTITIES, SUBDOMAIN_TOTAL, SUBDOMAIN_HEIGHT, MESH_WIDTH).transpose(2, 0, 1, 3, 4)

        def one_tile(inputs):
            tile_state, tile_values, tile_errors, tile_cells, tile_lists = inputs
            tile_obs = tile_state.reshape(SAMPLE_TOTAL, -1)[:, tile_cells]
            return analyse(tile_state, tile_obs, tile_values, tile_errors, tile_cells, tile_lists, 0)
        analysed = lax.map(jax.checkpoint(one_tile), (subdomain_slices, obs_value, obs_error, obs_location, patch_obs))
        return analysed.transpose(1, 2, 0, 3, 4).reshape(SAMPLE_TOTAL, STACK_QUANTITIES, MESH_HEIGHT, MESH_WIDTH)
    analysis, pullback = jax.vjp(whole, initial_ensemble)
    gradient = pullback(cotangent)[0]
    return (analysis, gradient)
```

```python
import functools
import math

import jax
import jax.numpy as jnp
from jax import lax
from jax.experimental import pallas as pl
from jax.experimental.pallas import tpu as pltpu
from jax.sharding import PartitionSpec as P

VARS = 6
ROWS = 8
COLS = 512
MEMBERS = 64
PER_DEV = 8
STRIDE = VARS * ROWS
NOBS = 2048
WINDOW = 80
LOCAL_OBS = 320
QUADS = 16
LOC_R = 8

time_step = 0.2
f32 = jnp.float32
bf16 = jnp.bfloat16
VMEM_LIMIT = 50 * 1024 * 1024


def call(kernel, outs, scratch, flops, moved, *args):
    spec = pl.BlockSpec(memory_space=pltpu.VMEM)
    return pl.pallas_call(
        kernel,
        out_shape=[jax.ShapeDtypeStruct(s, f32) for s in outs],
        in_specs=[spec] * len(args),
        out_specs=[spec] * len(outs),
        scratch_shapes=scratch,
        compiler_params=pltpu.CompilerParams(vmem_limit_bytes=VMEM_LIMIT),
        cost_estimate=pl.CostEstimate(flops=flops, bytes_accessed=moved, transcendentals=0),
    )(*args)


def lane_shift(q, by):
    return pltpu.roll(q, by % COLS, 1)


def col_diff(q):
    near = lane_shift(q, -1) - lane_shift(q, 1)
    far = lane_shift(q, -2) - lane_shift(q, 2)
    return near * (8.0 / 12.0) - far * (1.0 / 12.0)


def row_diff(ref, v, i):
    near = ref[v, i + 1] - ref[v, i - 1]
    far = ref[v, i + 2] - ref[v, i - 2]
    return near * (8.0 / 12.0) - far * (1.0 / 12.0)


def tendency(ref, i):
    rates = [None] * VARS
    for l in range(2):
        u, v, b = ref[l, i], ref[2 + l, i], ref[4 + l, i]
        ru, rv, rb = (row_diff(ref, k + l, i) for k in (0, 2, 4))
        cu, cv, cb = col_diff(u), col_diff(v), col_diff(b)
        rates[l] = 0.5 * v - (u * ru + v * cu) - rb + 0.3 * (ref[1 - l, i] - u)
        rates[2 + l] = -0.5 * u - (u * rv + v * cv) - cb + 0.3 * (ref[3 - l, i] - v)
        rates[4 + l] = -(u * rb + v * cb) - (ru + cv) + 0.3 * (ref[5 - l, i] - b)
    return rates


def planes_of(x_ref, v):
    return jnp.swapaxes(x_ref[:, v], 0, 1)


def edge_kernel(x_ref, first_ref, last_ref):
    for v in range(VARS):
        planes = planes_of(x_ref, v)
        first_ref[4 * v : 4 * v + 4] = planes[:4]
        last_ref[4 * v : 4 * v + 4] = planes[4:]


def pack_planes(even, odd, store):
    low = lax.broadcasted_iota(jnp.int32, (PER_DEV, 128), 1) < 64
    for t in range(4):
        a, b = even[:, 128 * t : 128 * t + 128], odd[:, 128 * t : 128 * t + 128]
        store(2 * t, jnp.where(low, a, pltpu.roll(b, 64, 1)))
        store(2 * t + 1, jnp.where(low, pltpu.roll(a, 64, 1), b))


def unpack_planes(load):
    low = lax.broadcasted_iota(jnp.int32, (PER_DEV, 128), 1) < 64
    even, odd = [], []
    for t in range(4):
        a, b = load(2 * t), load(2 * t + 1)
        even.append(jnp.where(low, a, pltpu.roll(b, 64, 1)))
        odd.append(jnp.where(low, pltpu.roll(a, 64, 1), b))
    return jnp.concatenate(even, axis=1), jnp.concatenate(odd, axis=1)


def cot_kernel(x_ref, out_ref):
    for v in range(VARS):
        planes = planes_of(x_ref, v)
        for r in range(4):

            def store(d, value, t=v * 4 + r):
                out_ref[d, t] = value

            pack_planes(planes[2 * r], planes[2 * r + 1], store)


def load_state(s_ref, x_ref, top_ref, bot_ref):
    for v in range(VARS):
        s_ref[v, 4:12] = planes_of(x_ref, v)
        for r in range(4):
            s_ref[v, r] = top_ref[v * 4 + r]
            s_ref[v, 12 + r] = bot_ref[v * 4 + r]


def forward_kernel(
    x_ref, top_ref, bot_ref, sel_ref, out_ref, mid_ref, first_ref, last_ref, s_ref, fore_ref
):
    load_state(s_ref, x_ref, top_ref, bot_ref)

    def middle(i, carry):
        rates = tendency(s_ref, i + 2)
        for v in range(VARS):
            mid_ref[v, i] = s_ref[v, i + 2] + time_step * rates[v]
        return carry

    lax.fori_loop(0, 12, middle, 0)

    def finish(i, carry):
        rates = tendency(mid_ref, i + 2)
        for v in range(VARS):
            fore_ref[v, i] = 0.5 * (s_ref[v, i + 4] + mid_ref[v, i + 2]) + 0.5 * time_step * rates[v]
        return carry

    lax.fori_loop(0, ROWS, finish, 0)

    for v in range(VARS):
        for r in range(2):
            first_ref[v * 2 + r] = mid_ref[v, 4 + r]
            last_ref[v * 2 + r] = mid_ref[v, 6 + r]

    def pack(v, carry):
        for r in range(4):

            def store(d, value, r=r):
                out_ref[d, v * 4 + r] = value

            pack_planes(fore_ref[v, 2 * r], fore_ref[v, 2 * r + 1], store)
        return carry

    lax.fori_loop(0, VARS, pack, 0)

    for o in range(4):
        chosen = jnp.broadcast_to(sel_ref[o : o + 1, :], (PER_DEV, COLS))

        def pick(v, acc, chosen=chosen):
            for r in range(ROWS):
                acc = jnp.where(chosen == v * ROWS + r, fore_ref[v, r], acc)
            return acc

        seen = lax.fori_loop(0, VARS, pick, jnp.zeros((PER_DEV, COLS), f32))
        for d in range(8):
            out_ref[d, 24 + o] = lane_shift(seen, 8 - 64 * d)[:, :128]


def collect_kernel(got_ref, sel_ref, g_ref, first_ref, last_ref):
    lane = lax.broadcasted_iota(jnp.int32, (PER_DEV, 128), 1)
    sums, chosen = [], []
    for o in range(4):
        total = jnp.zeros((PER_DEV, COLS), f32)
        for d in range(8):
            piece = jnp.where(lane < WINDOW, got_ref[d, 24 + o], 0.0)
            wide = jnp.concatenate([piece, jnp.zeros((PER_DEV, COLS - 128), f32)], axis=1)
            total = total + lane_shift(wide, 64 * d - 8)
        sums.append(total)
        chosen.append(jnp.broadcast_to(sel_ref[o : o + 1, :], (PER_DEV, COLS)))

    for v in range(VARS):
        for r in range(4):
            pair = unpack_planes(lambda d: got_ref[d, v * 4 + r])
            for k in range(2):
                row = 2 * r + k
                value = pair[k]
                for o in range(4):
                    value = value + jnp.where(chosen[o] == v * ROWS + row, sums[o], 0.0)
                g_ref[v * ROWS + row] = value
                if row < 4:
                    first_ref[v * 4 + row] = value
                else:
                    last_ref[v * 4 + row - 4] = value


def place_kernel(got_ref, out_ref):
    for v in range(VARS):
        planes = []
        for r in range(4):
            planes.extend(unpack_planes(lambda d: got_ref[d, v * 4 + r]))
        out_ref[:, v] = jnp.swapaxes(jnp.stack(planes), 0, 1)


def pull_products(s_ref, g_ref, prod_ref, start, stop):
    def body(i, carry):
        for l in range(2):
            u = s_ref[l, i]
            gu, gv, gb = g_ref[l, i], g_ref[2 + l, i], g_ref[4 + l, i]
            prod_ref[l, i] = u * gu + gb
            prod_ref[2 + l, i] = u * gv
            prod_ref[4 + l, i] = u * gb + gu
        return carry

    lax.fori_loop(start, stop, body, 0)


def pull_row(s_ref, g_ref, prod_ref, i):
    out = [None] * VARS
    for l in range(2):
        u, v, b = s_ref[l, i], s_ref[2 + l, i], s_ref[4 + l, i]
        gu, gv, gb = g_ref[l, i], g_ref[2 + l, i], g_ref[4 + l, i]
        ru, rv, rb = (row_diff(s_ref, k + l, i) for k in (0, 2, 4))
        cu, cv, cb = col_diff(u), col_diff(v), col_diff(b)
        out[l] = (
            row_diff(prod_ref, l, i) + col_diff(v * gu)
            - (gu * ru + gv * rv + gb * rb) - 0.5 * gv + 0.3 * (g_ref[1 - l, i] - gu)
        )
        out[2 + l] = (
            row_diff(prod_ref, 2 + l, i) + col_diff(v * gv + gb)
            - (gu * cu + gv * cv + gb * cb) + 0.5 * gu + 0.3 * (g_ref[3 - l, i] - gv)
        )
        out[4 + l] = (
            row_diff(prod_ref, 4 + l, i) + col_diff(v * gb + gv) + 0.3 * (g_ref[5 - l, i] - gb)
        )
    return out


def backward_kernel(
    x_ref, top_ref, bot_ref, mid_ref, mid_top_ref, mid_bot_ref, g_ref, g_top_ref, g_bot_ref,
    out_ref, s_ref, m_ref, c_ref, prod_ref, gm_ref,
):
    load_state(s_ref, x_ref, top_ref, bot_ref)
    for v in range(VARS):
        for r in range(2):
            m_ref[v, r] = mid_top_ref[v * 2 + r]
            m_ref[v, 14 + r] = mid_bot_ref[v * 2 + r]
        for r in range(12):
            m_ref[v, 2 + r] = mid_ref[v, r]
        for r in range(ROWS):
            c_ref[v, 4 + r] = g_ref[v * ROWS + r]
        for r in range(4):
            c_ref[v, r] = g_top_ref[v * 4 + r]
            c_ref[v, 12 + r] = g_bot_ref[v * 4 + r]

    pull_products(m_ref, c_ref, prod_ref, 0, 16)

    def second(i, carry):
        got = pull_row(m_ref, c_ref, prod_ref, i)
        for v in range(VARS):
            gm_ref[v, i] = 0.5 * time_step * got[v]
        return carry

    lax.fori_loop(2, 14, second, 0)

    def combine(i, carry):
        for v in range(VARS):
            g, gm = c_ref[v, i], gm_ref[v, i]
            c_ref[v, i] = 0.5 * time_step * g + time_step * gm
            gm_ref[v, i] = g + gm
        return carry

    lax.fori_loop(2, 14, combine, 0)
    pull_products(s_ref, c_ref, prod_ref, 2, 14)

    def first(i, carry):
        got = pull_row(s_ref, c_ref, prod_ref, i)
        for v in range(VARS):
            gm_ref[v, i] = gm_ref[v, i] + got[v]
        return carry

    lax.fori_loop(4, 12, first, 0)
    for v in range(VARS):
        out_ref[:, v] = jnp.swapaxes(gm_ref[v, 4:12], 0, 1)


def halves(x):
    high = x.astype(bf16)
    return high, (x - high.astype(f32)).astype(bf16)


def dot(a, b):
    return lax.dot_general(a, b, (((1,), (0,)), ((), ())), preferred_element_type=f32)


def dot_first(a, b):
    return lax.dot_general(a, b, (((0,), (0,)), ((), ())), preferred_element_type=f32)


def times(left, right, product=dot):
    lh, ll = left
    rh, rl = right
    return product(lh, rh) + (product(lh, rl) + product(ll, rh))


def stack(*parts):
    return tuple(jnp.concatenate(p, axis=0) for p in zip(*parts))


def analysis_kernel(
    fore_ref, cot_ref, list_ref, meta_ref, up_ref, gr_ref, x_ref, c_ref, y_ref, d_ref, go_ref, block_ref
):
    width = 4 * MEMBERS
    block_row = lax.broadcasted_iota(jnp.int32, (width, width), 0) // MEMBERS
    block_col = lax.broadcasted_iota(jnp.int32, (width, width), 1) // MEMBERS
    block_ref[...] = jnp.where(block_row == block_col, 1.0, 0.0).astype(bf16)

    for src, dst in ((fore_ref, x_ref), (cot_ref, c_ref)):

        def turn(v, carry, src=src, dst=dst):
            for h in range(2):
                tall = [src[s, v * 4 + 2 * h + k] for k in range(2) for s in range(8)]
                dst[v, :, 128 * h : 128 * h + 128] = jnp.concatenate(tall, axis=0).T
            return carry

        lax.fori_loop(0, VARS, turn, 0)

    for o in range(4):
        tall = [fore_ref[s, 24 + o] for s in range(8)]
        seen = jnp.concatenate(tall + tall, axis=0).T[:WINDOW]
        mean = jnp.sum(seen, axis=1, keepdims=True) * (1.0 / 128.0)
        spread = seen - mean
        at = pl.ds(o, WINDOW, stride=4)
        y_ref[at, :] = spread
        d_ref[at, :] = meta_ref[0, at, :] - mean
    go_ref[...] = jnp.zeros(go_ref.shape, f32)

    def block_of(pair):
        mask = block_ref[...]
        return tuple(jnp.concatenate([p] * 4, axis=0) * mask for p in pair)

    def block_sum(x):
        high, low = halves(x)
        return dot(high, block_ref[...]) + dot(low, block_ref[...])

    def row_sum(x):
        return block_sum(jnp.broadcast_to(jnp.sum(x, axis=0, keepdims=True), (8, width)))

    def one_row(x, right):
        return times(halves(x), right)

    lane = lax.broadcasted_iota(jnp.int32, (MEMBERS, width), 1)
    sub = lax.broadcasted_iota(jnp.int32, (MEMBERS, width), 0)
    identity = jnp.where(lane % MEMBERS == sub, 1.0, 0.0)
    entry = lax.broadcasted_iota(jnp.int32, (WINDOW, width), 0)
    patch_row = (lax.broadcasted_iota(jnp.int32, (WINDOW, width), 1) // MEMBERS).astype(f32)
    col_gap = (entry // 4).astype(f32) - 9.5
    col_gap_sq = col_gap * col_gap
    left_half = lax.broadcasted_iota(jnp.int32, (96, width), 0) % 8 < 4
    row8 = lax.broadcasted_iota(jnp.int32, (8, width), 0)

    def solve(quad):
        at = pl.ds(pl.multiple_of(16 * quad, 16), WINDOW)
        lists = list_ref[pl.ds(quad, 1), :]
        hits = jnp.where(jnp.broadcast_to(lists, (WINDOW, width)) == entry, 1.0, 0.0).astype(bf16)
        count = dot(hits, block_ref[...])
        obs_row = jnp.concatenate([meta_ref[1, at, :]] * 2, axis=1)
        error = jnp.concatenate([meta_ref[2, at, :]] * 2, axis=1)
        row_gap = obs_row - 2.0 * patch_row - 0.5
        weight = count * jnp.exp((row_gap * row_gap + col_gap_sq) * (-1.0 / (2.0 * LOC_R * LOC_R))) / error
        y = y_ref[at, :]
        scaled = weight * jnp.concatenate([y, y], axis=1)
        d = d_ref[at, :]
        gain = weight * jnp.concatenate([d, d], axis=1)
        scaled_pair = halves(scaled)
        gram = times(halves(y[:, :MEMBERS]), scaled_pair, dot_first) + (MEMBERS - 1.0) * identity
        inv = lax.rsqrt(row_sum(gram * gram))
        t0 = gram * inv[:1]
        forcing = jnp.sum(scaled * jnp.concatenate([d, d], axis=1), axis=0, keepdims=True)
        forcing = jnp.broadcast_to(forcing, (8, width))

        m0 = 1.5 * identity - 0.5 * t0
        z1 = halves(m0)
        r0 = block_of(z1)
        t0p = halves(t0)
        u0 = halves(times(t0p, r0))
        t1f = times(u0, r0)
        t1 = halves(t1f)
        r1 = block_of(halves(1.5 * identity - 0.5 * t1f))
        both = times(stack(z1, t1), r1)
        z2, u1 = halves(both[:MEMBERS]), halves(both[MEMBERS:])
        t2f = times(u1, r1)
        t2 = halves(t2f)
        r2 = block_of(halves(1.5 * identity - 0.5 * t2f))
        both = times(stack(z2, t2), r2)
        z3, u2 = halves(both[:MEMBERS]), halves(both[MEMBERS:])
        t3f = times(u2, r2)
        r3 = block_of(halves(1.5 * identity - 0.5 * t3f))
        z4 = block_of(halves(times(z3, r3)))
        half_way = one_row(forcing, z4)
        mean_weight = one_row(half_way, z4) * inv
        state = (t0, t0p, u0, t1, u1, t2, u2, z1, z2, z3, r0, r1, r2, r3)
        return at, inv, z4, forcing, half_way, mean_weight, scaled, scaled_pair, gain, state

    def pull_root(e, state):
        t0, t0p, u0, t1, u1, t2, u2, z1, z2, z3, r0, r1, r2, r3 = state
        dt0 = halves(e)
        dm = halves(-0.5 * e)
        s0 = block_of(dm)
        du0 = halves(times(dt0, r0) + times(t0p, s0))
        dt1f = times(du0, r0) + times(u0, s0)
        dt1 = halves(dt1f)
        s1 = block_of(halves(-0.5 * dt1f))
        both = times(stack(dm, dt1), r1) + times(stack(z1, t1), s1)
        dz2, du1 = halves(both[:MEMBERS]), halves(both[MEMBERS:])
        dt2f = times(du1, r1) + times(u1, s1)
        dt2 = halves(dt2f)
        s2 = block_of(halves(-0.5 * dt2f))
        both = times(stack(dz2, dt2), r2) + times(stack(z2, t2), s2)
        dz3, du2 = halves(both[:MEMBERS]), halves(both[MEMBERS:])
        dt3f = times(du2, r2) + times(u2, s2)
        s3 = block_of(halves(-0.5 * dt3f))
        return times(dz3, r3) + times(z3, s3)

    def fold(x):
        x = x[:, :128] + x[:, 128:]
        return x + pltpu.roll(x, 64, 1)

    def pair_of_quads(p, carry):
        pieces = [
            (v, pl.ds(pl.multiple_of(64 * k + 8 * p, 8), 8)) for v in range(VARS) for k in range(2)
        ]
        x = jnp.concatenate([x_ref[v, at, :] for v, at in pieces], axis=0)
        c = jnp.concatenate([c_ref[v, at, :] for v, at in pieces], axis=0)
        both = block_sum(jnp.concatenate([x, c], axis=0))
        centre = both[:96] * (1.0 / MEMBERS)
        c_sum = both[96:]
        a = x - centre
        a_c = halves(jnp.concatenate([a, c], axis=0))

        updates, pulls = [], []
        for q in range(2):
            at, inv, z4, forcing, half_way, mean_weight, scaled, scaled_pair, gain, state = solve(2 * p + q)
            alpha = math.sqrt(MEMBERS - 1.0) * jnp.sqrt(inv[:1])
            mine = left_half if q == 0 else jnp.logical_not(left_half)
            both = times(a_c, z4)
            moved = alpha * both[:96]
            updates.append(moved + block_sum(a * mean_weight[:1]))
            pulls.append(alpha * both[96:] + c_sum * mean_weight[:1])
            a_mine = jnp.where(mine, a, 0.0)
            g_mean = jnp.broadcast_to(jnp.sum(a_mine * c_sum, axis=0, keepdims=True), (8, width))
            g_half = one_row(g_mean, z4) * inv
            g_forcing = one_row(g_half, z4)
            left = jnp.where(row8 == 0, g_mean * inv, jnp.where(row8 == 1, g_half, 0.0))
            right = jnp.where(row8 == 0, half_way, jnp.where(row8 == 1, forcing, 0.0))
            scaled_a = a_mine * alpha
            lhs = halves(jnp.concatenate([scaled_a, c, left, right], axis=0))
            rhs = halves(jnp.concatenate([c, scaled_a, right, left], axis=0))
            full = times(lhs, rhs, dot_first)
            block = lane // MEMBERS
            e = jnp.where(
                block < 2,
                jnp.where(block == 0, full[:64], full[64:128]),
                jnp.where(block == 2, full[128:192], full[192:]),
            ) * 0.5
            g_root = pull_root(e, state)
            t0 = state[0]
            loss = jnp.sum(jnp.where(mine, c * moved, 0.0), axis=0, keepdims=True) * 0.5
            loss = loss + g_mean[:1] * mean_weight[:1] + jnp.sum(g_root * t0, axis=0, keepdims=True)
            loss = block_sum(jnp.broadcast_to(loss, (8, width)))
            g_gram = (g_root - loss[:1] * t0) * inv[:1]
            g_y = 2.0 * times(scaled_pair, block_of(halves(g_gram))) + gain * g_forcing[:1]
            g_d = scaled * g_forcing[:1]
            low = lax.broadcasted_iota(jnp.int32, (WINDOW, 128), 1) < 64
            go_ref[at, :] += jnp.where(low, fold(g_y), fold(g_d))

        update = centre + jnp.where(left_half, updates[0], updates[1])
        pull = jnp.where(left_half, pulls[0], pulls[1])
        pull = pull + (c_sum - block_sum(pull)) * (1.0 / MEMBERS)
        for n, (v, at) in enumerate(pieces):
            x_ref[v, at, :] = update[8 * n : 8 * n + 8]
            c_ref[v, at, :] = pull[8 * n : 8 * n + 8]
        return carry

    lax.fori_loop(0, QUADS // 2, pair_of_quads, 0)

    for src, dst in ((x_ref, up_ref), (c_ref, gr_ref)):

        def turn_back(v, carry, src=src, dst=dst):
            for h in range(2):
                tall = src[v, :, 128 * h : 128 * h + 128].T
                for k in range(2):
                    for s in range(8):
                        at = 64 * k + 8 * s
                        dst[s, v * 4 + 2 * h + k] = tall[at : at + 8]
            return carry

        lax.fori_loop(0, VARS, turn_back, 0)

    for o in range(4):
        got = go_ref[pl.ds(o, WINDOW, stride=4), :]
        got = got - jnp.sum(got, axis=1, keepdims=True) * (1.0 / MEMBERS)
        tall = jnp.concatenate([got, jnp.zeros((128 - WINDOW, 128), f32)], axis=0).T
        for s in range(8):
            gr_ref[s, 24 + o] = tall[8 * s : 8 * s + 8]


def ring(value, up):
    count = lax.axis_size("space")
    if up:
        pairs = [((i + 1) % count, i) for i in range(count)]
    else:
        pairs = [(i, (i + 1) % count) for i in range(count)]
    return lax.ppermute(value, "space", pairs)


def swap(value):
    return lax.all_to_all(value, "member", split_axis=0, concat_axis=0, tiled=True)


def plane_scratch(rows):
    return pltpu.VMEM((VARS, rows, PER_DEV, COLS), f32)


def shards(initial_ensemble, obs_value, obs_error, obs_location, patch_obs, cotangent):
    shape = initial_ensemble.shape
    half = (VARS * 4, PER_DEV, COLS)
    quarter = (VARS * 2, PER_DEV, COLS)
    size = 4 * PER_DEV * STRIDE * COLS

    state = initial_ensemble
    first, last = call(edge_kernel, [half, half], [], 1000, 2 * size, state)
    bot = ring(first, True)
    top = ring(last, False)

    (cot_sent,) = call(cot_kernel, [(8, 24, PER_DEV, 128)], [], 1000, 2 * size, cotangent)
    cot_owned = swap(cot_sent)

    position = lax.axis_index("member") * (NOBS // 8)
    plane = obs_location[0] // COLS
    chosen = plane.reshape(COLS, 4).T
    meta = jnp.stack([obs_value[0], (plane % ROWS).astype(f32), obs_error[0]])
    meta = jnp.concatenate([meta[:, -32:], meta, meta[:, :32]], axis=1)
    meta = lax.dynamic_slice_in_dim(meta, position, LOCAL_OBS, axis=1)
    meta = jnp.broadcast_to(meta[:, :, None], (3, LOCAL_OBS, 128))
    lists = (patch_obs[0] - position + 32) % NOBS
    lists = lists.reshape(QUADS, 256) - 16 * jnp.arange(QUADS, dtype=jnp.int32)[:, None]

    fore_sent, mid, mid_first, mid_last = call(
        forward_kernel,
        [(8, 28, PER_DEV, 128), (VARS, 12, PER_DEV, COLS), quarter, quarter],
        [plane_scratch(16), plane_scratch(ROWS)],
        10**7, 5 * size, state, top, bot, chosen,
    )
    fore_owned = swap(fore_sent)
    mid_bot = ring(mid_first, True)
    mid_top = ring(mid_last, False)

    cells = pltpu.VMEM((VARS, 128, 256), f32)
    update_sent, grad_sent = call(
        analysis_kernel,
        [(8, 24, PER_DEV, 128), (8, 28, PER_DEV, 128)],
        [
            cells, cells, pltpu.VMEM((LOCAL_OBS, 128), f32), pltpu.VMEM((LOCAL_OBS, 128), f32),
            pltpu.VMEM((LOCAL_OBS, 128), f32), pltpu.VMEM((256, 256), bf16),
        ],
        10**10, 5 * size, fore_owned, cot_owned, lists, meta,
    )
    update = swap(update_sent)
    grad = swap(grad_sent)

    g, g_first, g_last = call(
        collect_kernel, [(STRIDE, PER_DEV, COLS), half, half], [], 10**6, 3 * size, grad, chosen
    )
    g_bot = ring(g_first, True)
    g_top = ring(g_last, False)
    (analysis,) = call(place_kernel, [shape], [], 1000, 2 * size, update)
    (gradient,) = call(
        backward_kernel,
        [shape],
        [plane_scratch(16)] * 5,
        10**7, 6 * size, state, top, bot, mid, mid_top, mid_bot, g, g_top, g_bot,
    )
    return analysis, gradient


def solution(mesh):
    placed = (
        P("member", None, "space", None),
        P("space", None),
        P("space", None),
        P("space", None),
        P("space", "member", None),
        P("member", None, "space", None),
    )
    return jax.shard_map(
        shards,
        mesh=mesh,
        in_specs=placed,
        out_specs=(P("member", None, "space", None), P("member", None, "space", None)),
        check_vma=False,
    )
```

```python
import functools
import math

import jax
import jax.numpy as jnp
from jax import lax
from jax.experimental import pallas as pl
from jax.experimental.pallas import tpu as pltpu
from jax.sharding import PartitionSpec as P

VARS = 6
ROWS = 8
COLS = 512
MEMBERS = 64
PER_DEV = 8
STRIDE = VARS * ROWS
NOBS = 2048
WINDOW = 80
LOCAL_OBS = 320
QUADS = 16
HALO = 6
PAIRS = 4
LOC_R = 8

time_step = 0.2
f32 = jnp.float32
bf16 = jnp.bfloat16
VMEM_LIMIT = 50 * 1024 * 1024


def call(kernel, outs, scratch, flops, moved, *args):
    spec = pl.BlockSpec(memory_space=pltpu.VMEM)
    return pl.pallas_call(
        kernel,
        out_shape=[jax.ShapeDtypeStruct(s, f32) for s in outs],
        in_specs=[spec] * len(args),
        out_specs=[spec] * len(outs),
        scratch_shapes=scratch,
        compiler_params=pltpu.CompilerParams(vmem_limit_bytes=VMEM_LIMIT),
        cost_estimate=pl.CostEstimate(flops=flops, bytes_accessed=moved, transcendentals=0),
    )(*args)


def lane_shift(q, by):
    return pltpu.roll(q, by % COLS, 1)


def col_diff(q):
    near = lane_shift(q, -1) - lane_shift(q, 1)
    far = lane_shift(q, -2) - lane_shift(q, 2)
    return near * (8.0 / 12.0) - far * (1.0 / 12.0)


def row_diff(ref, v, i):
    near = ref[v, i + 1] - ref[v, i - 1]
    far = ref[v, i + 2] - ref[v, i - 2]
    return near * (8.0 / 12.0) - far * (1.0 / 12.0)


def tendency(ref, i):
    rates = [None] * VARS
    for l in range(2):
        u, v, b = ref[l, i], ref[2 + l, i], ref[4 + l, i]
        ru, rv, rb = (row_diff(ref, k + l, i) for k in (0, 2, 4))
        cu, cv, cb = col_diff(u), col_diff(v), col_diff(b)
        rates[l] = 0.5 * v - (u * ru + v * cu) - rb + 0.3 * (ref[1 - l, i] - u)
        rates[2 + l] = -0.5 * u - (u * rv + v * cv) - cb + 0.3 * (ref[3 - l, i] - v)
        rates[4 + l] = -(u * rb + v * cb) - (ru + cv) + 0.3 * (ref[5 - l, i] - b)
    return rates


def planes_of(x_ref, v):
    return jnp.swapaxes(x_ref[:, v], 0, 1)


def edge_kernel(x_ref, first_ref, last_ref):
    for v in range(VARS):
        planes = planes_of(x_ref, v)
        first_ref[HALO * v : HALO * v + HALO] = planes[:HALO]
        last_ref[HALO * v : HALO * v + HALO] = planes[ROWS - HALO :]


def pack_planes(even, odd, store):
    low = lax.broadcasted_iota(jnp.int32, (PER_DEV, 128), 1) < 64
    for t in range(4):
        a, b = even[:, 128 * t : 128 * t + 128], odd[:, 128 * t : 128 * t + 128]
        store(2 * t, jnp.where(low, a, pltpu.roll(b, 64, 1)))
        store(2 * t + 1, jnp.where(low, pltpu.roll(a, 64, 1), b))


def unpack_planes(load):
    low = lax.broadcasted_iota(jnp.int32, (PER_DEV, 128), 1) < 64
    even, odd = [], []
    for t in range(4):
        a, b = load(2 * t), load(2 * t + 1)
        even.append(jnp.where(low, a, pltpu.roll(b, 64, 1)))
        odd.append(jnp.where(low, pltpu.roll(a, 64, 1), b))
    return jnp.concatenate(even, axis=1), jnp.concatenate(odd, axis=1)


def cot_kernel(x_ref, out_ref):
    for v in range(VARS):
        planes = planes_of(x_ref, v)
        for r in range(4):

            def store(d, value, t=v * 4 + r):
                out_ref[d, t] = value

            pack_planes(planes[2 * r], planes[2 * r + 1], store)


def load_state(s_ref, x_ref, top_ref, bot_ref):
    for v in range(VARS):
        s_ref[v, HALO : HALO + ROWS] = planes_of(x_ref, v)
        for r in range(HALO):
            s_ref[v, r] = top_ref[v * HALO + r]
            s_ref[v, HALO + ROWS + r] = bot_ref[v * HALO + r]


def forward_kernel(x_ref, top_ref, bot_ref, sel_ref, out_ref, mid_ref, s_ref, fore_ref):
    load_state(s_ref, x_ref, top_ref, bot_ref)

    def middle(i, carry):
        rates = tendency(s_ref, i + 2)
        for v in range(VARS):
            mid_ref[v, i] = s_ref[v, i + 2] + time_step * rates[v]
        return carry

    lax.fori_loop(0, 16, middle, 0)

    def finish(i, carry):
        rates = tendency(mid_ref, i + 4)
        for v in range(VARS):
            fore_ref[v, i] = 0.5 * (s_ref[v, i + HALO] + mid_ref[v, i + 4]) + 0.5 * time_step * rates[v]
        return carry

    lax.fori_loop(0, ROWS, finish, 0)

    def pack(v, carry):
        for r in range(4):

            def store(d, value, r=r):
                out_ref[d, v * 4 + r] = value

            pack_planes(fore_ref[v, 2 * r], fore_ref[v, 2 * r + 1], store)
        return carry

    lax.fori_loop(0, VARS, pack, 0)

    for o in range(4):
        chosen = jnp.broadcast_to(sel_ref[o : o + 1, :], (PER_DEV, COLS))

        def pick(v, acc, chosen=chosen):
            for r in range(ROWS):
                acc = jnp.where(chosen == v * ROWS + r, fore_ref[v, r], acc)
            return acc

        seen = lax.fori_loop(0, VARS, pick, jnp.zeros((PER_DEV, COLS), f32))
        for d in range(8):
            out_ref[d, 24 + o] = lane_shift(seen, 8 - 64 * d)[:, :128]


def collect_kernel(got_ref, sel_ref, g_ref, first_ref, last_ref):
    lane = lax.broadcasted_iota(jnp.int32, (PER_DEV, 128), 1)
    sums, chosen = [], []
    for o in range(4):
        total = jnp.zeros((PER_DEV, COLS), f32)
        for d in range(8):
            piece = jnp.where(lane < WINDOW, got_ref[d, 24 + o], 0.0)
            wide = jnp.concatenate([piece, jnp.zeros((PER_DEV, COLS - 128), f32)], axis=1)
            total = total + lane_shift(wide, 64 * d - 8)
        sums.append(total)
        chosen.append(jnp.broadcast_to(sel_ref[o : o + 1, :], (PER_DEV, COLS)))

    for v in range(VARS):
        for r in range(4):
            pair = unpack_planes(lambda d: got_ref[d, v * 4 + r])
            for k in range(2):
                row = 2 * r + k
                value = pair[k]
                for o in range(4):
                    value = value + jnp.where(chosen[o] == v * ROWS + row, sums[o], 0.0)
                g_ref[v * ROWS + row] = value
                if row < 4:
                    first_ref[v * 4 + row] = value
                else:
                    last_ref[v * 4 + row - 4] = value


def place_kernel(got_ref, out_ref):
    for v in range(VARS):
        planes = []
        for r in range(4):
            planes.extend(unpack_planes(lambda d: got_ref[d, v * 4 + r]))
        out_ref[:, v] = jnp.swapaxes(jnp.stack(planes), 0, 1)


def pull_products(s_ref, g_ref, prod_ref, start, stop, shift):
    def body(i, carry):
        for l in range(2):
            u = s_ref[l, i + shift]
            gu, gv, gb = g_ref[l, i], g_ref[2 + l, i], g_ref[4 + l, i]
            prod_ref[l, i] = u * gu + gb
            prod_ref[2 + l, i] = u * gv
            prod_ref[4 + l, i] = u * gb + gu
        return carry

    lax.fori_loop(start, stop, body, 0)


def pull_row(s_ref, g_ref, prod_ref, i, shift):
    out = [None] * VARS
    for l in range(2):
        u, v, b = (s_ref[k + l, i + shift] for k in (0, 2, 4))
        gu, gv, gb = g_ref[l, i], g_ref[2 + l, i], g_ref[4 + l, i]
        ru, rv, rb = (row_diff(s_ref, k + l, i + shift) for k in (0, 2, 4))
        cu, cv, cb = col_diff(u), col_diff(v), col_diff(b)
        out[l] = (
            row_diff(prod_ref, l, i) + col_diff(v * gu)
            - (gu * ru + gv * rv + gb * rb) - 0.5 * gv + 0.3 * (g_ref[1 - l, i] - gu)
        )
        out[2 + l] = (
            row_diff(prod_ref, 2 + l, i) + col_diff(v * gv + gb)
            - (gu * cu + gv * cv + gb * cb) + 0.5 * gu + 0.3 * (g_ref[3 - l, i] - gv)
        )
        out[4 + l] = (
            row_diff(prod_ref, 4 + l, i) + col_diff(v * gb + gv) + 0.3 * (g_ref[5 - l, i] - gb)
        )
    return out


def backward_kernel(
    x_ref, top_ref, bot_ref, mid_ref, g_ref, g_top_ref, g_bot_ref,
    out_ref, s_ref, c_ref, prod_ref, gm_ref,
):
    load_state(s_ref, x_ref, top_ref, bot_ref)
    for v in range(VARS):
        for r in range(ROWS):
            c_ref[v, 4 + r] = g_ref[v * ROWS + r]
        for r in range(4):
            c_ref[v, r] = g_top_ref[v * 4 + r]
            c_ref[v, 12 + r] = g_bot_ref[v * 4 + r]

    pull_products(mid_ref, c_ref, prod_ref, 0, 16, 0)

    def second(i, carry):
        got = pull_row(mid_ref, c_ref, prod_ref, i, 0)
        for v in range(VARS):
            gm_ref[v, i] = 0.5 * time_step * got[v]
        return carry

    lax.fori_loop(2, 14, second, 0)

    def combine(i, carry):
        for v in range(VARS):
            g, gm = c_ref[v, i], gm_ref[v, i]
            c_ref[v, i] = 0.5 * time_step * g + time_step * gm
            gm_ref[v, i] = g + gm
        return carry

    lax.fori_loop(2, 14, combine, 0)
    pull_products(s_ref, c_ref, prod_ref, 2, 14, HALO - 4)

    def first(i, carry):
        got = pull_row(s_ref, c_ref, prod_ref, i, HALO - 4)
        for v in range(VARS):
            gm_ref[v, i] = gm_ref[v, i] + got[v]
        return carry

    lax.fori_loop(4, 12, first, 0)
    for v in range(VARS):
        out_ref[:, v] = jnp.swapaxes(gm_ref[v, 4:12], 0, 1)


def halves(x):
    high = x.astype(bf16)
    return high, (x - high.astype(f32)).astype(bf16)


def dot(a, b):
    return lax.dot_general(a, b, (((1,), (0,)), ((), ())), preferred_element_type=f32)


def dot_first(a, b):
    return lax.dot_general(a, b, (((0,), (0,)), ((), ())), preferred_element_type=f32)


def times(left, right, product=dot):
    lh, ll = left
    rh, rl = right
    if product is dot_first:
        return product(lh, rh) + (product(lh, rl) + product(ll, rh))
    n = lh.shape[0]
    if n % 16:
        return product(lh, rh) + (product(lh, rl) + product(ll, rh))
    both = product(jnp.concatenate([lh, ll], axis=0), rh)
    return both[:n] + (both[n:] + product(lh, rl))


def in_step(jobs):
    results = [None] * len(jobs)
    left = list(range(len(jobs)))
    while left:
        for n in list(left):
            try:
                next(jobs[n])
            except StopIteration as done:
                results[n] = done.value
                left.remove(n)
    return results


def stack(*parts):
    return tuple(jnp.concatenate(p, axis=0) for p in zip(*parts))


def analysis_kernel(
    fore_ref, cot_ref, list_ref, meta_ref, up_ref, gr_ref, x_ref, c_ref, y_ref, d_ref, go_ref, block_ref
):
    width = 4 * MEMBERS
    block_row = lax.broadcasted_iota(jnp.int32, (width, width), 0) // MEMBERS
    block_col = lax.broadcasted_iota(jnp.int32, (width, width), 1) // MEMBERS
    block_ref[...] = jnp.where(block_row == block_col, 1.0, 0.0).astype(bf16)

    for src, dst in ((fore_ref, x_ref), (cot_ref, c_ref)):

        def turn(v, carry, src=src, dst=dst):
            for h in range(2):
                tall = [src[s, v * 4 + 2 * h + k] for k in range(2) for s in range(8)]
                dst[v, :, 128 * h : 128 * h + 128] = jnp.concatenate(tall, axis=0).T
            return carry

        lax.fori_loop(0, VARS, turn, 0)

    for o in range(4):
        tall = [fore_ref[s, 24 + o] for s in range(8)]
        seen = jnp.concatenate(tall + tall, axis=0).T[:WINDOW]
        mean = jnp.sum(seen, axis=1, keepdims=True) * (1.0 / 128.0)
        spread = seen - mean
        at = pl.ds(o, WINDOW, stride=4)
        y_ref[at, :] = spread
        d_ref[at, :] = meta_ref[0, at, :] - mean
    go_ref[...] = jnp.zeros(go_ref.shape, f32)

    def block_of(pair):
        mask = block_ref[...]
        return tuple(jnp.concatenate([p] * 4, axis=0) * mask for p in pair)

    def block_sum(x):
        high, low = halves(x)
        return dot(high, block_ref[...]) + dot(low, block_ref[...])

    def row_sum(x):
        return block_sum(jnp.broadcast_to(jnp.sum(x, axis=0, keepdims=True), (8, width)))

    def one_row(x, right):
        return times(halves(x), right)

    lane = lax.broadcasted_iota(jnp.int32, (MEMBERS, width), 1)
    sub = lax.broadcasted_iota(jnp.int32, (MEMBERS, width), 0)
    identity = jnp.where(lane % MEMBERS == sub, 1.0, 0.0)
    entry = lax.broadcasted_iota(jnp.int32, (WINDOW, width), 0)
    patch_row = (lax.broadcasted_iota(jnp.int32, (WINDOW, width), 1) // MEMBERS).astype(f32)
    col_gap = (entry // 4).astype(f32) - 9.5
    col_gap_sq = col_gap * col_gap
    left_half = lax.broadcasted_iota(jnp.int32, (96, width), 0) % 8 < 4
    row8 = lax.broadcasted_iota(jnp.int32, (8, width), 0)

    def solve(quad):
        at = pl.ds(pl.multiple_of(16 * quad, 16), WINDOW)
        lists = list_ref[pl.ds(quad, 1), :]
        hits = jnp.where(jnp.broadcast_to(lists, (WINDOW, width)) == entry, 1.0, 0.0).astype(bf16)
        count = dot(hits, block_ref[...])
        yield
        obs_row = jnp.concatenate([meta_ref[1, at, :]] * 2, axis=1)
        error = jnp.concatenate([meta_ref[2, at, :]] * 2, axis=1)
        row_gap = obs_row - 2.0 * patch_row - 0.5
        weight = count * jnp.exp((row_gap * row_gap + col_gap_sq) * (-1.0 / (2.0 * LOC_R * LOC_R))) / error
        y = y_ref[at, :]
        scaled = weight * jnp.concatenate([y, y], axis=1)
        d = d_ref[at, :]
        gain = weight * jnp.concatenate([d, d], axis=1)
        scaled_pair = halves(scaled)
        gram = times(halves(y[:, :MEMBERS]), scaled_pair, dot_first) + (MEMBERS - 1.0) * identity
        yield
        inv = lax.rsqrt(row_sum(gram * gram))
        yield
        t0 = gram * inv[:1]
        forcing = jnp.sum(scaled * jnp.concatenate([d, d], axis=1), axis=0, keepdims=True)
        forcing = jnp.broadcast_to(forcing, (8, width))

        m0 = 1.5 * identity - 0.5 * t0
        z1 = halves(m0)
        r0 = block_of(z1)
        t0p = halves(t0)
        u0 = halves(times(t0p, r0))
        yield
        t1f = times(u0, r0)
        yield
        t1 = halves(t1f)
        r1 = block_of(halves(1.5 * identity - 0.5 * t1f))
        both = times(stack(z1, t1), r1)
        yield
        z2, u1 = halves(both[:MEMBERS]), halves(both[MEMBERS:])
        t2f = times(u1, r1)
        yield
        t2 = halves(t2f)
        r2 = block_of(halves(1.5 * identity - 0.5 * t2f))
        both = times(stack(z2, t2), r2)
        yield
        z3, u2 = halves(both[:MEMBERS]), halves(both[MEMBERS:])
        t3f = times(u2, r2)
        yield
        r3 = block_of(halves(1.5 * identity - 0.5 * t3f))
        z4 = block_of(halves(times(z3, r3)))
        yield
        half_way = one_row(forcing, z4)
        yield
        mean_weight = one_row(half_way, z4) * inv
        yield
        state = (t0, t0p, u0, t1, u1, t2, u2, z1, z2, z3, r0, r1, r2, r3)
        return at, inv, z4, forcing, half_way, mean_weight, scaled, scaled_pair, gain, state

    def pull_root(e, state):
        t0, t0p, u0, t1, u1, t2, u2, z1, z2, z3, r0, r1, r2, r3 = state
        dt0 = halves(e)
        dm = halves(-0.5 * e)
        s0 = block_of(dm)
        du0 = halves(times(dt0, r0) + times(t0p, s0))
        yield
        dt1f = times(du0, r0) + times(u0, s0)
        yield
        dt1 = halves(dt1f)
        s1 = block_of(halves(-0.5 * dt1f))
        both = times(stack(dm, dt1), r1) + times(stack(z1, t1), s1)
        yield
        dz2, du1 = halves(both[:MEMBERS]), halves(both[MEMBERS:])
        dt2f = times(du1, r1) + times(u1, s1)
        yield
        dt2 = halves(dt2f)
        s2 = block_of(halves(-0.5 * dt2f))
        both = times(stack(dz2, dt2), r2) + times(stack(z2, t2), s2)
        yield
        dz3, du2 = halves(both[:MEMBERS]), halves(both[MEMBERS:])
        dt3f = times(du2, r2) + times(u2, s2)
        yield
        s3 = block_of(halves(-0.5 * dt3f))
        got = times(dz3, r3) + times(z3, s3)
        yield
        return got

    def fold(x):
        x = x[:, :128] + x[:, 128:]
        return x + pltpu.roll(x, 64, 1)

    def open_pair(p):
        pieces = [
            (v, pl.ds(pl.multiple_of(64 * k + 8 * p, 8), 8)) for v in range(VARS) for k in range(2)
        ]
        x = jnp.concatenate([x_ref[v, at, :] for v, at in pieces], axis=0)
        c = jnp.concatenate([c_ref[v, at, :] for v, at in pieces], axis=0)
        both = block_sum(jnp.concatenate([x, c], axis=0))
        centre = both[:96] * (1.0 / MEMBERS)
        c_sum = both[96:]
        a = x - centre
        a_c = halves(jnp.concatenate([a, c], axis=0))

        return pieces, centre, c_sum, a, c, a_c

    def one_quad(p, q, opened):
        pieces, centre, c_sum, a, c, a_c = opened
        at, inv, z4, forcing, half_way, mean_weight, scaled, scaled_pair, gain, state = yield from solve(2 * p + q)
        alpha = math.sqrt(MEMBERS - 1.0) * jnp.sqrt(inv[:1])
        mine = left_half if q == 0 else jnp.logical_not(left_half)
        both = times(a_c, z4)
        yield
        moved = alpha * both[:96]
        update = moved + block_sum(a * mean_weight[:1])
        yield
        pull = alpha * both[96:] + c_sum * mean_weight[:1]
        a_mine = jnp.where(mine, a, 0.0)
        g_mean = jnp.broadcast_to(jnp.sum(a_mine * c_sum, axis=0, keepdims=True), (8, width))
        g_half = one_row(g_mean, z4) * inv
        yield
        g_forcing = one_row(g_half, z4)
        yield
        left = jnp.where(row8 == 0, g_mean * inv, jnp.where(row8 == 1, g_half, 0.0))
        right = jnp.where(row8 == 0, half_way, jnp.where(row8 == 1, forcing, 0.0))
        scaled_a = a_mine * alpha
        lhs = halves(jnp.concatenate([scaled_a, c, left, right], axis=0))
        rhs = halves(jnp.concatenate([c, scaled_a, right, left], axis=0))
        full = times(lhs, rhs, dot_first)
        yield
        block = lane // MEMBERS
        e = jnp.where(
            block < 2,
            jnp.where(block == 0, full[:64], full[64:128]),
            jnp.where(block == 2, full[128:192], full[192:]),
        ) * 0.5
        g_root = yield from pull_root(e, state)
        t0 = state[0]
        loss = jnp.sum(jnp.where(mine, c * moved, 0.0), axis=0, keepdims=True) * 0.5
        loss = loss + g_mean[:1] * mean_weight[:1] + jnp.sum(g_root * t0, axis=0, keepdims=True)
        loss = block_sum(jnp.broadcast_to(loss, (8, width)))
        yield
        g_gram = (g_root - loss[:1] * t0) * inv[:1]
        g_y = 2.0 * times(scaled_pair, block_of(halves(g_gram))) + gain * g_forcing[:1]
        yield
        g_d = scaled * g_forcing[:1]
        low = lax.broadcasted_iota(jnp.int32, (WINDOW, 128), 1) < 64
        go_ref[at, :] += jnp.where(low, fold(g_y), fold(g_d))
        return update, pull

    def close_pair(opened, updates, pulls):
        pieces, centre, c_sum = opened[:3]
        update = centre + jnp.where(left_half, updates[0], updates[1])
        pull = jnp.where(left_half, pulls[0], pulls[1])
        pull = pull + (c_sum - block_sum(pull)) * (1.0 / MEMBERS)
        for n, (v, at) in enumerate(pieces):
            x_ref[v, at, :] = update[8 * n : 8 * n + 8]
            c_ref[v, at, :] = pull[8 * n : 8 * n + 8]

    def group_of_pairs(g, carry):
        pairs = [PAIRS * g + k for k in range(PAIRS)]
        opened = [open_pair(p) for p in pairs]
        done = in_step([one_quad(p, q, o) for p, o in zip(pairs, opened) for q in range(2)])
        for k, o in enumerate(opened):
            close_pair(o, *zip(*done[2 * k : 2 * k + 2]))
        return carry

    lax.fori_loop(0, QUADS // (2 * PAIRS), group_of_pairs, 0)

    for src, dst in ((x_ref, up_ref), (c_ref, gr_ref)):

        def turn_back(v, carry, src=src, dst=dst):
            for h in range(2):
                tall = src[v, :, 128 * h : 128 * h + 128].T
                for k in range(2):
                    for s in range(8):
                        at = 64 * k + 8 * s
                        dst[s, v * 4 + 2 * h + k] = tall[at : at + 8]
            return carry

        lax.fori_loop(0, VARS, turn_back, 0)

    for o in range(4):
        got = go_ref[pl.ds(o, WINDOW, stride=4), :]
        got = got - jnp.sum(got, axis=1, keepdims=True) * (1.0 / MEMBERS)
        tall = jnp.concatenate([got, jnp.zeros((128 - WINDOW, 128), f32)], axis=0).T
        for s in range(8):
            gr_ref[s, 24 + o] = tall[8 * s : 8 * s + 8]


def ring(value, up):
    count = lax.axis_size("space")
    if up:
        pairs = [((i + 1) % count, i) for i in range(count)]
    else:
        pairs = [(i, (i + 1) % count) for i in range(count)]
    return lax.ppermute(value, "space", pairs)


def swap(value):
    return lax.all_to_all(value, "member", split_axis=0, concat_axis=0, tiled=True)


def plane_scratch(rows):
    return pltpu.VMEM((VARS, rows, PER_DEV, COLS), f32)


def shards(initial_ensemble, obs_value, obs_error, obs_location, patch_obs, cotangent):
    shape = initial_ensemble.shape
    edge = (VARS * HALO, PER_DEV, COLS)
    half = (VARS * 4, PER_DEV, COLS)
    size = 4 * PER_DEV * STRIDE * COLS

    state = initial_ensemble
    first, last = call(edge_kernel, [edge, edge], [], 1000, 2 * size, state)
    first, last, cotangent = lax.optimization_barrier((first, last, cotangent))
    bot = ring(first, True)
    top = ring(last, False)

    (cot_sent,) = call(cot_kernel, [(8, 24, PER_DEV, 128)], [], 1000, 2 * size, cotangent)
    cot_owned = swap(cot_sent)

    position = lax.axis_index("member") * (NOBS // 8)
    plane = obs_location[0] // COLS
    chosen = plane.reshape(COLS, 4).T
    meta = jnp.stack([obs_value[0], (plane % ROWS).astype(f32), obs_error[0]])
    meta = jnp.concatenate([meta[:, -32:], meta, meta[:, :32]], axis=1)
    meta = lax.dynamic_slice_in_dim(meta, position, LOCAL_OBS, axis=1)
    meta = jnp.broadcast_to(meta[:, :, None], (3, LOCAL_OBS, 128))
    lists = (patch_obs[0] - position + 32) % NOBS
    lists = lists.reshape(QUADS, 256) - 16 * jnp.arange(QUADS, dtype=jnp.int32)[:, None]

    fore_sent, mid = call(
        forward_kernel,
        [(8, 28, PER_DEV, 128), (VARS, 16, PER_DEV, COLS)],
        [plane_scratch(ROWS + 2 * HALO), plane_scratch(ROWS)],
        10**7, 5 * size, state, top, bot, chosen,
    )
    fore_owned = swap(fore_sent)

    cells = pltpu.VMEM((VARS, 128, 256), f32)
    update_sent, grad_sent = call(
        analysis_kernel,
        [(8, 24, PER_DEV, 128), (8, 28, PER_DEV, 128)],
        [
            cells, cells, pltpu.VMEM((LOCAL_OBS, 128), f32), pltpu.VMEM((LOCAL_OBS, 128), f32),
            pltpu.VMEM((LOCAL_OBS, 128), f32), pltpu.VMEM((256, 256), bf16),
        ],
        10**10, 5 * size, fore_owned, cot_owned, lists, meta,
    )
    update = swap(update_sent)
    grad = swap(grad_sent)

    g, g_first, g_last = call(
        collect_kernel, [(STRIDE, PER_DEV, COLS), half, half], [], 10**6, 3 * size, grad, chosen
    )
    g_bot = ring(g_first, True)
    g_top = ring(g_last, False)
    (analysis,) = call(place_kernel, [shape], [], 1000, 2 * size, update)
    (gradient,) = call(
        backward_kernel,
        [shape],
        [plane_scratch(ROWS + 2 * HALO)] + [plane_scratch(16)] * 3,
        10**7, 6 * size, state, top, bot, mid, g, g_top, g_bot,
    )
    return analysis, gradient


def solution(mesh):
    placed = (
        P("member", None, "space", None),
        P("space", None),
        P("space", None),
        P("space", None),
        P("space", "member", None),
        P("member", None, "space", None),
    )
    return jax.shard_map(
        shards,
        mesh=mesh,
        in_specs=placed,
        out_specs=(P("member", None, "space", None), P("member", None, "space", None)),
        check_vma=False,
    )
```

```python
import functools
import math

import jax
import jax.numpy as jnp
from jax import lax
from jax.experimental import pallas as pl
from jax.experimental.pallas import tpu as pltpu
from jax.sharding import PartitionSpec as P

VARS = 6
ROWS = 8
COLS = 512
MEMBERS = 64
PER_DEV = 8
STRIDE = VARS * ROWS
NOBS = 2048
WINDOW = 80
LOCAL_OBS = 320
QUADS = 16
HALO = 6
PAIRS = 4
LOC_R = 8

time_step = 0.2
f32 = jnp.float32
bf16 = jnp.bfloat16
VMEM_LIMIT = 50 * 1024 * 1024


def call(kernel, outs, scratch, flops, moved, *args):
    spec = pl.BlockSpec(memory_space=pltpu.VMEM)
    return pl.pallas_call(
        kernel,
        out_shape=[jax.ShapeDtypeStruct(s, f32) for s in outs],
        in_specs=[spec] * len(args),
        out_specs=[spec] * len(outs),
        scratch_shapes=scratch,
        compiler_params=pltpu.CompilerParams(vmem_limit_bytes=VMEM_LIMIT),
        cost_estimate=pl.CostEstimate(flops=flops, bytes_accessed=moved, transcendentals=0),
    )(*args)


def lane_shift(q, by):
    return pltpu.roll(q, by % COLS, 1)


def col_diff(q):
    near = lane_shift(q, -1) - lane_shift(q, 1)
    far = lane_shift(q, -2) - lane_shift(q, 2)
    return near * (8.0 / 12.0) - far * (1.0 / 12.0)


def row_diff(ref, v, i):
    near = ref[v, i + 1] - ref[v, i - 1]
    far = ref[v, i + 2] - ref[v, i - 2]
    return near * (8.0 / 12.0) - far * (1.0 / 12.0)


def tendency(ref, i):
    rates = [None] * VARS
    for l in range(2):
        u, v, b = ref[l, i], ref[2 + l, i], ref[4 + l, i]
        ru, rv, rb = (row_diff(ref, k + l, i) for k in (0, 2, 4))
        cu, cv, cb = col_diff(u), col_diff(v), col_diff(b)
        rates[l] = 0.5 * v - (u * ru + v * cu) - rb + 0.3 * (ref[1 - l, i] - u)
        rates[2 + l] = -0.5 * u - (u * rv + v * cv) - cb + 0.3 * (ref[3 - l, i] - v)
        rates[4 + l] = -(u * rb + v * cb) - (ru + cv) + 0.3 * (ref[5 - l, i] - b)
    return rates


def planes_of(x_ref, v):
    return jnp.swapaxes(x_ref[:, v], 0, 1)


def edge_kernel(x_ref, first_ref, last_ref):
    for v in range(VARS):
        planes = planes_of(x_ref, v)
        first_ref[HALO * v : HALO * v + HALO] = planes[:HALO]
        last_ref[HALO * v : HALO * v + HALO] = planes[ROWS - HALO :]


def pack_planes(even, odd, store):
    low = lax.broadcasted_iota(jnp.int32, (PER_DEV, 128), 1) < 64
    for t in range(4):
        a, b = even[:, 128 * t : 128 * t + 128], odd[:, 128 * t : 128 * t + 128]
        store(2 * t, jnp.where(low, a, pltpu.roll(b, 64, 1)))
        store(2 * t + 1, jnp.where(low, pltpu.roll(a, 64, 1), b))


def unpack_planes(load):
    low = lax.broadcasted_iota(jnp.int32, (PER_DEV, 128), 1) < 64
    even, odd = [], []
    for t in range(4):
        a, b = load(2 * t), load(2 * t + 1)
        even.append(jnp.where(low, a, pltpu.roll(b, 64, 1)))
        odd.append(jnp.where(low, pltpu.roll(a, 64, 1), b))
    return jnp.concatenate(even, axis=1), jnp.concatenate(odd, axis=1)


def cot_kernel(x_ref, out_ref):
    for v in range(VARS):
        planes = planes_of(x_ref, v)
        for r in range(4):

            def store(d, value, t=v * 4 + r):
                out_ref[d, t] = value

            pack_planes(planes[2 * r], planes[2 * r + 1], store)


def load_state(s_ref, x_ref, top_ref, bot_ref):
    for v in range(VARS):
        s_ref[v, HALO : HALO + ROWS] = planes_of(x_ref, v)
        for r in range(HALO):
            s_ref[v, r] = top_ref[v * HALO + r]
            s_ref[v, HALO + ROWS + r] = bot_ref[v * HALO + r]


def forward_kernel(x_ref, top_ref, bot_ref, sel_ref, out_ref, mid_ref, s_ref, fore_ref):
    load_state(s_ref, x_ref, top_ref, bot_ref)

    def middle(i, carry):
        rates = tendency(s_ref, i + 2)
        for v in range(VARS):
            mid_ref[v, i] = s_ref[v, i + 2] + time_step * rates[v]
        return carry

    lax.fori_loop(0, 16, middle, 0, unroll=4)

    def finish(i, carry):
        rates = tendency(mid_ref, i + 4)
        for v in range(VARS):
            fore_ref[v, i] = 0.5 * (s_ref[v, i + HALO] + mid_ref[v, i + 4]) + 0.5 * time_step * rates[v]
        return carry

    lax.fori_loop(0, ROWS, finish, 0, unroll=4)

    def pack(v, carry):
        for r in range(4):

            def store(d, value, r=r):
                out_ref[d, v * 4 + r] = value

            pack_planes(fore_ref[v, 2 * r], fore_ref[v, 2 * r + 1], store)
        return carry

    lax.fori_loop(0, VARS, pack, 0, unroll=2)

    for o in range(4):
        chosen = jnp.broadcast_to(sel_ref[o : o + 1, :], (PER_DEV, COLS))

        def pick(v, acc, chosen=chosen):
            for r in range(ROWS):
                acc = jnp.where(chosen == v * ROWS + r, fore_ref[v, r], acc)
            return acc

        seen = lax.fori_loop(0, VARS, pick, jnp.zeros((PER_DEV, COLS), f32), unroll=2)
        for d in range(8):
            out_ref[d, 24 + o] = lane_shift(seen, 8 - 64 * d)[:, :128]


def collect_kernel(got_ref, sel_ref, g_ref, first_ref, last_ref):
    lane = lax.broadcasted_iota(jnp.int32, (PER_DEV, 128), 1)
    sums, chosen = [], []
    for o in range(4):
        total = jnp.zeros((PER_DEV, COLS), f32)
        for d in range(8):
            piece = jnp.where(lane < WINDOW, got_ref[d, 24 + o], 0.0)
            wide = jnp.concatenate([piece, jnp.zeros((PER_DEV, COLS - 128), f32)], axis=1)
            total = total + lane_shift(wide, 64 * d - 8)
        sums.append(total)
        chosen.append(jnp.broadcast_to(sel_ref[o : o + 1, :], (PER_DEV, COLS)))

    for v in range(VARS):
        for r in range(4):
            pair = unpack_planes(lambda d: got_ref[d, v * 4 + r])
            for k in range(2):
                row = 2 * r + k
                value = pair[k]
                for o in range(4):
                    value = value + jnp.where(chosen[o] == v * ROWS + row, sums[o], 0.0)
                g_ref[v * ROWS + row] = value
                if row < 4:
                    first_ref[v * 4 + row] = value
                else:
                    last_ref[v * 4 + row - 4] = value


def place_kernel(got_ref, out_ref):
    for v in range(VARS):
        planes = []
        for r in range(4):
            planes.extend(unpack_planes(lambda d: got_ref[d, v * 4 + r]))
        out_ref[:, v] = jnp.swapaxes(jnp.stack(planes), 0, 1)


def pull_products(s_ref, g_ref, prod_ref, start, stop, shift):
    def body(i, carry):
        for l in range(2):
            u = s_ref[l, i + shift]
            gu, gv, gb = g_ref[l, i], g_ref[2 + l, i], g_ref[4 + l, i]
            prod_ref[l, i] = u * gu + gb
            prod_ref[2 + l, i] = u * gv
            prod_ref[4 + l, i] = u * gb + gu
        return carry

    lax.fori_loop(start, stop, body, 0, unroll=2)


def pull_row(s_ref, g_ref, prod_ref, i, shift):
    out = [None] * VARS
    for l in range(2):
        u, v, b = (s_ref[k + l, i + shift] for k in (0, 2, 4))
        gu, gv, gb = g_ref[l, i], g_ref[2 + l, i], g_ref[4 + l, i]
        ru, rv, rb = (row_diff(s_ref, k + l, i + shift) for k in (0, 2, 4))
        cu, cv, cb = col_diff(u), col_diff(v), col_diff(b)
        out[l] = (
            row_diff(prod_ref, l, i) + col_diff(v * gu)
            - (gu * ru + gv * rv + gb * rb) - 0.5 * gv + 0.3 * (g_ref[1 - l, i] - gu)
        )
        out[2 + l] = (
            row_diff(prod_ref, 2 + l, i) + col_diff(v * gv + gb)
            - (gu * cu + gv * cv + gb * cb) + 0.5 * gu + 0.3 * (g_ref[3 - l, i] - gv)
        )
        out[4 + l] = (
            row_diff(prod_ref, 4 + l, i) + col_diff(v * gb + gv) + 0.3 * (g_ref[5 - l, i] - gb)
        )
    return out


def backward_kernel(
    x_ref, top_ref, bot_ref, mid_ref, g_ref, g_top_ref, g_bot_ref,
    out_ref, s_ref, c_ref, prod_ref, gm_ref,
):
    load_state(s_ref, x_ref, top_ref, bot_ref)
    for v in range(VARS):
        for r in range(ROWS):
            c_ref[v, 4 + r] = g_ref[v * ROWS + r]
        for r in range(4):
            c_ref[v, r] = g_top_ref[v * 4 + r]
            c_ref[v, 12 + r] = g_bot_ref[v * 4 + r]

    pull_products(mid_ref, c_ref, prod_ref, 0, 16, 0)

    def second(i, carry):
        got = pull_row(mid_ref, c_ref, prod_ref, i, 0)
        for v in range(VARS):
            gm_ref[v, i] = 0.5 * time_step * got[v]
        return carry

    lax.fori_loop(2, 14, second, 0, unroll=4)

    def combine(i, carry):
        for v in range(VARS):
            g, gm = c_ref[v, i], gm_ref[v, i]
            c_ref[v, i] = 0.5 * time_step * g + time_step * gm
            gm_ref[v, i] = g + gm
        return carry

    lax.fori_loop(2, 14, combine, 0, unroll=2)
    pull_products(s_ref, c_ref, prod_ref, 2, 14, HALO - 4)

    def first(i, carry):
        got = pull_row(s_ref, c_ref, prod_ref, i, HALO - 4)
        for v in range(VARS):
            gm_ref[v, i] = gm_ref[v, i] + got[v]
        return carry

    lax.fori_loop(4, 12, first, 0, unroll=4)
    for v in range(VARS):
        out_ref[:, v] = jnp.swapaxes(gm_ref[v, 4:12], 0, 1)


def halves(x):
    high = x.astype(bf16)
    return high, (x - high.astype(f32)).astype(bf16)


def dot(a, b):
    return lax.dot_general(a, b, (((1,), (0,)), ((), ())), preferred_element_type=f32)


def dot_first(a, b):
    return lax.dot_general(a, b, (((0,), (0,)), ((), ())), preferred_element_type=f32)


def times(left, right, product=dot):
    lh, ll = left
    rh, rl = right
    if product is dot_first:
        return product(lh, rh) + (product(lh, rl) + product(ll, rh))
    n = lh.shape[0]
    if n % 16:
        return product(lh, rh) + (product(lh, rl) + product(ll, rh))
    both = product(jnp.concatenate([lh, ll], axis=0), rh)
    return both[:n] + (both[n:] + product(lh, rl))


def in_step(jobs):
    results = [None] * len(jobs)
    left = list(range(len(jobs)))
    while left:
        for n in list(left):
            try:
                next(jobs[n])
            except StopIteration as done:
                results[n] = done.value
                left.remove(n)
    return results


def stack(*parts):
    return tuple(jnp.concatenate(p, axis=0) for p in zip(*parts))


def analysis_kernel(
    fore_ref, cot_ref, list_ref, meta_ref, up_ref, gr_ref, x_ref, c_ref, y_ref, d_ref, go_ref, block_ref
):
    width = 4 * MEMBERS
    block_row = lax.broadcasted_iota(jnp.int32, (width, width), 0) // MEMBERS
    block_col = lax.broadcasted_iota(jnp.int32, (width, width), 1) // MEMBERS
    block_ref[...] = jnp.where(block_row == block_col, 1.0, 0.0).astype(bf16)

    for src, dst in ((fore_ref, x_ref), (cot_ref, c_ref)):

        def turn(v, carry, src=src, dst=dst):
            for h in range(2):
                tall = [src[s, v * 4 + 2 * h + k] for k in range(2) for s in range(8)]
                dst[v, :, 128 * h : 128 * h + 128] = jnp.concatenate(tall, axis=0).T
            return carry

        lax.fori_loop(0, VARS, turn, 0)

    for o in range(4):
        tall = [fore_ref[s, 24 + o] for s in range(8)]
        seen = jnp.concatenate(tall + tall, axis=0).T[:WINDOW]
        mean = jnp.sum(seen, axis=1, keepdims=True) * (1.0 / 128.0)
        spread = seen - mean
        at = pl.ds(o, WINDOW, stride=4)
        y_ref[at, :] = spread
        d_ref[at, :] = meta_ref[0, at, :] - mean
    go_ref[...] = jnp.zeros(go_ref.shape, f32)

    def block_of(pair):
        mask = block_ref[...]
        return tuple(jnp.concatenate([p] * 4, axis=0) * mask for p in pair)

    def block_sum(x):
        high, low = halves(x)
        return dot(high, block_ref[...]) + dot(low, block_ref[...])

    def row_sum(x):
        return block_sum(jnp.broadcast_to(jnp.sum(x, axis=0, keepdims=True), (8, width)))

    def one_row(x, right):
        return times(halves(x), right)

    lane = lax.broadcasted_iota(jnp.int32, (MEMBERS, width), 1)
    sub = lax.broadcasted_iota(jnp.int32, (MEMBERS, width), 0)
    identity = jnp.where(lane % MEMBERS == sub, 1.0, 0.0)
    entry = lax.broadcasted_iota(jnp.int32, (WINDOW, width), 0)
    patch_row = (lax.broadcasted_iota(jnp.int32, (WINDOW, width), 1) // MEMBERS).astype(f32)
    col_gap = (entry // 4).astype(f32) - 9.5
    col_gap_sq = col_gap * col_gap
    left_half = lax.broadcasted_iota(jnp.int32, (96, width), 0) % 8 < 4
    row8 = lax.broadcasted_iota(jnp.int32, (8, width), 0)

    def solve(quad):
        at = pl.ds(pl.multiple_of(16 * quad, 16), WINDOW)
        lists = list_ref[pl.ds(quad, 1), :]
        hits = jnp.where(jnp.broadcast_to(lists, (WINDOW, width)) == entry, 1.0, 0.0).astype(bf16)
        count = dot(hits, block_ref[...])
        yield
        obs_row = jnp.concatenate([meta_ref[1, at, :]] * 2, axis=1)
        error = jnp.concatenate([meta_ref[2, at, :]] * 2, axis=1)
        row_gap = obs_row - 2.0 * patch_row - 0.5
        weight = count * jnp.exp((row_gap * row_gap + col_gap_sq) * (-1.0 / (2.0 * LOC_R * LOC_R))) / error
        y = y_ref[at, :]
        scaled = weight * jnp.concatenate([y, y], axis=1)
        d = d_ref[at, :]
        gain = weight * jnp.concatenate([d, d], axis=1)
        scaled_pair = halves(scaled)
        gram = times(halves(y[:, :MEMBERS]), scaled_pair, dot_first) + (MEMBERS - 1.0) * identity
        yield
        inv = lax.rsqrt(row_sum(gram * gram))
        yield
        t0 = gram * inv[:1]
        forcing = jnp.sum(scaled * jnp.concatenate([d, d], axis=1), axis=0, keepdims=True)
        forcing = jnp.broadcast_to(forcing, (8, width))

        m0 = 1.5 * identity - 0.5 * t0
        z1 = halves(m0)
        r0 = block_of(z1)
        t0p = halves(t0)
        u0 = halves(times(t0p, r0))
        yield
        t1f = times(u0, r0)
        yield
        t1 = halves(t1f)
        r1 = block_of(halves(1.5 * identity - 0.5 * t1f))
        both = times(stack(z1, t1), r1)
        yield
        z2, u1 = halves(both[:MEMBERS]), halves(both[MEMBERS:])
        t2f = times(u1, r1)
        yield
        t2 = halves(t2f)
        r2 = block_of(halves(1.5 * identity - 0.5 * t2f))
        both = times(stack(z2, t2), r2)
        yield
        z3, u2 = halves(both[:MEMBERS]), halves(both[MEMBERS:])
        t3f = times(u2, r2)
        yield
        r3 = block_of(halves(1.5 * identity - 0.5 * t3f))
        z4 = block_of(halves(times(z3, r3)))
        yield
        half_way = one_row(forcing, z4)
        yield
        mean_weight = one_row(half_way, z4) * inv
        yield
        state = (t0, t0p, u0, t1, u1, t2, u2, z1, z2, z3, r0, r1, r2, r3)
        return at, inv, z4, forcing, half_way, mean_weight, scaled, scaled_pair, gain, state

    def pull_root(e, state):
        t0, t0p, u0, t1, u1, t2, u2, z1, z2, z3, r0, r1, r2, r3 = state
        dt0 = halves(e)
        dm = halves(-0.5 * e)
        s0 = block_of(dm)
        du0 = halves(times(dt0, r0) + times(t0p, s0))
        yield
        dt1f = times(du0, r0) + times(u0, s0)
        yield
        dt1 = halves(dt1f)
        s1 = block_of(halves(-0.5 * dt1f))
        both = times(stack(dm, dt1), r1) + times(stack(z1, t1), s1)
        yield
        dz2, du1 = halves(both[:MEMBERS]), halves(both[MEMBERS:])
        dt2f = times(du1, r1) + times(u1, s1)
        yield
        dt2 = halves(dt2f)
        s2 = block_of(halves(-0.5 * dt2f))
        both = times(stack(dz2, dt2), r2) + times(stack(z2, t2), s2)
        yield
        dz3, du2 = halves(both[:MEMBERS]), halves(both[MEMBERS:])
        dt3f = times(du2, r2) + times(u2, s2)
        yield
        s3 = block_of(halves(-0.5 * dt3f))
        got = times(dz3, r3) + times(z3, s3)
        yield
        return got

    def fold(x):
        x = x[:, :128] + x[:, 128:]
        return x + pltpu.roll(x, 64, 1)

    def open_pair(p):
        pieces = [
            (v, pl.ds(pl.multiple_of(64 * k + 8 * p, 8), 8)) for v in range(VARS) for k in range(2)
        ]
        x = jnp.concatenate([x_ref[v, at, :] for v, at in pieces], axis=0)
        c = jnp.concatenate([c_ref[v, at, :] for v, at in pieces], axis=0)
        both = block_sum(jnp.concatenate([x, c], axis=0))
        centre = both[:96] * (1.0 / MEMBERS)
        c_sum = both[96:]
        a = x - centre
        a_c = halves(jnp.concatenate([a, c], axis=0))

        return pieces, centre, c_sum, a, c, a_c

    def one_quad(p, q, opened):
        pieces, centre, c_sum, a, c, a_c = opened
        at, inv, z4, forcing, half_way, mean_weight, scaled, scaled_pair, gain, state = yield from solve(2 * p + q)
        alpha = math.sqrt(MEMBERS - 1.0) * jnp.sqrt(inv[:1])
        mine = left_half if q == 0 else jnp.logical_not(left_half)
        both = times(a_c, z4)
        yield
        moved = alpha * both[:96]
        update = moved + block_sum(a * mean_weight[:1])
        yield
        pull = alpha * both[96:] + c_sum * mean_weight[:1]
        a_mine = jnp.where(mine, a, 0.0)
        g_mean = jnp.broadcast_to(jnp.sum(a_mine * c_sum, axis=0, keepdims=True), (8, width))
        g_half = one_row(g_mean, z4) * inv
        yield
        g_forcing = one_row(g_half, z4)
        yield
        left = jnp.where(row8 == 0, g_mean * inv, jnp.where(row8 == 1, g_half, 0.0))
        right = jnp.where(row8 == 0, half_way, jnp.where(row8 == 1, forcing, 0.0))
        scaled_a = a_mine * alpha
        lhs = halves(jnp.concatenate([scaled_a, c, left, right], axis=0))
        rhs = halves(jnp.concatenate([c, scaled_a, right, left], axis=0))
        full = times(lhs, rhs, dot_first)
        yield
        block = lane // MEMBERS
        e = jnp.where(
            block < 2,
            jnp.where(block == 0, full[:64], full[64:128]),
            jnp.where(block == 2, full[128:192], full[192:]),
        ) * 0.5
        g_root = yield from pull_root(e, state)
        t0 = state[0]
        loss = jnp.sum(jnp.where(mine, c * moved, 0.0), axis=0, keepdims=True) * 0.5
        loss = loss + g_mean[:1] * mean_weight[:1] + jnp.sum(g_root * t0, axis=0, keepdims=True)
        loss = block_sum(jnp.broadcast_to(loss, (8, width)))
        yield
        g_gram = (g_root - loss[:1] * t0) * inv[:1]
        g_y = 2.0 * times(scaled_pair, block_of(halves(g_gram))) + gain * g_forcing[:1]
        yield
        g_d = scaled * g_forcing[:1]
        low = lax.broadcasted_iota(jnp.int32, (WINDOW, 128), 1) < 64
        go_ref[at, :] += jnp.where(low, fold(g_y), fold(g_d))
        return update, pull

    def close_pair(opened, updates, pulls):
        pieces, centre, c_sum = opened[:3]
        update = centre + jnp.where(left_half, updates[0], updates[1])
        pull = jnp.where(left_half, pulls[0], pulls[1])
        pull = pull + (c_sum - block_sum(pull)) * (1.0 / MEMBERS)
        for n, (v, at) in enumerate(pieces):
            x_ref[v, at, :] = update[8 * n : 8 * n + 8]
            c_ref[v, at, :] = pull[8 * n : 8 * n + 8]

    def group_of_pairs(g, carry):
        pairs = [PAIRS * g + k for k in range(PAIRS)]
        opened = [open_pair(p) for p in pairs]
        done = in_step([one_quad(p, q, o) for p, o in zip(pairs, opened) for q in range(2)])
        for k, o in enumerate(opened):
            close_pair(o, *zip(*done[2 * k : 2 * k + 2]))
        return carry

    lax.fori_loop(0, QUADS // (2 * PAIRS), group_of_pairs, 0)

    for src, dst in ((x_ref, up_ref), (c_ref, gr_ref)):

        def turn_back(v, carry, src=src, dst=dst):
            for h in range(2):
                tall = src[v, :, 128 * h : 128 * h + 128].T
                for k in range(2):
                    for s in range(8):
                        at = 64 * k + 8 * s
                        dst[s, v * 4 + 2 * h + k] = tall[at : at + 8]
            return carry

        lax.fori_loop(0, VARS, turn_back, 0)

    for o in range(4):
        got = go_ref[pl.ds(o, WINDOW, stride=4), :]
        got = got - jnp.sum(got, axis=1, keepdims=True) * (1.0 / MEMBERS)
        tall = jnp.concatenate([got, jnp.zeros((128 - WINDOW, 128), f32)], axis=0).T
        for s in range(8):
            gr_ref[s, 24 + o] = tall[8 * s : 8 * s + 8]


def ring(value, up):
    count = lax.axis_size("space")
    if up:
        pairs = [((i + 1) % count, i) for i in range(count)]
    else:
        pairs = [(i, (i + 1) % count) for i in range(count)]
    return lax.ppermute(value, "space", pairs)


def swap(value):
    return lax.all_to_all(value, "member", split_axis=0, concat_axis=0, tiled=True)


def plane_scratch(rows):
    return pltpu.VMEM((VARS, rows, PER_DEV, COLS), f32)


def shards(initial_ensemble, obs_value, obs_error, obs_location, patch_obs, cotangent):
    shape = initial_ensemble.shape
    edge = (VARS * HALO, PER_DEV, COLS)
    half = (VARS * 4, PER_DEV, COLS)
    size = 4 * PER_DEV * STRIDE * COLS

    state = initial_ensemble
    first, last = call(edge_kernel, [edge, edge], [], 1000, 2 * size, state)
    bot = ring(first, True)
    top = ring(last, False)
    (cot_sent,) = call(cot_kernel, [(8, 24, PER_DEV, 128)], [], 1000, 2 * size, cotangent)
    top, bot, cot_sent = lax.optimization_barrier((top, bot, cot_sent))
    cot_owned = swap(cot_sent)


    position = lax.axis_index("member") * (NOBS // 8)
    plane = obs_location[0] // COLS
    chosen = plane.reshape(COLS, 4).T
    meta = jnp.stack([obs_value[0], (plane % ROWS).astype(f32), obs_error[0]])
    meta = jnp.concatenate([meta[:, -32:], meta, meta[:, :32]], axis=1)
    meta = lax.dynamic_slice_in_dim(meta, position, LOCAL_OBS, axis=1)
    meta = jnp.broadcast_to(meta[:, :, None], (3, LOCAL_OBS, 128))
    lists = (patch_obs[0] - position + 32) % NOBS
    lists = lists.reshape(QUADS, 256) - 16 * jnp.arange(QUADS, dtype=jnp.int32)[:, None]

    fore_sent, mid = call(
        forward_kernel,
        [(8, 28, PER_DEV, 128), (VARS, 16, PER_DEV, COLS)],
        [plane_scratch(ROWS + 2 * HALO), plane_scratch(ROWS)],
        10**7, 5 * size, state, top, bot, chosen,
    )
    fore_owned = swap(fore_sent)

    cells = pltpu.VMEM((VARS, 128, 256), f32)
    update_sent, grad_sent = call(
        analysis_kernel,
        [(8, 24, PER_DEV, 128), (8, 28, PER_DEV, 128)],
        [
            cells, cells, pltpu.VMEM((LOCAL_OBS, 128), f32), pltpu.VMEM((LOCAL_OBS, 128), f32),
            pltpu.VMEM((LOCAL_OBS, 128), f32), pltpu.VMEM((256, 256), bf16),
        ],
        10**10, 5 * size, fore_owned, cot_owned, lists, meta,
    )
    grad = swap(grad_sent)

    g, g_first, g_last = call(
        collect_kernel, [(STRIDE, PER_DEV, COLS), half, half], [], 10**6, 3 * size, grad, chosen
    )
    g_bot = ring(g_first, True)
    g_top = ring(g_last, False)
    g_top, g_bot, update_sent = lax.optimization_barrier((g_top, g_bot, update_sent))
    update = swap(update_sent)
    (analysis,) = call(place_kernel, [shape], [], 1000, 2 * size, update)
    (gradient,) = call(
        backward_kernel,
        [shape],
        [plane_scratch(ROWS + 2 * HALO)] + [plane_scratch(16)] * 3,
        10**7, 6 * size, state, top, bot, mid, g, g_top, g_bot,
    )
    return analysis, gradient


def solution(mesh):
    placed = (
        P("member", None, "space", None),
        P("space", None),
        P("space", None),
        P("space", None),
        P("space", "member", None),
        P("member", None, "space", None),
    )
    return jax.shard_map(
        shards,
        mesh=mesh,
        in_specs=placed,
        out_specs=(P("member", None, "space", None), P("member", None, "space", None)),
        check_vma=False,
    )
```

```python
import functools
import math

import jax
import jax.numpy as jnp
from jax import lax
from jax.experimental import pallas as pl
from jax.experimental.pallas import tpu as pltpu
from jax.sharding import PartitionSpec as P

VARS = 6
ROWS = 8
COLS = 512
MEMBERS = 64
PER_DEV = 8
STRIDE = VARS * ROWS
NOBS = 2048
WINDOW = 80
LOCAL_OBS = 320
QUADS = 16
HALO = 6
PAIRS = 4
LOC_R = 8

time_step = 0.2
f32 = jnp.float32
bf16 = jnp.bfloat16
VMEM_LIMIT = 50 * 1024 * 1024


def call(kernel, outs, scratch, flops, moved, *args):
    spec = pl.BlockSpec(memory_space=pltpu.VMEM)
    return pl.pallas_call(
        kernel,
        out_shape=[jax.ShapeDtypeStruct(s, f32) for s in outs],
        in_specs=[spec] * len(args),
        out_specs=[spec] * len(outs),
        scratch_shapes=scratch,
        compiler_params=pltpu.CompilerParams(vmem_limit_bytes=VMEM_LIMIT),
        cost_estimate=pl.CostEstimate(flops=flops, bytes_accessed=moved, transcendentals=0),
    )(*args)


def lane_shift(q, by):
    return pltpu.roll(q, by % COLS, 1)


def col_diff(q):
    near = lane_shift(q, -1) - lane_shift(q, 1)
    far = lane_shift(q, -2) - lane_shift(q, 2)
    return near * (8.0 / 12.0) - far * (1.0 / 12.0)


def row_diff(ref, v, i):
    near = ref[v, i + 1] - ref[v, i - 1]
    far = ref[v, i + 2] - ref[v, i - 2]
    return near * (8.0 / 12.0) - far * (1.0 / 12.0)


def tendency(ref, i):
    rates = [None] * VARS
    for l in range(2):
        u, v, b = ref[l, i], ref[2 + l, i], ref[4 + l, i]
        ru, rv, rb = (row_diff(ref, k + l, i) for k in (0, 2, 4))
        cu, cv, cb = col_diff(u), col_diff(v), col_diff(b)
        rates[l] = 0.5 * v - (u * ru + v * cu) - rb + 0.3 * (ref[1 - l, i] - u)
        rates[2 + l] = -0.5 * u - (u * rv + v * cv) - cb + 0.3 * (ref[3 - l, i] - v)
        rates[4 + l] = -(u * rb + v * cb) - (ru + cv) + 0.3 * (ref[5 - l, i] - b)
    return rates


def planes_of(x_ref, v):
    return jnp.swapaxes(x_ref[:, v], 0, 1)


def edge_kernel(x_ref, first_ref, last_ref):
    for v in range(VARS):
        planes = planes_of(x_ref, v)
        first_ref[HALO * v : HALO * v + HALO] = planes[:HALO]
        last_ref[HALO * v : HALO * v + HALO] = planes[ROWS - HALO :]


def pack_planes(even, odd, store):
    low = lax.broadcasted_iota(jnp.int32, (PER_DEV, 128), 1) < 64
    for t in range(4):
        a, b = even[:, 128 * t : 128 * t + 128], odd[:, 128 * t : 128 * t + 128]
        store(2 * t, jnp.where(low, a, pltpu.roll(b, 64, 1)))
        store(2 * t + 1, jnp.where(low, pltpu.roll(a, 64, 1), b))


def unpack_planes(load):
    low = lax.broadcasted_iota(jnp.int32, (PER_DEV, 128), 1) < 64
    even, odd = [], []
    for t in range(4):
        a, b = load(2 * t), load(2 * t + 1)
        even.append(jnp.where(low, a, pltpu.roll(b, 64, 1)))
        odd.append(jnp.where(low, pltpu.roll(a, 64, 1), b))
    return jnp.concatenate(even, axis=1), jnp.concatenate(odd, axis=1)


def cot_kernel(x_ref, out_ref):
    for v in range(VARS):
        planes = planes_of(x_ref, v)
        for r in range(4):

            def store(d, value, t=v * 4 + r):
                out_ref[d, t] = value

            pack_planes(planes[2 * r], planes[2 * r + 1], store)


def load_state(s_ref, x_ref, top_ref, bot_ref):
    for v in range(VARS):
        s_ref[v, HALO : HALO + ROWS] = planes_of(x_ref, v)
        for r in range(HALO):
            s_ref[v, r] = top_ref[v * HALO + r]
            s_ref[v, HALO + ROWS + r] = bot_ref[v * HALO + r]


def forward_kernel(x_ref, top_ref, bot_ref, sel_ref, cot_ref, out_ref, mid_ref, s_ref, fore_ref):
    for d in range(8):
        out_ref[d, 28:] = cot_ref[d]
    load_state(s_ref, x_ref, top_ref, bot_ref)

    def middle(i, carry):
        rates = tendency(s_ref, i + 2)
        for v in range(VARS):
            mid_ref[v, i] = s_ref[v, i + 2] + time_step * rates[v]
        return carry

    lax.fori_loop(0, 16, middle, 0, unroll=4)

    def finish(i, carry):
        rates = tendency(mid_ref, i + 4)
        for v in range(VARS):
            fore_ref[v, i] = 0.5 * (s_ref[v, i + HALO] + mid_ref[v, i + 4]) + 0.5 * time_step * rates[v]
        return carry

    lax.fori_loop(0, ROWS, finish, 0, unroll=4)

    def pack(v, carry):
        for r in range(4):

            def store(d, value, r=r):
                out_ref[d, v * 4 + r] = value

            pack_planes(fore_ref[v, 2 * r], fore_ref[v, 2 * r + 1], store)
        return carry

    lax.fori_loop(0, VARS, pack, 0, unroll=2)

    for o in range(4):
        chosen = jnp.broadcast_to(sel_ref[o : o + 1, :], (PER_DEV, COLS))

        def pick(v, acc, chosen=chosen):
            for r in range(ROWS):
                acc = jnp.where(chosen == v * ROWS + r, fore_ref[v, r], acc)
            return acc

        seen = lax.fori_loop(0, VARS, pick, jnp.zeros((PER_DEV, COLS), f32), unroll=2)
        for d in range(8):
            out_ref[d, 24 + o] = lane_shift(seen, 8 - 64 * d)[:, :128]


def collect_kernel(got_ref, sel_ref, g_ref, first_ref, last_ref):
    lane = lax.broadcasted_iota(jnp.int32, (PER_DEV, 128), 1)
    sums, chosen = [], []
    for o in range(4):
        total = jnp.zeros((PER_DEV, COLS), f32)
        for d in range(8):
            piece = jnp.where(lane < WINDOW, got_ref[d, 24 + o], 0.0)
            wide = jnp.concatenate([piece, jnp.zeros((PER_DEV, COLS - 128), f32)], axis=1)
            total = total + lane_shift(wide, 64 * d - 8)
        sums.append(total)
        chosen.append(jnp.broadcast_to(sel_ref[o : o + 1, :], (PER_DEV, COLS)))

    for v in range(VARS):
        for r in range(4):
            pair = unpack_planes(lambda d: got_ref[d, v * 4 + r])
            for k in range(2):
                row = 2 * r + k
                value = pair[k]
                for o in range(4):
                    value = value + jnp.where(chosen[o] == v * ROWS + row, sums[o], 0.0)
                g_ref[v * ROWS + row] = value
                if row < 4:
                    first_ref[v * 4 + row] = value
                else:
                    last_ref[v * 4 + row - 4] = value


def place_kernel(got_ref, out_ref):
    for v in range(VARS):
        planes = []
        for r in range(4):
            planes.extend(unpack_planes(lambda d: got_ref[d, 28 + v * 4 + r]))
        out_ref[:, v] = jnp.swapaxes(jnp.stack(planes), 0, 1)


def pull_products(s_ref, g_ref, prod_ref, start, stop, shift):
    def body(i, carry):
        for l in range(2):
            u = s_ref[l, i + shift]
            gu, gv, gb = g_ref[l, i], g_ref[2 + l, i], g_ref[4 + l, i]
            prod_ref[l, i] = u * gu + gb
            prod_ref[2 + l, i] = u * gv
            prod_ref[4 + l, i] = u * gb + gu
        return carry

    lax.fori_loop(start, stop, body, 0, unroll=2)


def pull_row(s_ref, g_ref, prod_ref, i, shift):
    out = [None] * VARS
    for l in range(2):
        u, v, b = (s_ref[k + l, i + shift] for k in (0, 2, 4))
        gu, gv, gb = g_ref[l, i], g_ref[2 + l, i], g_ref[4 + l, i]
        ru, rv, rb = (row_diff(s_ref, k + l, i + shift) for k in (0, 2, 4))
        cu, cv, cb = col_diff(u), col_diff(v), col_diff(b)
        out[l] = (
            row_diff(prod_ref, l, i) + col_diff(v * gu)
            - (gu * ru + gv * rv + gb * rb) - 0.5 * gv + 0.3 * (g_ref[1 - l, i] - gu)
        )
        out[2 + l] = (
            row_diff(prod_ref, 2 + l, i) + col_diff(v * gv + gb)
            - (gu * cu + gv * cv + gb * cb) + 0.5 * gu + 0.3 * (g_ref[3 - l, i] - gv)
        )
        out[4 + l] = (
            row_diff(prod_ref, 4 + l, i) + col_diff(v * gb + gv) + 0.3 * (g_ref[5 - l, i] - gb)
        )
    return out


def backward_kernel(
    x_ref, top_ref, bot_ref, mid_ref, g_ref, g_top_ref, g_bot_ref,
    out_ref, s_ref, c_ref, prod_ref, gm_ref,
):
    load_state(s_ref, x_ref, top_ref, bot_ref)
    for v in range(VARS):
        for r in range(ROWS):
            c_ref[v, 4 + r] = g_ref[v * ROWS + r]
        for r in range(4):
            c_ref[v, r] = g_top_ref[v * 4 + r]
            c_ref[v, 12 + r] = g_bot_ref[v * 4 + r]

    pull_products(mid_ref, c_ref, prod_ref, 0, 16, 0)

    def second(i, carry):
        got = pull_row(mid_ref, c_ref, prod_ref, i, 0)
        for v in range(VARS):
            gm_ref[v, i] = 0.5 * time_step * got[v]
        return carry

    lax.fori_loop(2, 14, second, 0, unroll=4)

    def combine(i, carry):
        for v in range(VARS):
            g, gm = c_ref[v, i], gm_ref[v, i]
            c_ref[v, i] = 0.5 * time_step * g + time_step * gm
            gm_ref[v, i] = g + gm
        return carry

    lax.fori_loop(2, 14, combine, 0, unroll=2)
    pull_products(s_ref, c_ref, prod_ref, 2, 14, HALO - 4)

    def first(i, carry):
        got = pull_row(s_ref, c_ref, prod_ref, i, HALO - 4)
        for v in range(VARS):
            gm_ref[v, i] = gm_ref[v, i] + got[v]
        return carry

    lax.fori_loop(4, 12, first, 0, unroll=4)
    for v in range(VARS):
        out_ref[:, v] = jnp.swapaxes(gm_ref[v, 4:12], 0, 1)


def halves(x):
    high = x.astype(bf16)
    return high, (x - high.astype(f32)).astype(bf16)


def dot(a, b):
    return lax.dot_general(a, b, (((1,), (0,)), ((), ())), preferred_element_type=f32)


def dot_first(a, b):
    return lax.dot_general(a, b, (((0,), (0,)), ((), ())), preferred_element_type=f32)


def times(left, right, product=dot):
    lh, ll = left
    rh, rl = right
    if product is dot_first:
        return product(lh, rh) + (product(lh, rl) + product(ll, rh))
    n = lh.shape[0]
    if n % 16:
        return product(lh, rh) + (product(lh, rl) + product(ll, rh))
    both = product(jnp.concatenate([lh, ll], axis=0), rh)
    return both[:n] + (both[n:] + product(lh, rl))


def in_step(jobs):
    results = [None] * len(jobs)
    left = list(range(len(jobs)))
    while left:
        for n in list(left):
            try:
                next(jobs[n])
            except StopIteration as done:
                results[n] = done.value
                left.remove(n)
    return results


def stack(*parts):
    return tuple(jnp.concatenate(p, axis=0) for p in zip(*parts))


def analysis_kernel(
    got_ref, list_ref, meta_ref, out_ref, x_ref, c_ref, y_ref, d_ref, go_ref, block_ref
):
    width = 4 * MEMBERS
    block_row = lax.broadcasted_iota(jnp.int32, (width, width), 0) // MEMBERS
    block_col = lax.broadcasted_iota(jnp.int32, (width, width), 1) // MEMBERS
    block_ref[...] = jnp.where(block_row == block_col, 1.0, 0.0).astype(bf16)

    for first, dst in ((0, x_ref), (28, c_ref)):

        def turn(v, carry, first=first, dst=dst):
            for h in range(2):
                tall = [got_ref[s, first + v * 4 + 2 * h + k] for k in range(2) for s in range(8)]
                dst[v, :, 128 * h : 128 * h + 128] = jnp.concatenate(tall, axis=0).T
            return carry

        lax.fori_loop(0, VARS, turn, 0)

    for o in range(4):
        tall = [got_ref[s, 24 + o] for s in range(8)]
        seen = jnp.concatenate(tall + tall, axis=0).T[:WINDOW]
        mean = jnp.sum(seen, axis=1, keepdims=True) * (1.0 / 128.0)
        spread = seen - mean
        at = pl.ds(o, WINDOW, stride=4)
        y_ref[at, :] = spread
        d_ref[at, :] = meta_ref[0, at, :] - mean
    go_ref[...] = jnp.zeros(go_ref.shape, f32)

    def block_of(pair):
        mask = block_ref[...]
        return tuple(jnp.concatenate([p] * 4, axis=0) * mask for p in pair)

    def block_sum(x):
        high, low = halves(x)
        return dot(high, block_ref[...]) + dot(low, block_ref[...])

    def row_sum(x):
        return block_sum(jnp.broadcast_to(jnp.sum(x, axis=0, keepdims=True), (8, width)))

    def one_row(x, right):
        return times(halves(x), right)

    lane = lax.broadcasted_iota(jnp.int32, (MEMBERS, width), 1)
    sub = lax.broadcasted_iota(jnp.int32, (MEMBERS, width), 0)
    identity = jnp.where(lane % MEMBERS == sub, 1.0, 0.0)
    entry = lax.broadcasted_iota(jnp.int32, (WINDOW, width), 0)
    patch_row = (lax.broadcasted_iota(jnp.int32, (WINDOW, width), 1) // MEMBERS).astype(f32)
    col_gap = (entry // 4).astype(f32) - 9.5
    col_gap_sq = col_gap * col_gap
    left_half = lax.broadcasted_iota(jnp.int32, (96, width), 0) % 8 < 4
    row8 = lax.broadcasted_iota(jnp.int32, (8, width), 0)

    def solve(quad):
        at = pl.ds(pl.multiple_of(16 * quad, 16), WINDOW)
        lists = list_ref[pl.ds(quad, 1), :]
        hits = jnp.where(jnp.broadcast_to(lists, (WINDOW, width)) == entry, 1.0, 0.0).astype(bf16)
        count = dot(hits, block_ref[...])
        yield
        obs_row = jnp.concatenate([meta_ref[1, at, :]] * 2, axis=1)
        error = jnp.concatenate([meta_ref[2, at, :]] * 2, axis=1)
        row_gap = obs_row - 2.0 * patch_row - 0.5
        weight = count * jnp.exp((row_gap * row_gap + col_gap_sq) * (-1.0 / (2.0 * LOC_R * LOC_R))) / error
        y = y_ref[at, :]
        scaled = weight * jnp.concatenate([y, y], axis=1)
        d = d_ref[at, :]
        gain = weight * jnp.concatenate([d, d], axis=1)
        scaled_pair = halves(scaled)
        gram = times(halves(y[:, :MEMBERS]), scaled_pair, dot_first) + (MEMBERS - 1.0) * identity
        yield
        inv = lax.rsqrt(row_sum(gram * gram))
        yield
        t0 = gram * inv[:1]
        forcing = jnp.sum(scaled * jnp.concatenate([d, d], axis=1), axis=0, keepdims=True)
        forcing = jnp.broadcast_to(forcing, (8, width))

        m0 = 1.5 * identity - 0.5 * t0
        z1 = halves(m0)
        r0 = block_of(z1)
        t0p = halves(t0)
        u0 = halves(times(t0p, r0))
        yield
        t1f = times(u0, r0)
        yield
        t1 = halves(t1f)
        r1 = block_of(halves(1.5 * identity - 0.5 * t1f))
        both = times(stack(z1, t1), r1)
        yield
        z2, u1 = halves(both[:MEMBERS]), halves(both[MEMBERS:])
        t2f = times(u1, r1)
        yield
        t2 = halves(t2f)
        r2 = block_of(halves(1.5 * identity - 0.5 * t2f))
        both = times(stack(z2, t2), r2)
        yield
        z3, u2 = halves(both[:MEMBERS]), halves(both[MEMBERS:])
        t3f = times(u2, r2)
        yield
        r3 = block_of(halves(1.5 * identity - 0.5 * t3f))
        z4 = block_of(halves(times(z3, r3)))
        yield
        half_way = one_row(forcing, z4)
        yield
        mean_weight = one_row(half_way, z4) * inv
        yield
        state = (t0, t0p, u0, t1, u1, t2, u2, z1, z2, z3, r0, r1, r2, r3)
        return at, inv, z4, forcing, half_way, mean_weight, scaled, scaled_pair, gain, state

    def pull_root(e, state):
        t0, t0p, u0, t1, u1, t2, u2, z1, z2, z3, r0, r1, r2, r3 = state
        dt0 = halves(e)
        dm = halves(-0.5 * e)
        s0 = block_of(dm)
        du0 = halves(times(dt0, r0) + times(t0p, s0))
        yield
        dt1f = times(du0, r0) + times(u0, s0)
        yield
        dt1 = halves(dt1f)
        s1 = block_of(halves(-0.5 * dt1f))
        both = times(stack(dm, dt1), r1) + times(stack(z1, t1), s1)
        yield
        dz2, du1 = halves(both[:MEMBERS]), halves(both[MEMBERS:])
        dt2f = times(du1, r1) + times(u1, s1)
        yield
        dt2 = halves(dt2f)
        s2 = block_of(halves(-0.5 * dt2f))
        both = times(stack(dz2, dt2), r2) + times(stack(z2, t2), s2)
        yield
        dz3, du2 = halves(both[:MEMBERS]), halves(both[MEMBERS:])
        dt3f = times(du2, r2) + times(u2, s2)
        yield
        s3 = block_of(halves(-0.5 * dt3f))
        got = times(dz3, r3) + times(z3, s3)
        yield
        return got

    def fold(x):
        x = x[:, :128] + x[:, 128:]
        return x + pltpu.roll(x, 64, 1)

    def open_pair(p):
        pieces = [
            (v, pl.ds(pl.multiple_of(64 * k + 8 * p, 8), 8)) for v in range(VARS) for k in range(2)
        ]
        x = jnp.concatenate([x_ref[v, at, :] for v, at in pieces], axis=0)
        c = jnp.concatenate([c_ref[v, at, :] for v, at in pieces], axis=0)
        both = block_sum(jnp.concatenate([x, c], axis=0))
        centre = both[:96] * (1.0 / MEMBERS)
        c_sum = both[96:]
        a = x - centre
        a_c = halves(jnp.concatenate([a, c], axis=0))

        return pieces, centre, c_sum, a, c, a_c

    def one_quad(p, q, opened):
        pieces, centre, c_sum, a, c, a_c = opened
        at, inv, z4, forcing, half_way, mean_weight, scaled, scaled_pair, gain, state = yield from solve(2 * p + q)
        alpha = math.sqrt(MEMBERS - 1.0) * jnp.sqrt(inv[:1])
        mine = left_half if q == 0 else jnp.logical_not(left_half)
        both = times(a_c, z4)
        yield
        moved = alpha * both[:96]
        update = moved + block_sum(a * mean_weight[:1])
        yield
        pull = alpha * both[96:] + c_sum * mean_weight[:1]
        a_mine = jnp.where(mine, a, 0.0)
        g_mean = jnp.broadcast_to(jnp.sum(a_mine * c_sum, axis=0, keepdims=True), (8, width))
        g_half = one_row(g_mean, z4) * inv
        yield
        g_forcing = one_row(g_half, z4)
        yield
        left = jnp.where(row8 == 0, g_mean * inv, jnp.where(row8 == 1, g_half, 0.0))
        right = jnp.where(row8 == 0, half_way, jnp.where(row8 == 1, forcing, 0.0))
        scaled_a = a_mine * alpha
        lhs = halves(jnp.concatenate([scaled_a, c, left, right], axis=0))
        rhs = halves(jnp.concatenate([c, scaled_a, right, left], axis=0))
        full = times(lhs, rhs, dot_first)
        yield
        block = lane // MEMBERS
        e = jnp.where(
            block < 2,
            jnp.where(block == 0, full[:64], full[64:128]),
            jnp.where(block == 2, full[128:192], full[192:]),
        ) * 0.5
        g_root = yield from pull_root(e, state)
        t0 = state[0]
        loss = jnp.sum(jnp.where(mine, c * moved, 0.0), axis=0, keepdims=True) * 0.5
        loss = loss + g_mean[:1] * mean_weight[:1] + jnp.sum(g_root * t0, axis=0, keepdims=True)
        loss = block_sum(jnp.broadcast_to(loss, (8, width)))
        yield
        g_gram = (g_root - loss[:1] * t0) * inv[:1]
        g_y = 2.0 * times(scaled_pair, block_of(halves(g_gram))) + gain * g_forcing[:1]
        yield
        g_d = scaled * g_forcing[:1]
        low = lax.broadcasted_iota(jnp.int32, (WINDOW, 128), 1) < 64
        go_ref[at, :] += jnp.where(low, fold(g_y), fold(g_d))
        return update, pull

    def close_pair(opened, updates, pulls):
        pieces, centre, c_sum = opened[:3]
        update = centre + jnp.where(left_half, updates[0], updates[1])
        pull = jnp.where(left_half, pulls[0], pulls[1])
        pull = pull + (c_sum - block_sum(pull)) * (1.0 / MEMBERS)
        for n, (v, at) in enumerate(pieces):
            x_ref[v, at, :] = update[8 * n : 8 * n + 8]
            c_ref[v, at, :] = pull[8 * n : 8 * n + 8]

    def group_of_pairs(g, carry):
        pairs = [PAIRS * g + k for k in range(PAIRS)]
        opened = [open_pair(p) for p in pairs]
        done = in_step([one_quad(p, q, o) for p, o in zip(pairs, opened) for q in range(2)])
        for k, o in enumerate(opened):
            close_pair(o, *zip(*done[2 * k : 2 * k + 2]))
        return carry

    lax.fori_loop(0, QUADS // (2 * PAIRS), group_of_pairs, 0)

    for src, first in ((x_ref, 28), (c_ref, 0)):

        def turn_back(v, carry, src=src, first=first):
            for h in range(2):
                tall = src[v, :, 128 * h : 128 * h + 128].T
                for k in range(2):
                    for s in range(8):
                        at = 64 * k + 8 * s
                        out_ref[s, first + v * 4 + 2 * h + k] = tall[at : at + 8]
            return carry

        lax.fori_loop(0, VARS, turn_back, 0)

    for o in range(4):
        got = go_ref[pl.ds(o, WINDOW, stride=4), :]
        got = got - jnp.sum(got, axis=1, keepdims=True) * (1.0 / MEMBERS)
        tall = jnp.concatenate([got, jnp.zeros((128 - WINDOW, 128), f32)], axis=0).T
        for s in range(8):
            out_ref[s, 24 + o] = tall[8 * s : 8 * s + 8]


def ring(value, up):
    count = lax.axis_size("space")
    if up:
        pairs = [((i + 1) % count, i) for i in range(count)]
    else:
        pairs = [(i, (i + 1) % count) for i in range(count)]
    return lax.ppermute(value, "space", pairs)


def swap(value):
    return lax.all_to_all(value, "member", split_axis=0, concat_axis=0, tiled=True)


def plane_scratch(rows):
    return pltpu.VMEM((VARS, rows, PER_DEV, COLS), f32)


def shards(initial_ensemble, obs_value, obs_error, obs_location, patch_obs, cotangent):
    shape = initial_ensemble.shape
    edge = (VARS * HALO, PER_DEV, COLS)
    half = (VARS * 4, PER_DEV, COLS)
    size = 4 * PER_DEV * STRIDE * COLS

    state = initial_ensemble
    first, last = call(edge_kernel, [edge, edge], [], 1000, 2 * size, state)
    bot = ring(first, True)
    top = ring(last, False)

    position = lax.axis_index("member") * (NOBS // 8)
    plane = obs_location[0] // COLS
    chosen = plane.reshape(COLS, 4).T
    meta = jnp.stack([obs_value[0], (plane % ROWS).astype(f32), obs_error[0]])
    meta = jnp.concatenate([meta[:, -32:], meta, meta[:, :32]], axis=1)
    meta = lax.dynamic_slice_in_dim(meta, position, LOCAL_OBS, axis=1)
    meta = jnp.broadcast_to(meta[:, :, None], (3, LOCAL_OBS, 128))
    lists = (patch_obs[0] - position + 32) % NOBS
    lists = lists.reshape(QUADS, 256) - 16 * jnp.arange(QUADS, dtype=jnp.int32)[:, None]
    chosen, meta, lists, cotangent = lax.optimization_barrier((chosen, meta, lists, cotangent))
    (cot_sent,) = call(cot_kernel, [(8, 24, PER_DEV, 128)], [], 1000, 2 * size, cotangent)

    sent, mid = call(
        forward_kernel,
        [(8, 52, PER_DEV, 128), (VARS, 16, PER_DEV, COLS)],
        [plane_scratch(ROWS + 2 * HALO), plane_scratch(ROWS)],
        10**7, 6 * size, state, top, bot, chosen, cot_sent,
    )
    owned = swap(sent)

    cells = pltpu.VMEM((VARS, 128, 256), f32)
    (returned,) = call(
        analysis_kernel,
        [(8, 52, PER_DEV, 128)],
        [
            cells, cells, pltpu.VMEM((LOCAL_OBS, 128), f32), pltpu.VMEM((LOCAL_OBS, 128), f32),
            pltpu.VMEM((LOCAL_OBS, 128), f32), pltpu.VMEM((256, 256), bf16),
        ],
        10**10, 5 * size, owned, lists, meta,
    )
    got = swap(returned)

    g, g_first, g_last = call(
        collect_kernel, [(STRIDE, PER_DEV, COLS), half, half], [], 10**6, 3 * size, got, chosen
    )
    g_bot = ring(g_first, True)
    g_top = ring(g_last, False)
    (analysis,) = call(place_kernel, [shape], [], 1000, 2 * size, got)
    (gradient,) = call(
        backward_kernel,
        [shape],
        [plane_scratch(ROWS + 2 * HALO)] + [plane_scratch(16)] * 3,
        10**7, 6 * size, state, top, bot, mid, g, g_top, g_bot,
    )
    return analysis, gradient


def solution(mesh):
    placed = (
        P("member", None, "space", None),
        P("space", None),
        P("space", None),
        P("space", None),
        P("space", "member", None),
        P("member", None, "space", None),
    )
    return jax.shard_map(
        shards,
        mesh=mesh,
        in_specs=placed,
        out_specs=(P("member", None, "space", None), P("member", None, "space", None)),
        check_vma=False,
    )
```

```python
import functools
import math

import jax
import jax.numpy as jnp
from jax import lax
from jax.experimental import pallas as pl
from jax.experimental.pallas import tpu as pltpu
from jax.sharding import PartitionSpec as P

VARS = 6
ROWS = 8
COLS = 512
MEMBERS = 64
PER_DEV = 8
STRIDE = VARS * ROWS
NOBS = 2048
WINDOW = 80
LOCAL_OBS = 320
QUADS = 16
HALO = 6
TOGETHER = 8
CELLS = 48
LOC_R = 8

time_step = 0.2
f32 = jnp.float32
bf16 = jnp.bfloat16
VMEM_LIMIT = 50 * 1024 * 1024


def call(kernel, outs, scratch, flops, moved, *args):
    spec = pl.BlockSpec(memory_space=pltpu.VMEM)
    return pl.pallas_call(
        kernel,
        out_shape=[jax.ShapeDtypeStruct(s, f32) for s in outs],
        in_specs=[spec] * len(args),
        out_specs=[spec] * len(outs),
        scratch_shapes=scratch,
        compiler_params=pltpu.CompilerParams(vmem_limit_bytes=VMEM_LIMIT),
        cost_estimate=pl.CostEstimate(flops=flops, bytes_accessed=moved, transcendentals=0),
    )(*args)


def lane_shift(q, by):
    return pltpu.roll(q, by % COLS, 1)


def col_diff(q):
    near = lane_shift(q, -1) - lane_shift(q, 1)
    far = lane_shift(q, -2) - lane_shift(q, 2)
    return near * (8.0 / 12.0) - far * (1.0 / 12.0)


def row_diff(ref, v, i):
    near = ref[v, i + 1] - ref[v, i - 1]
    far = ref[v, i + 2] - ref[v, i - 2]
    return near * (8.0 / 12.0) - far * (1.0 / 12.0)


def tendency(ref, i):
    rates = [None] * VARS
    for l in range(2):
        u, v, b = ref[l, i], ref[2 + l, i], ref[4 + l, i]
        ru, rv, rb = (row_diff(ref, k + l, i) for k in (0, 2, 4))
        cu, cv, cb = col_diff(u), col_diff(v), col_diff(b)
        rates[l] = 0.5 * v - (u * ru + v * cu) - rb + 0.3 * (ref[1 - l, i] - u)
        rates[2 + l] = -0.5 * u - (u * rv + v * cv) - cb + 0.3 * (ref[3 - l, i] - v)
        rates[4 + l] = -(u * rb + v * cb) - (ru + cv) + 0.3 * (ref[5 - l, i] - b)
    return rates


def planes_of(x_ref, v):
    return jnp.swapaxes(x_ref[:, v], 0, 1)


def edge_kernel(x_ref, first_ref, last_ref):
    for v in range(VARS):
        planes = planes_of(x_ref, v)
        first_ref[HALO * v : HALO * v + HALO] = planes[:HALO]
        last_ref[HALO * v : HALO * v + HALO] = planes[ROWS - HALO :]


def pack_planes(even, odd, store):
    low = lax.broadcasted_iota(jnp.int32, (PER_DEV, 128), 1) < 64
    for t in range(4):
        a, b = even[:, 128 * t : 128 * t + 128], odd[:, 128 * t : 128 * t + 128]
        store(2 * t, jnp.where(low, a, pltpu.roll(b, 64, 1)))
        store(2 * t + 1, jnp.where(low, pltpu.roll(a, 64, 1), b))


def unpack_planes(load):
    low = lax.broadcasted_iota(jnp.int32, (PER_DEV, 128), 1) < 64
    even, odd = [], []
    for t in range(4):
        a, b = load(2 * t), load(2 * t + 1)
        even.append(jnp.where(low, a, pltpu.roll(b, 64, 1)))
        odd.append(jnp.where(low, pltpu.roll(a, 64, 1), b))
    return jnp.concatenate(even, axis=1), jnp.concatenate(odd, axis=1)


def cot_kernel(x_ref, out_ref):
    for v in range(VARS):
        planes = planes_of(x_ref, v)
        for r in range(4):

            def store(d, value, t=v * 4 + r):
                out_ref[d, t] = value

            pack_planes(planes[2 * r], planes[2 * r + 1], store)


def load_state(s_ref, x_ref, top_ref, bot_ref):
    for v in range(VARS):
        s_ref[v, HALO : HALO + ROWS] = planes_of(x_ref, v)
        for r in range(HALO):
            s_ref[v, r] = top_ref[v * HALO + r]
            s_ref[v, HALO + ROWS + r] = bot_ref[v * HALO + r]


def forward_kernel(x_ref, top_ref, bot_ref, sel_ref, cot_ref, out_ref, mid_ref, s_ref, fore_ref):
    for d in range(8):
        out_ref[d, 28:] = cot_ref[d]
    load_state(s_ref, x_ref, top_ref, bot_ref)

    def middle(i, carry):
        rates = tendency(s_ref, i + 2)
        for v in range(VARS):
            mid_ref[v, i] = s_ref[v, i + 2] + time_step * rates[v]
        return carry

    lax.fori_loop(0, 16, middle, 0, unroll=4)

    def finish(i, carry):
        rates = tendency(mid_ref, i + 4)
        for v in range(VARS):
            fore_ref[v, i] = 0.5 * (s_ref[v, i + HALO] + mid_ref[v, i + 4]) + 0.5 * time_step * rates[v]
        return carry

    lax.fori_loop(0, ROWS, finish, 0, unroll=4)

    def pack(v, carry):
        for r in range(4):

            def store(d, value, r=r):
                out_ref[d, v * 4 + r] = value

            pack_planes(fore_ref[v, 2 * r], fore_ref[v, 2 * r + 1], store)
        return carry

    lax.fori_loop(0, VARS, pack, 0, unroll=2)

    for o in range(4):
        chosen = jnp.broadcast_to(sel_ref[o : o + 1, :], (PER_DEV, COLS))

        def pick(v, acc, chosen=chosen):
            for r in range(ROWS):
                acc = jnp.where(chosen == v * ROWS + r, fore_ref[v, r], acc)
            return acc

        seen = lax.fori_loop(0, VARS, pick, jnp.zeros((PER_DEV, COLS), f32), unroll=2)
        for d in range(8):
            out_ref[d, 24 + o] = lane_shift(seen, 8 - 64 * d)[:, :128]


def collect_kernel(got_ref, sel_ref, g_ref, first_ref, last_ref):
    lane = lax.broadcasted_iota(jnp.int32, (PER_DEV, 128), 1)
    sums, chosen = [], []
    for o in range(4):
        total = jnp.zeros((PER_DEV, COLS), f32)
        for d in range(8):
            piece = jnp.where(lane < WINDOW, got_ref[d, 24 + o], 0.0)
            wide = jnp.concatenate([piece, jnp.zeros((PER_DEV, COLS - 128), f32)], axis=1)
            total = total + lane_shift(wide, 64 * d - 8)
        sums.append(total)
        chosen.append(jnp.broadcast_to(sel_ref[o : o + 1, :], (PER_DEV, COLS)))

    for v in range(VARS):
        for r in range(4):
            pair = unpack_planes(lambda d: got_ref[d, v * 4 + r])
            for k in range(2):
                row = 2 * r + k
                value = pair[k]
                for o in range(4):
                    value = value + jnp.where(chosen[o] == v * ROWS + row, sums[o], 0.0)
                g_ref[v * ROWS + row] = value
                if row < 4:
                    first_ref[v * 4 + row] = value
                else:
                    last_ref[v * 4 + row - 4] = value


def place_kernel(got_ref, out_ref):
    for v in range(VARS):
        planes = []
        for r in range(4):
            planes.extend(unpack_planes(lambda d: got_ref[d, 28 + v * 4 + r]))
        out_ref[:, v] = jnp.swapaxes(jnp.stack(planes), 0, 1)


def pull_products(s_ref, g_ref, prod_ref, start, stop, shift):
    def body(i, carry):
        for l in range(2):
            u = s_ref[l, i + shift]
            gu, gv, gb = g_ref[l, i], g_ref[2 + l, i], g_ref[4 + l, i]
            prod_ref[l, i] = u * gu + gb
            prod_ref[2 + l, i] = u * gv
            prod_ref[4 + l, i] = u * gb + gu
        return carry

    lax.fori_loop(start, stop, body, 0, unroll=2)


def pull_row(s_ref, g_ref, prod_ref, i, shift):
    out = [None] * VARS
    for l in range(2):
        u, v, b = (s_ref[k + l, i + shift] for k in (0, 2, 4))
        gu, gv, gb = g_ref[l, i], g_ref[2 + l, i], g_ref[4 + l, i]
        ru, rv, rb = (row_diff(s_ref, k + l, i + shift) for k in (0, 2, 4))
        cu, cv, cb = col_diff(u), col_diff(v), col_diff(b)
        out[l] = (
            row_diff(prod_ref, l, i) + col_diff(v * gu)
            - (gu * ru + gv * rv + gb * rb) - 0.5 * gv + 0.3 * (g_ref[1 - l, i] - gu)
        )
        out[2 + l] = (
            row_diff(prod_ref, 2 + l, i) + col_diff(v * gv + gb)
            - (gu * cu + gv * cv + gb * cb) + 0.5 * gu + 0.3 * (g_ref[3 - l, i] - gv)
        )
        out[4 + l] = (
            row_diff(prod_ref, 4 + l, i) + col_diff(v * gb + gv) + 0.3 * (g_ref[5 - l, i] - gb)
        )
    return out


def backward_kernel(
    x_ref, top_ref, bot_ref, mid_ref, g_ref, g_top_ref, g_bot_ref,
    out_ref, s_ref, c_ref, prod_ref, gm_ref,
):
    load_state(s_ref, x_ref, top_ref, bot_ref)
    for v in range(VARS):
        for r in range(ROWS):
            c_ref[v, 4 + r] = g_ref[v * ROWS + r]
        for r in range(4):
            c_ref[v, r] = g_top_ref[v * 4 + r]
            c_ref[v, 12 + r] = g_bot_ref[v * 4 + r]

    pull_products(mid_ref, c_ref, prod_ref, 0, 16, 0)

    def second(i, carry):
        got = pull_row(mid_ref, c_ref, prod_ref, i, 0)
        for v in range(VARS):
            gm_ref[v, i] = 0.5 * time_step * got[v]
        return carry

    lax.fori_loop(2, 14, second, 0, unroll=4)

    def combine(i, carry):
        for v in range(VARS):
            g, gm = c_ref[v, i], gm_ref[v, i]
            c_ref[v, i] = 0.5 * time_step * g + time_step * gm
            gm_ref[v, i] = g + gm
        return carry

    lax.fori_loop(2, 14, combine, 0, unroll=2)
    pull_products(s_ref, c_ref, prod_ref, 2, 14, HALO - 4)

    def first(i, carry):
        got = pull_row(s_ref, c_ref, prod_ref, i, HALO - 4)
        for v in range(VARS):
            gm_ref[v, i] = gm_ref[v, i] + got[v]
        return carry

    lax.fori_loop(4, 12, first, 0, unroll=4)
    for v in range(VARS):
        out_ref[:, v] = jnp.swapaxes(gm_ref[v, 4:12], 0, 1)


def halves(x):
    high = x.astype(bf16)
    return high, (x - high.astype(f32)).astype(bf16)


def dot(a, b):
    return lax.dot_general(a, b, (((1,), (0,)), ((), ())), preferred_element_type=f32)


def dot_first(a, b):
    return lax.dot_general(a, b, (((0,), (0,)), ((), ())), preferred_element_type=f32)


def times(left, right, more_left=None, more_right=None):
    n = left[0].shape[0]
    out = []
    for p in range(2):
        at = slice(128 * p, 128 * p + 128)
        rows = [x[:, at] for x in left]
        weights = right[p]
        if more_left is not None:
            rows = [jnp.concatenate([r, x[:, at]], axis=1) for r, x in zip(rows, more_left)]
            weights = jnp.concatenate([weights, more_right[p]], axis=0)
        if n % 16:
            high, low = dot(rows[0], weights), dot(rows[1], weights[:, :128])
        else:
            both = dot(jnp.concatenate(rows, axis=0), weights)
            high, low = both[:n], both[n:, :128]
        out.append(high[:, :128] + (high[:, 128:] + low))
    return jnp.concatenate(out, axis=1)


def in_step(jobs):
    results = [None] * len(jobs)
    left = list(range(len(jobs)))
    while left:
        for n in list(left):
            try:
                next(jobs[n])
            except StopIteration as done:
                results[n] = done.value
                left.remove(n)
    return results


def stack(*parts):
    return tuple(jnp.concatenate(p, axis=0) for p in zip(*parts))


def analysis_kernel(
    got_ref, list_ref, meta_ref, out_ref, x_ref, c_ref, y_ref, d_ref, go_ref, block_ref
):
    width = 4 * MEMBERS
    block_row = lax.broadcasted_iota(jnp.int32, (width, 128), 0) // MEMBERS % 2
    block_col = lax.broadcasted_iota(jnp.int32, (width, 128), 1) // MEMBERS
    block_ref[...] = jnp.where(block_row == block_col, 1.0, 0.0).astype(bf16)

    top_half = lax.broadcasted_iota(jnp.int32, (8, 128), 0) < 4

    for first, dst in ((0, x_ref), (28, c_ref)):

        def turn(v, carry, first=first, dst=dst):
            for h in range(2):
                tall = [got_ref[s, first + v * 4 + 2 * h + k] for k in range(2) for s in range(8)]
                tall = jnp.concatenate(tall, axis=0).T
                for p in range(QUADS // 2):
                    upper, lower = tall[8 * p : 8 * p + 8], tall[64 + 8 * p : 72 + 8 * p]
                    at = slice(128 * h, 128 * h + 128)
                    dst[v, 2 * p, :, at] = jnp.where(top_half, upper, pltpu.roll(lower, 4, 0))
                    dst[v, 2 * p + 1, :, at] = jnp.where(top_half, pltpu.roll(upper, 4, 0), lower)
            return carry

        lax.fori_loop(0, VARS, turn, 0, unroll=3)

    for o in range(4):
        tall = [got_ref[s, 24 + o] for s in range(8)]
        seen = jnp.concatenate(tall + tall, axis=0).T[:WINDOW]
        mean = jnp.sum(seen, axis=1, keepdims=True) * (1.0 / 128.0)
        spread = seen - mean
        at = pl.ds(o, WINDOW, stride=4)
        y_ref[at, :] = spread
        d_ref[at, :] = meta_ref[0, at, :] - mean
    go_ref[...] = jnp.zeros(go_ref.shape, f32)

    def block_of(pair):
        mask = block_ref[:128]
        out = []
        for p in range(2):
            parts = [x[:, 128 * p : 128 * p + 128] for x in pair]
            parts = [jnp.concatenate([x, x], axis=0) * mask for x in parts]
            out.append(jnp.concatenate(parts, axis=1))
        return out

    def block_sum(x):
        parts = halves(x)
        out = []
        for p in range(2):
            wide = jnp.concatenate([x[:, 128 * p : 128 * p + 128] for x in parts], axis=1)
            out.append(dot(wide, block_ref[...]))
        return jnp.concatenate(out, axis=1)

    def row_sum(x):
        return block_sum(jnp.broadcast_to(jnp.sum(x, axis=0, keepdims=True), (8, width)))

    def one_row(x, right):
        return times(halves(x), right)

    lane = lax.broadcasted_iota(jnp.int32, (MEMBERS, width), 1)
    sub = lax.broadcasted_iota(jnp.int32, (MEMBERS, width), 0)
    identity = jnp.where(lane % MEMBERS == sub, 1.0, 0.0)
    entry = lax.broadcasted_iota(jnp.int32, (WINDOW, width), 0)
    patch_row = (lax.broadcasted_iota(jnp.int32, (WINDOW, width), 1) // MEMBERS).astype(f32)
    col_gap = (entry // 4).astype(f32) - 9.5
    col_gap_sq = col_gap * col_gap
    row8 = lax.broadcasted_iota(jnp.int32, (8, width), 0)

    def solve(quad):
        at = pl.ds(pl.multiple_of(16 * quad, 16), WINDOW)
        lists = list_ref[pl.ds(quad, 1), :]
        hits = jnp.where(jnp.broadcast_to(lists, (WINDOW, width)) == entry, 1.0, 0.0).astype(bf16)
        count = [dot(hits[:, 128 * p : 128 * p + 128], block_ref[:128]) for p in range(2)]
        count = jnp.concatenate(count, axis=1)
        yield
        obs_row = jnp.concatenate([meta_ref[1, at, :]] * 2, axis=1)
        error = jnp.concatenate([meta_ref[2, at, :]] * 2, axis=1)
        row_gap = obs_row - 2.0 * patch_row - 0.5
        weight = count * jnp.exp((row_gap * row_gap + col_gap_sq) * (-1.0 / (2.0 * LOC_R * LOC_R))) / error
        y = y_ref[at, :]
        scaled = weight * jnp.concatenate([y, y], axis=1)
        d = d_ref[at, :]
        gain = weight * jnp.concatenate([d, d], axis=1)
        scaled_pair = halves(scaled)
        yh, yl = halves(y[:, :MEMBERS])
        sh, sl = scaled_pair
        gram = dot_first(jnp.concatenate([yh, yl, yh], axis=0), jnp.concatenate([sh, sh, sl], axis=0))
        gram = gram + (MEMBERS - 1.0) * identity
        yield
        inv = lax.rsqrt(row_sum(gram * gram))
        yield
        t0 = gram * inv[:1]
        forcing = jnp.sum(scaled * jnp.concatenate([d, d], axis=1), axis=0, keepdims=True)
        forcing = jnp.broadcast_to(forcing, (8, width))

        m0 = 1.5 * identity - 0.5 * t0
        z1 = halves(m0)
        r0 = block_of(z1)
        t0p = halves(t0)
        u0 = halves(times(t0p, r0))
        yield
        t1f = times(u0, r0)
        yield
        t1 = halves(t1f)
        r1 = block_of(halves(1.5 * identity - 0.5 * t1f))
        both = times(stack(z1, t1), r1)
        yield
        z2, u1 = halves(both[:MEMBERS]), halves(both[MEMBERS:])
        t2f = times(u1, r1)
        yield
        t2 = halves(t2f)
        r2 = block_of(halves(1.5 * identity - 0.5 * t2f))
        both = times(stack(z2, t2), r2)
        yield
        z3, u2 = halves(both[:MEMBERS]), halves(both[MEMBERS:])
        t3f = times(u2, r2)
        yield
        r3 = block_of(halves(1.5 * identity - 0.5 * t3f))
        z4 = block_of(halves(times(z3, r3)))
        yield
        half_way = one_row(forcing, z4)
        yield
        mean_weight = one_row(half_way, z4) * inv
        yield
        state = (t0, t0p, u0, t1, u1, t2, u2, z1, z2, z3, r0, r1, r2, r3)
        return at, inv, z4, forcing, half_way, mean_weight, scaled, scaled_pair, gain, state

    def pull_root(e, state):
        t0, t0p, u0, t1, u1, t2, u2, z1, z2, z3, r0, r1, r2, r3 = state
        dt0 = halves(e)
        dm = halves(-0.5 * e)
        s0 = block_of(dm)
        du0 = halves(times(dt0, r0, t0p, s0))
        yield
        dt1f = times(du0, r0, u0, s0)
        yield
        dt1 = halves(dt1f)
        s1 = block_of(halves(-0.5 * dt1f))
        both = times(stack(dm, dt1), r1, stack(z1, t1), s1)
        yield
        dz2, du1 = halves(both[:MEMBERS]), halves(both[MEMBERS:])
        dt2f = times(du1, r1, u1, s1)
        yield
        dt2 = halves(dt2f)
        s2 = block_of(halves(-0.5 * dt2f))
        both = times(stack(dz2, dt2), r2, stack(z2, t2), s2)
        yield
        dz3, du2 = halves(both[:MEMBERS]), halves(both[MEMBERS:])
        dt3f = times(du2, r2, u2, s2)
        yield
        s3 = block_of(halves(-0.5 * dt3f))
        got = times(dz3, r3, z3, s3)
        yield
        return got

    def fold(x):
        x = x[:, :128] + x[:, 128:]
        return x + pltpu.roll(x, 64, 1)

    def one_quad(quad):
        x = jnp.concatenate([x_ref[v, quad] for v in range(VARS)], axis=0)
        c = jnp.concatenate([c_ref[v, quad] for v in range(VARS)], axis=0)
        both = block_sum(jnp.concatenate([x, c], axis=0))
        centre = both[:CELLS] * (1.0 / MEMBERS)
        c_sum = both[CELLS:]
        a = x - centre
        yield
        at, inv, z4, forcing, half_way, mean_weight, scaled, scaled_pair, gain, state = yield from solve(quad)
        alpha = math.sqrt(MEMBERS - 1.0) * jnp.sqrt(inv[:1])
        both = times(halves(jnp.concatenate([a, c], axis=0)), z4)
        yield
        moved = alpha * both[:CELLS]
        update = centre + moved + block_sum(a * mean_weight[:1])
        for v in range(VARS):
            x_ref[v, quad] = update[8 * v : 8 * v + 8]
        yield
        pull = alpha * both[CELLS:] + c_sum * mean_weight[:1]
        pull = pull + (c_sum - block_sum(pull)) * (1.0 / MEMBERS)
        for v in range(VARS):
            c_ref[v, quad] = pull[8 * v : 8 * v + 8]
        yield
        g_mean = jnp.broadcast_to(jnp.sum(a * c_sum, axis=0, keepdims=True), (8, width))
        g_half = one_row(g_mean, z4) * inv
        yield
        g_forcing = one_row(g_half, z4)
        yield
        left = jnp.where(row8 == 0, g_mean * inv, jnp.where(row8 == 1, g_half, 0.0))
        right = jnp.where(row8 == 0, half_way, jnp.where(row8 == 1, forcing, 0.0))
        scaled_a = a * alpha
        lhs = halves(jnp.concatenate([scaled_a, c, left, right], axis=0))
        rhs = halves(jnp.concatenate([c, scaled_a, right, left], axis=0))
        e = []
        for p in range(2):
            part = slice(128 * p, 128 * p + 128)
            tall = jnp.concatenate([x[:, part] for x in lhs], axis=1)
            wide = jnp.concatenate([x[:, part] for x in rhs], axis=1)
            full = dot_first(tall, wide)
            full = full[:128, :128] + (full[:128, 128:] + full[128:, :128])
            e.append(jnp.where(lane[:, :128] < MEMBERS, full[:64], full[64:]))
        e = jnp.concatenate(e, axis=1) * 0.5
        yield
        g_root = yield from pull_root(e, state)
        t0 = state[0]
        loss = jnp.sum(c * moved, axis=0, keepdims=True) * 0.5
        loss = loss + g_mean[:1] * mean_weight[:1] + jnp.sum(g_root * t0, axis=0, keepdims=True)
        loss = block_sum(jnp.broadcast_to(loss, (8, width)))
        yield
        g_gram = (g_root - loss[:1] * t0) * inv[:1]
        g_y = 2.0 * times(scaled_pair, block_of(halves(g_gram))) + gain * g_forcing[:1]
        yield
        g_d = scaled * g_forcing[:1]
        low = lax.broadcasted_iota(jnp.int32, (WINDOW, 128), 1) < 64
        go_ref[at, :] += jnp.where(low, fold(g_y), fold(g_d))

    def group(g, carry):
        in_step([one_quad(TOGETHER * g + k) for k in range(TOGETHER)])
        return carry

    lax.fori_loop(0, QUADS // TOGETHER, group, 0)

    for src, first in ((x_ref, 28), (c_ref, 0)):

        def turn_back(v, carry, src=src, first=first):
            for h in range(2):
                upper, lower = [], []
                for p in range(QUADS // 2):
                    a, b = (src[v, 2 * p + k, :, 128 * h : 128 * h + 128] for k in range(2))
                    upper.append(jnp.where(top_half, a, pltpu.roll(b, 4, 0)))
                    lower.append(jnp.where(top_half, pltpu.roll(a, 4, 0), b))
                tall = jnp.concatenate(upper + lower, axis=0).T
                for k in range(2):
                    for s in range(8):
                        at = 64 * k + 8 * s
                        out_ref[s, first + v * 4 + 2 * h + k] = tall[at : at + 8]
            return carry

        lax.fori_loop(0, VARS, turn_back, 0, unroll=3)

    for o in range(4):
        got = go_ref[pl.ds(o, WINDOW, stride=4), :]
        got = got - jnp.sum(got, axis=1, keepdims=True) * (1.0 / MEMBERS)
        tall = jnp.concatenate([got, jnp.zeros((128 - WINDOW, 128), f32)], axis=0).T
        for s in range(8):
            out_ref[s, 24 + o] = tall[8 * s : 8 * s + 8]


def ring(value, up):
    count = lax.axis_size("space")
    if up:
        pairs = [((i + 1) % count, i) for i in range(count)]
    else:
        pairs = [(i, (i + 1) % count) for i in range(count)]
    return lax.ppermute(value, "space", pairs)


def swap(value):
    return lax.all_to_all(value, "member", split_axis=0, concat_axis=0, tiled=True)


def plane_scratch(rows):
    return pltpu.VMEM((VARS, rows, PER_DEV, COLS), f32)


def shards(initial_ensemble, obs_value, obs_error, obs_location, patch_obs, cotangent):
    shape = initial_ensemble.shape
    edge = (VARS * HALO, PER_DEV, COLS)
    half = (VARS * 4, PER_DEV, COLS)
    size = 4 * PER_DEV * STRIDE * COLS

    state = initial_ensemble
    first, last = call(edge_kernel, [edge, edge], [], 1000, 2 * size, state)
    bot = ring(first, True)
    top = ring(last, False)

    position = lax.axis_index("member") * (NOBS // 8)
    plane = obs_location[0] // COLS
    chosen = plane.reshape(COLS, 4).T
    meta = jnp.stack([obs_value[0], (plane % ROWS).astype(f32), obs_error[0]])
    meta = jnp.concatenate([meta[:, -32:], meta, meta[:, :32]], axis=1)
    meta = lax.dynamic_slice_in_dim(meta, position, LOCAL_OBS, axis=1)
    meta = jnp.broadcast_to(meta[:, :, None], (3, LOCAL_OBS, 128))
    lists = (patch_obs[0] - position + 32) % NOBS
    lists = lists.reshape(QUADS, 256) - 16 * jnp.arange(QUADS, dtype=jnp.int32)[:, None]
    chosen, meta, lists, cotangent = lax.optimization_barrier((chosen, meta, lists, cotangent))
    (cot_sent,) = call(cot_kernel, [(8, 24, PER_DEV, 128)], [], 1000, 2 * size, cotangent)

    sent, mid = call(
        forward_kernel,
        [(8, 52, PER_DEV, 128), (VARS, 16, PER_DEV, COLS)],
        [plane_scratch(ROWS + 2 * HALO), plane_scratch(ROWS)],
        10**7, 6 * size, state, top, bot, chosen, cot_sent,
    )
    owned = swap(sent)

    cells = pltpu.VMEM((VARS, QUADS, 8, 256), f32)
    (returned,) = call(
        analysis_kernel,
        [(8, 52, PER_DEV, 128)],
        [
            cells, cells, pltpu.VMEM((LOCAL_OBS, 128), f32), pltpu.VMEM((LOCAL_OBS, 128), f32),
            pltpu.VMEM((LOCAL_OBS, 128), f32), pltpu.VMEM((256, 128), bf16),
        ],
        10**10, 5 * size, owned, lists, meta,
    )
    got = swap(returned)

    g, g_first, g_last = call(
        collect_kernel, [(STRIDE, PER_DEV, COLS), half, half], [], 10**6, 3 * size, got, chosen
    )
    g_bot = ring(g_first, True)
    g_top = ring(g_last, False)
    (analysis,) = call(place_kernel, [shape], [], 1000, 2 * size, got)
    (gradient,) = call(
        backward_kernel,
        [shape],
        [plane_scratch(ROWS + 2 * HALO)] + [plane_scratch(16)] * 3,
        10**7, 6 * size, state, top, bot, mid, g, g_top, g_bot,
    )
    return analysis, gradient


def solution(mesh):
    placed = (
        P("member", None, "space", None),
        P("space", None),
        P("space", None),
        P("space", None),
        P("space", "member", None),
        P("member", None, "space", None),
    )
    return jax.shard_map(
        shards,
        mesh=mesh,
        in_specs=placed,
        out_specs=(P("member", None, "space", None), P("member", None, "space", None)),
        check_vma=False,
    )
```

```python
import functools
import math

import jax
import jax.numpy as jnp
from jax import lax
from jax.experimental import pallas as pl
from jax.experimental.pallas import tpu as pltpu
from jax.sharding import PartitionSpec as P

VARS = 6
ROWS = 8
COLS = 512
MEMBERS = 64
PER_DEV = 8
STRIDE = VARS * ROWS
NOBS = 2048
WINDOW = 80
LOCAL_OBS = 320
QUADS = 16
HALO = 4
TOGETHER = 8
CELLS = 48
LOC_R = 8

time_step = 0.2
HALF_STEP = 0.1
f32 = jnp.float32
bf16 = jnp.bfloat16
VMEM_LIMIT = 32 * 1024 * 1024


def call(kernel, outs, scratch, flops, moved, *args):
    spec = pl.BlockSpec(memory_space=pltpu.VMEM)
    return pl.pallas_call(
        kernel,
        out_shape=[jax.ShapeDtypeStruct(s, f32) for s in outs],
        in_specs=[spec] * len(args),
        out_specs=[spec] * len(outs),
        scratch_shapes=scratch,
        compiler_params=pltpu.CompilerParams(vmem_limit_bytes=VMEM_LIMIT),
        cost_estimate=pl.CostEstimate(flops=flops, bytes_accessed=moved, transcendentals=0),
    )(*args)


def lane_shift(q, by):
    return pltpu.roll(q, by % COLS, 1)


def col_diff(q):
    near = lane_shift(q, -1) - lane_shift(q, 1)
    far = lane_shift(q, -2) - lane_shift(q, 2)
    return near * (8.0 / 12.0) - far * (1.0 / 12.0)


def row_diff(ref, v, i):
    near = ref[v, i + 1] - ref[v, i - 1]
    far = ref[v, i + 2] - ref[v, i - 2]
    return near * (8.0 / 12.0) - far * (1.0 / 12.0)


def tendency(ref, i):
    rates = [None] * VARS
    for l in range(2):
        u, v, b = ref[l, i], ref[2 + l, i], ref[4 + l, i]
        ru, rv, rb = (row_diff(ref, k + l, i) for k in (0, 2, 4))
        cu, cv, cb = col_diff(u), col_diff(v), col_diff(b)
        rates[l] = 0.5 * v - (u * ru + v * cu) - rb + 0.3 * (ref[1 - l, i] - u)
        rates[2 + l] = -0.5 * u - (u * rv + v * cv) - cb + 0.3 * (ref[3 - l, i] - v)
        rates[4 + l] = -(u * rb + v * cb) - (ru + cv) + 0.3 * (ref[5 - l, i] - b)
    return rates


def planes_of(x_ref, v):
    return jnp.swapaxes(x_ref[:, v], 0, 1)


def edge_kernel(x_ref, first_ref, last_ref):
    for v in range(VARS):
        planes = planes_of(x_ref, v)
        first_ref[HALO * v : HALO * v + HALO] = planes[:HALO]
        last_ref[HALO * v : HALO * v + HALO] = planes[ROWS - HALO :]


def pack_planes(even, odd, store):
    low = lax.broadcasted_iota(jnp.int32, (PER_DEV, 128), 1) < 64
    for t in range(4):
        a, b = even[:, 128 * t : 128 * t + 128], odd[:, 128 * t : 128 * t + 128]
        store(2 * t, jnp.where(low, a, pltpu.roll(b, 64, 1)))
        store(2 * t + 1, jnp.where(low, pltpu.roll(a, 64, 1), b))


def unpack_planes(load):
    low = lax.broadcasted_iota(jnp.int32, (PER_DEV, 128), 1) < 64
    even, odd = [], []
    for t in range(4):
        a, b = load(2 * t), load(2 * t + 1)
        even.append(jnp.where(low, a, pltpu.roll(b, 64, 1)))
        odd.append(jnp.where(low, pltpu.roll(a, 64, 1), b))
    return jnp.concatenate(even, axis=1), jnp.concatenate(odd, axis=1)


def cot_kernel(x_ref, out_ref):
    for v in range(VARS):
        planes = planes_of(x_ref, v)
        for r in range(4):

            def store(d, value, t=v * 4 + r):
                out_ref[d, t] = value

            pack_planes(planes[2 * r], planes[2 * r + 1], store)


def load_state(s_ref, x_ref, top_ref, bot_ref):
    for v in range(VARS):
        s_ref[v, HALO : HALO + ROWS] = planes_of(x_ref, v)
        for r in range(HALO):
            s_ref[v, r] = top_ref[v * HALO + r]
            s_ref[v, HALO + ROWS + r] = bot_ref[v * HALO + r]


def forward_kernel(x_ref, top_ref, bot_ref, sel_ref, cot_ref, out_ref, mid_ref, s_ref, fore_ref):
    for d in range(8):
        out_ref[d, 28:] = cot_ref[d]
    load_state(s_ref, x_ref, top_ref, bot_ref)

    def middle(i, carry):
        rates = tendency(s_ref, i + 2)
        for v in range(VARS):
            mid_ref[v, i] = s_ref[v, i + 2] + time_step * rates[v]
        return carry

    lax.fori_loop(0, 12, middle, 0, unroll=4)

    def finish(i, carry):
        rates = tendency(mid_ref, i + 2)
        for v in range(VARS):
            fore_ref[v, i] = 0.5 * (s_ref[v, i + HALO] + mid_ref[v, i + 2]) + 0.5 * time_step * rates[v]
        return carry

    lax.fori_loop(0, ROWS, finish, 0, unroll=4)

    def pack(v, carry):
        for r in range(4):

            def store(d, value, r=r):
                out_ref[d, v * 4 + r] = value

            pack_planes(fore_ref[v, 2 * r], fore_ref[v, 2 * r + 1], store)
        return carry

    lax.fori_loop(0, VARS, pack, 0, unroll=2)

    for o in range(4):
        chosen = jnp.broadcast_to(sel_ref[o : o + 1, :], (PER_DEV, COLS))

        def pick(v, acc, chosen=chosen):
            for r in range(ROWS):
                acc = jnp.where(chosen == v * ROWS + r, fore_ref[v, r], acc)
            return acc

        seen = lax.fori_loop(0, VARS, pick, jnp.zeros((PER_DEV, COLS), f32), unroll=2)
        for d in range(8):
            out_ref[d, 24 + o] = lane_shift(seen, 8 - 64 * d)[:, :128]


def place_kernel(got_ref, out_ref):
    for v in range(VARS):
        planes = []
        for r in range(4):
            planes.extend(unpack_planes(lambda d: got_ref[d, 28 + v * 4 + r]))
        out_ref[:, v] = jnp.swapaxes(jnp.stack(planes), 0, 1)


def pull_products(s_ref, s_at, g_ref, prod_ref, prod_at, count):
    def body(i, carry):
        for l in range(2):
            u = s_ref[l, i + s_at]
            gu, gv, gb = g_ref[l, i], g_ref[2 + l, i], g_ref[4 + l, i]
            prod_ref[l, i + prod_at] = u * gu + gb
            prod_ref[2 + l, i + prod_at] = u * gv
            prod_ref[4 + l, i + prod_at] = u * gb + gu
        return carry

    lax.fori_loop(0, count, body, 0, unroll=2)


def pull_row(s_ref, s_at, g_ref, g_at, prod_ref, prod_at):
    out = [None] * VARS
    for l in range(2):
        u, v, b = (s_ref[k + l, s_at] for k in (0, 2, 4))
        gu, gv, gb = (g_ref[k + l, g_at] for k in (0, 2, 4))
        ru, rv, rb = (row_diff(s_ref, k + l, s_at) for k in (0, 2, 4))
        cu, cv, cb = col_diff(u), col_diff(v), col_diff(b)
        pu, pv, pb = (row_diff(prod_ref, k + l, prod_at) for k in (0, 2, 4))
        out[l] = (
            pu + col_diff(v * gu)
            - (gu * ru + gv * rv + gb * rb) - 0.5 * gv + 0.3 * (g_ref[1 - l, g_at] - gu)
        )
        out[2 + l] = (
            pv + col_diff(v * gv + gb)
            - (gu * cu + gv * cv + gb * cb) + 0.5 * gu + 0.3 * (g_ref[3 - l, g_at] - gv)
        )
        out[4 + l] = pb + col_diff(v * gb + gv) + 0.3 * (g_ref[5 - l, g_at] - gb)
    return out


def collect_kernel(got_ref, sel_ref, mid_ref, g_ref, prod_ref, edge_ref, first_ref, last_ref):
    lane = lax.broadcasted_iota(jnp.int32, (PER_DEV, 128), 1)
    sums, chosen = [], []
    for o in range(4):
        total = jnp.zeros((PER_DEV, COLS), f32)
        for d in range(8):
            piece = jnp.where(lane < WINDOW, got_ref[d, 24 + o], 0.0)
            wide = jnp.concatenate([piece, jnp.zeros((PER_DEV, COLS - 128), f32)], axis=1)
            total = total + lane_shift(wide, 64 * d - 8)
        sums.append(total)
        chosen.append(jnp.broadcast_to(sel_ref[o : o + 1, :], (PER_DEV, COLS)))

    for v in range(VARS):
        for r in range(4):
            pair = unpack_planes(lambda d: got_ref[d, v * 4 + r])
            for k in range(2):
                row = 2 * r + k
                value = pair[k]
                for o in range(4):
                    value = value + jnp.where(chosen[o] == v * ROWS + row, sums[o], 0.0)
                g_ref[v, row] = value

    for v in range(VARS):
        for r in (0, 1, 10, 11):
            prod_ref[v, r] = jnp.zeros((PER_DEV, COLS), f32)
    pull_products(mid_ref, 2, g_ref, prod_ref, 2, ROWS)
    for n, r in enumerate((0, 1, 6, 7)):
        got = pull_row(mid_ref, r + 2, g_ref, r, prod_ref, r + 2)
        to_ref = first_ref if r < 2 else last_ref
        for v in range(VARS):
            pulled = HALF_STEP * got[v]
            edge_ref[v, n] = pulled
            to_ref[2 * v + n % 2] = HALF_STEP * g_ref[v, r] + time_step * pulled
            to_ref[12 + 2 * v + n % 2] = prod_ref[v, r + 2]


def inner_kernel(mid_ref, g_ref, prod_ref, out_ref):
    for r in range(2, 6):
        got = pull_row(mid_ref, r + 2, g_ref, r, prod_ref, r + 2)
        for v in range(VARS):
            out_ref[v, r - 2] = HALF_STEP * got[v]


def backward_kernel(
    x_ref, top_ref, bot_ref, g_ref, prod_ref, edge_ref, inner_ref, from_top_ref, from_bot_ref,
    out_ref, s_ref, h_ref, prod2_ref, total_ref,
):
    load_state(s_ref, x_ref, top_ref, bot_ref)
    near, far = 8.0 / 12.0, 1.0 / 12.0
    for v in range(VARS):
        p = [prod_ref[v, 2 + r] for r in (0, 1, 6, 7)]
        t = [from_top_ref[12 + 2 * v + k] for k in range(2)]
        b = [from_bot_ref[12 + 2 * v + k] for k in range(2)]
        step = time_step * HALF_STEP
        h_ref[v, 0] = from_top_ref[2 * v] - (step * far) * p[0]
        h_ref[v, 1] = from_top_ref[2 * v + 1] + step * (near * p[0] - far * p[1])
        h_ref[v, 10] = from_bot_ref[2 * v] + step * (far * p[2] - near * p[3])
        h_ref[v, 11] = from_bot_ref[2 * v + 1] + (step * far) * p[3]
        pulled = [
            edge_ref[v, 0] + HALF_STEP * (far * t[0] - near * t[1]),
            edge_ref[v, 1] + (HALF_STEP * far) * t[1],
            *(inner_ref[v, k] for k in range(4)),
            edge_ref[v, 2] - (HALF_STEP * far) * b[0],
            edge_ref[v, 3] + HALF_STEP * (near * b[0] - far * b[1]),
        ]
        for r in range(ROWS):
            g = g_ref[v, r]
            h_ref[v, 2 + r] = HALF_STEP * g + time_step * pulled[r]
            total_ref[v, r] = g + pulled[r]

    pull_products(s_ref, HALO - 2, h_ref, prod2_ref, 0, ROWS + 4)

    def first(i, carry):
        got = pull_row(s_ref, i + HALO, h_ref, i + 2, prod2_ref, i + 2)
        for v in range(VARS):
            total_ref[v, i] = total_ref[v, i] + got[v]
        return carry

    lax.fori_loop(0, ROWS, first, 0, unroll=4)
    for v in range(VARS):
        out_ref[:, v] = jnp.swapaxes(total_ref[v], 0, 1)


def halves(x):
    high = x.astype(bf16)
    return high, (x - high.astype(f32)).astype(bf16)


def dot(a, b):
    return lax.dot_general(a, b, (((1,), (0,)), ((), ())), preferred_element_type=f32)


def dot_first(a, b):
    return lax.dot_general(a, b, (((0,), (0,)), ((), ())), preferred_element_type=f32)


def times(left, right, more_left=None, more_right=None):
    n = left[0].shape[0]
    out = []
    for p in range(2):
        at = slice(128 * p, 128 * p + 128)
        rows = [x[:, at] for x in left]
        weights = right[p]
        if more_left is not None:
            rows = [jnp.concatenate([r, x[:, at]], axis=1) for r, x in zip(rows, more_left)]
            weights = jnp.concatenate([weights, more_right[p]], axis=0)
        if n % 16:
            high, low = dot(rows[0], weights), dot(rows[1], weights[:, :128])
        else:
            both = dot(jnp.concatenate(rows, axis=0), weights)
            high, low = both[:n], both[n:, :128]
        out.append(high[:, :128] + (high[:, 128:] + low))
    return jnp.concatenate(out, axis=1)


def in_step(jobs):
    results = [None] * len(jobs)
    left = list(range(len(jobs)))
    while left:
        for n in list(left):
            try:
                next(jobs[n])
            except StopIteration as done:
                results[n] = done.value
                left.remove(n)
    return results


def stack(*parts):
    return tuple(jnp.concatenate(p, axis=0) for p in zip(*parts))


def analysis_kernel(
    got_ref, list_ref, meta_ref, out_ref, x_ref, c_ref, y_ref, d_ref, go_ref, block_ref
):
    width = 4 * MEMBERS
    block_row = lax.broadcasted_iota(jnp.int32, (width, 128), 0) // MEMBERS % 2
    block_col = lax.broadcasted_iota(jnp.int32, (width, 128), 1) // MEMBERS
    block_ref[...] = jnp.where(block_row == block_col, 1.0, 0.0).astype(bf16)

    top_half = lax.broadcasted_iota(jnp.int32, (8, 128), 0) < 4

    for first, dst in ((0, x_ref), (28, c_ref)):

        def turn(v, carry, first=first, dst=dst):
            for h in range(2):
                tall = [got_ref[s, first + v * 4 + 2 * h + k] for k in range(2) for s in range(8)]
                tall = jnp.concatenate(tall, axis=0).T
                for p in range(QUADS // 2):
                    upper, lower = tall[8 * p : 8 * p + 8], tall[64 + 8 * p : 72 + 8 * p]
                    at = slice(128 * h, 128 * h + 128)
                    dst[v, 2 * p, :, at] = jnp.where(top_half, upper, pltpu.roll(lower, 4, 0))
                    dst[v, 2 * p + 1, :, at] = jnp.where(top_half, pltpu.roll(upper, 4, 0), lower)
            return carry

        lax.fori_loop(0, VARS, turn, 0, unroll=3)

    for o in range(4):
        tall = [got_ref[s, 24 + o] for s in range(8)]
        seen = jnp.concatenate(tall + tall, axis=0).T[:WINDOW]
        mean = jnp.sum(seen, axis=1, keepdims=True) * (1.0 / 128.0)
        spread = seen - mean
        at = pl.ds(o, WINDOW, stride=4)
        y_ref[at, :] = spread
        d_ref[at, :] = meta_ref[0, at, :] - mean
    go_ref[...] = jnp.zeros(go_ref.shape, f32)

    def block_of(pair):
        mask = block_ref[:128]
        out = []
        for p in range(2):
            parts = [x[:, 128 * p : 128 * p + 128] for x in pair]
            parts = [jnp.concatenate([x, x], axis=0) * mask for x in parts]
            out.append(jnp.concatenate(parts, axis=1))
        return out

    def block_sum(x):
        parts = halves(x)
        out = []
        for p in range(2):
            wide = jnp.concatenate([x[:, 128 * p : 128 * p + 128] for x in parts], axis=1)
            out.append(dot(wide, block_ref[...]))
        return jnp.concatenate(out, axis=1)

    def row_sum(x):
        return block_sum(jnp.broadcast_to(jnp.sum(x, axis=0, keepdims=True), (8, width)))

    def one_row(x, right):
        return times(halves(x), right)

    lane = lax.broadcasted_iota(jnp.int32, (MEMBERS, width), 1)
    sub = lax.broadcasted_iota(jnp.int32, (MEMBERS, width), 0)
    identity = jnp.where(lane % MEMBERS == sub, 1.0, 0.0)
    entry = lax.broadcasted_iota(jnp.int32, (WINDOW, width), 0)
    patch_row = (lax.broadcasted_iota(jnp.int32, (WINDOW, width), 1) // MEMBERS).astype(f32)
    col_gap = (entry // 4).astype(f32) - 9.5
    col_gap_sq = col_gap * col_gap
    row8 = lax.broadcasted_iota(jnp.int32, (8, width), 0)

    def solve(quad):
        at = pl.ds(pl.multiple_of(16 * quad, 16), WINDOW)
        lists = list_ref[pl.ds(quad, 1), :]
        hits = jnp.where(jnp.broadcast_to(lists, (WINDOW, width)) == entry, 1.0, 0.0).astype(bf16)
        count = [dot(hits[:, 128 * p : 128 * p + 128], block_ref[:128]) for p in range(2)]
        count = jnp.concatenate(count, axis=1)
        yield
        obs_row = jnp.concatenate([meta_ref[1, at, :]] * 2, axis=1)
        error = jnp.concatenate([meta_ref[2, at, :]] * 2, axis=1)
        row_gap = obs_row - 2.0 * patch_row - 0.5
        weight = count * jnp.exp((row_gap * row_gap + col_gap_sq) * (-1.0 / (2.0 * LOC_R * LOC_R))) / error
        y = y_ref[at, :]
        scaled = weight * jnp.concatenate([y, y], axis=1)
        d = d_ref[at, :]
        gain = weight * jnp.concatenate([d, d], axis=1)
        scaled_pair = halves(scaled)
        yh, yl = halves(y[:, :MEMBERS])
        sh, sl = scaled_pair
        gram = dot_first(jnp.concatenate([yh, yl, yh], axis=0), jnp.concatenate([sh, sh, sl], axis=0))
        gram = gram + (MEMBERS - 1.0) * identity
        yield
        inv = lax.rsqrt(row_sum(gram * gram))
        yield
        t0 = gram * inv[:1]
        forcing = jnp.sum(scaled * jnp.concatenate([d, d], axis=1), axis=0, keepdims=True)
        forcing = jnp.broadcast_to(forcing, (8, width))

        m0 = 1.5 * identity - 0.5 * t0
        z1 = halves(m0)
        r0 = block_of(z1)
        t0p = halves(t0)
        u0 = halves(times(t0p, r0))
        yield
        t1f = times(u0, r0)
        yield
        t1 = halves(t1f)
        r1 = block_of(halves(1.5 * identity - 0.5 * t1f))
        both = times(stack(z1, t1), r1)
        yield
        z2, u1 = halves(both[:MEMBERS]), halves(both[MEMBERS:])
        t2f = times(u1, r1)
        yield
        t2 = halves(t2f)
        r2 = block_of(halves(1.5 * identity - 0.5 * t2f))
        both = times(stack(z2, t2), r2)
        yield
        z3, u2 = halves(both[:MEMBERS]), halves(both[MEMBERS:])
        t3f = times(u2, r2)
        yield
        r3 = block_of(halves(1.5 * identity - 0.5 * t3f))
        z4 = block_of(halves(times(z3, r3)))
        yield
        half_way = one_row(forcing, z4)
        yield
        mean_weight = one_row(half_way, z4) * inv
        yield
        state = (t0, t0p, u0, t1, u1, t2, u2, z1, z2, z3, r0, r1, r2, r3)
        return at, inv, z4, forcing, half_way, mean_weight, scaled, scaled_pair, gain, state

    def pull_root(e, state):
        t0, t0p, u0, t1, u1, t2, u2, z1, z2, z3, r0, r1, r2, r3 = state
        dt0 = halves(e)
        dm = halves(-0.5 * e)
        s0 = block_of(dm)
        du0 = halves(times(dt0, r0, t0p, s0))
        yield
        dt1f = times(du0, r0, u0, s0)
        yield
        dt1 = halves(dt1f)
        s1 = block_of(halves(-0.5 * dt1f))
        both = times(stack(dm, dt1), r1, stack(z1, t1), s1)
        yield
        dz2, du1 = halves(both[:MEMBERS]), halves(both[MEMBERS:])
        dt2f = times(du1, r1, u1, s1)
        yield
        dt2 = halves(dt2f)
        s2 = block_of(halves(-0.5 * dt2f))
        both = times(stack(dz2, dt2), r2, stack(z2, t2), s2)
        yield
        dz3, du2 = halves(both[:MEMBERS]), halves(both[MEMBERS:])
        dt3f = times(du2, r2, u2, s2)
        yield
        s3 = block_of(halves(-0.5 * dt3f))
        got = times(dz3, r3, z3, s3)
        yield
        return got

    def fold(x):
        x = x[:, :128] + x[:, 128:]
        return x + pltpu.roll(x, 64, 1)

    def one_quad(quad):
        x = jnp.concatenate([x_ref[v, quad] for v in range(VARS)], axis=0)
        c = jnp.concatenate([c_ref[v, quad] for v in range(VARS)], axis=0)
        both = block_sum(jnp.concatenate([x, c], axis=0))
        centre = both[:CELLS] * (1.0 / MEMBERS)
        c_sum = both[CELLS:]
        a = x - centre
        yield
        at, inv, z4, forcing, half_way, mean_weight, scaled, scaled_pair, gain, state = yield from solve(quad)
        alpha = math.sqrt(MEMBERS - 1.0) * jnp.sqrt(inv[:1])
        both = times(halves(jnp.concatenate([a, c], axis=0)), z4)
        yield
        moved = alpha * both[:CELLS]
        update = centre + moved + block_sum(a * mean_weight[:1])
        for v in range(VARS):
            x_ref[v, quad] = update[8 * v : 8 * v + 8]
        yield
        pull = alpha * both[CELLS:] + c_sum * mean_weight[:1]
        pull = pull + (c_sum - block_sum(pull)) * (1.0 / MEMBERS)
        for v in range(VARS):
            c_ref[v, quad] = pull[8 * v : 8 * v + 8]
        yield
        g_mean = jnp.broadcast_to(jnp.sum(a * c_sum, axis=0, keepdims=True), (8, width))
        g_half = one_row(g_mean, z4) * inv
        yield
        g_forcing = one_row(g_half, z4)
        yield
        left = jnp.where(row8 == 0, g_mean * inv, jnp.where(row8 == 1, g_half, 0.0))
        right = jnp.where(row8 == 0, half_way, jnp.where(row8 == 1, forcing, 0.0))
        scaled_a = a * alpha
        lhs = halves(jnp.concatenate([scaled_a, c, left, right], axis=0))
        rhs = halves(jnp.concatenate([c, scaled_a, right, left], axis=0))
        e = []
        for p in range(2):
            part = slice(128 * p, 128 * p + 128)
            tall = jnp.concatenate([x[:, part] for x in lhs], axis=1)
            wide = jnp.concatenate([x[:, part] for x in rhs], axis=1)
            full = dot_first(tall, wide)
            full = full[:128, :128] + (full[:128, 128:] + full[128:, :128])
            e.append(jnp.where(lane[:, :128] < MEMBERS, full[:64], full[64:]))
        e = jnp.concatenate(e, axis=1) * 0.5
        yield
        g_root = yield from pull_root(e, state)
        t0 = state[0]
        loss = jnp.sum(c * moved, axis=0, keepdims=True) * 0.5
        loss = loss + g_mean[:1] * mean_weight[:1] + jnp.sum(g_root * t0, axis=0, keepdims=True)
        loss = block_sum(jnp.broadcast_to(loss, (8, width)))
        yield
        g_gram = (g_root - loss[:1] * t0) * inv[:1]
        g_y = 2.0 * times(scaled_pair, block_of(halves(g_gram))) + gain * g_forcing[:1]
        yield
        g_d = scaled * g_forcing[:1]
        low = lax.broadcasted_iota(jnp.int32, (WINDOW, 128), 1) < 64
        go_ref[at, :] += jnp.where(low, fold(g_y), fold(g_d))

    def group(g, carry):
        in_step([one_quad(TOGETHER * g + k) for k in range(TOGETHER)])
        return carry

    lax.fori_loop(0, QUADS // TOGETHER, group, 0)

    for src, first in ((x_ref, 28), (c_ref, 0)):

        def turn_back(v, carry, src=src, first=first):
            for h in range(2):
                upper, lower = [], []
                for p in range(QUADS // 2):
                    a, b = (src[v, 2 * p + k, :, 128 * h : 128 * h + 128] for k in range(2))
                    upper.append(jnp.where(top_half, a, pltpu.roll(b, 4, 0)))
                    lower.append(jnp.where(top_half, pltpu.roll(a, 4, 0), b))
                tall = jnp.concatenate(upper + lower, axis=0).T
                for k in range(2):
                    for s in range(8):
                        at = 64 * k + 8 * s
                        out_ref[s, first + v * 4 + 2 * h + k] = tall[at : at + 8]
            return carry

        lax.fori_loop(0, VARS, turn_back, 0, unroll=3)

    for o in range(4):
        got = go_ref[pl.ds(o, WINDOW, stride=4), :]
        got = got - jnp.sum(got, axis=1, keepdims=True) * (1.0 / MEMBERS)
        tall = jnp.concatenate([got, jnp.zeros((128 - WINDOW, 128), f32)], axis=0).T
        for s in range(8):
            out_ref[s, 24 + o] = tall[8 * s : 8 * s + 8]


def ring(value, up):
    count = lax.axis_size("space")
    if up:
        pairs = [((i + 1) % count, i) for i in range(count)]
    else:
        pairs = [(i, (i + 1) % count) for i in range(count)]
    return lax.ppermute(value, "space", pairs)


def swap(value):
    return lax.all_to_all(value, "member", split_axis=0, concat_axis=0, tiled=True)


def plane_scratch(rows):
    return pltpu.VMEM((VARS, rows, PER_DEV, COLS), f32)


def shards(initial_ensemble, obs_value, obs_error, obs_location, patch_obs, cotangent):
    shape = initial_ensemble.shape
    edge = (VARS * HALO, PER_DEV, COLS)
    half = (VARS * 4, PER_DEV, COLS)
    size = 4 * PER_DEV * STRIDE * COLS

    state = initial_ensemble
    first, last = call(edge_kernel, [edge, edge], [], 1000, 2 * size, state)
    bot = ring(first, True)
    top = ring(last, False)

    position = lax.axis_index("member") * (NOBS // 8)
    plane = obs_location[0] // COLS
    chosen = plane.reshape(COLS, 4).T
    meta = jnp.stack([obs_value[0], (plane % ROWS).astype(f32), obs_error[0]])
    meta = jnp.concatenate([meta[:, -32:], meta, meta[:, :32]], axis=1)
    meta = lax.dynamic_slice_in_dim(meta, position, LOCAL_OBS, axis=1)
    meta = jnp.broadcast_to(meta[:, :, None], (3, LOCAL_OBS, 128))
    lists = (patch_obs[0] - position + 32) % NOBS
    lists = lists.reshape(QUADS, 256) - 16 * jnp.arange(QUADS, dtype=jnp.int32)[:, None]
    chosen, meta, lists, cotangent = lax.optimization_barrier((chosen, meta, lists, cotangent))
    (cot_sent,) = call(cot_kernel, [(8, 24, PER_DEV, 128)], [], 1000, 2 * size, cotangent)

    sent, mid = call(
        forward_kernel,
        [(8, 52, PER_DEV, 128), (VARS, 12, PER_DEV, COLS)],
        [plane_scratch(ROWS + 2 * HALO), plane_scratch(ROWS)],
        10**7, 6 * size, state, top, bot, chosen, cot_sent,
    )
    owned = swap(sent)

    cells = pltpu.VMEM((VARS, QUADS, 8, 256), f32)
    (returned,) = call(
        analysis_kernel,
        [(8, 52, PER_DEV, 128)],
        [
            cells, cells, pltpu.VMEM((LOCAL_OBS, 128), f32), pltpu.VMEM((LOCAL_OBS, 128), f32),
            pltpu.VMEM((LOCAL_OBS, 128), f32), pltpu.VMEM((256, 128), bf16),
        ],
        10**10, 5 * size, owned, lists, meta,
    )
    got = swap(returned)

    planes = lambda rows: (VARS, rows, PER_DEV, COLS)
    g, prod, outer, g_first, g_last = call(
        collect_kernel,
        [planes(ROWS), planes(12), planes(4), half, half],
        [], 10**6, 4 * size, got, chosen, mid,
    )
    g_bot = ring(g_first, True)
    g_top = ring(g_last, False)
    (inner,) = call(inner_kernel, [planes(4)], [], 10**6, 3 * size, mid, g, prod)
    (analysis,) = call(place_kernel, [shape], [], 1000, 2 * size, got)
    (gradient,) = call(
        backward_kernel,
        [shape],
        [plane_scratch(ROWS + 2 * HALO), plane_scratch(12), plane_scratch(12), plane_scratch(ROWS)],
        10**7, 6 * size, state, top, bot, g, prod, outer, inner, g_top, g_bot,
    )
    return analysis, gradient


def solution(mesh):
    placed = (
        P("member", None, "space", None),
        P("space", None),
        P("space", None),
        P("space", None),
        P("space", "member", None),
        P("member", None, "space", None),
    )
    return jax.shard_map(
        shards,
        mesh=mesh,
        in_specs=placed,
        out_specs=(P("member", None, "space", None), P("member", None, "space", None)),
        check_vma=False,
    )
```

```python
import functools
import math

import jax
import jax.numpy as jnp
from jax import lax
from jax.experimental import pallas as pl
from jax.experimental.pallas import tpu as pltpu
from jax.sharding import PartitionSpec as P

VARS = 6
ROWS = 8
COLS = 512
MEMBERS = 64
PER_DEV = 8
STRIDE = VARS * ROWS
NOBS = 2048
WINDOW = 80
LOCAL_OBS = 320
QUADS = 16
HALO = 4
TOGETHER = 8
CELLS = 48
LOC_R = 8

time_step = 0.2
HALF_STEP = 0.1
f32 = jnp.float32
bf16 = jnp.bfloat16
VMEM_LIMIT = 32 * 1024 * 1024


def call(kernel, outs, scratch, flops, moved, *args):
    spec = pl.BlockSpec(memory_space=pltpu.VMEM)
    return pl.pallas_call(
        kernel,
        out_shape=[jax.ShapeDtypeStruct(s, f32) for s in outs],
        in_specs=[spec] * len(args),
        out_specs=[spec] * len(outs),
        scratch_shapes=scratch,
        compiler_params=pltpu.CompilerParams(vmem_limit_bytes=VMEM_LIMIT),
        cost_estimate=pl.CostEstimate(flops=flops, bytes_accessed=moved, transcendentals=0),
    )(*args)


def lane_shift(q, by):
    return pltpu.roll(q, by % COLS, 1)


def col_diff(q):
    near = lane_shift(q, -1) - lane_shift(q, 1)
    far = lane_shift(q, -2) - lane_shift(q, 2)
    return near * (8.0 / 12.0) - far * (1.0 / 12.0)


def row_diff(ref, v, i):
    near = ref[v, i + 1] - ref[v, i - 1]
    far = ref[v, i + 2] - ref[v, i - 2]
    return near * (8.0 / 12.0) - far * (1.0 / 12.0)


def tendency(ref, i):
    rates = [None] * VARS
    for l in range(2):
        u, v, b = ref[l, i], ref[2 + l, i], ref[4 + l, i]
        ru, rv, rb = (row_diff(ref, k + l, i) for k in (0, 2, 4))
        cu, cv, cb = col_diff(u), col_diff(v), col_diff(b)
        rates[l] = 0.5 * v - (u * ru + v * cu) - rb + 0.3 * (ref[1 - l, i] - u)
        rates[2 + l] = -0.5 * u - (u * rv + v * cv) - cb + 0.3 * (ref[3 - l, i] - v)
        rates[4 + l] = -(u * rb + v * cb) - (ru + cv) + 0.3 * (ref[5 - l, i] - b)
    return rates


def planes_of(x_ref, v):
    return jnp.swapaxes(x_ref[:, v], 0, 1)


def edge_kernel(x_ref, first_ref, last_ref):
    for v in range(VARS):
        planes = planes_of(x_ref, v)
        first_ref[HALO * v : HALO * v + HALO] = planes[:HALO]
        last_ref[HALO * v : HALO * v + HALO] = planes[ROWS - HALO :]


def pack_planes(even, odd, store):
    low = lax.broadcasted_iota(jnp.int32, (PER_DEV, 128), 1) < 64
    for t in range(4):
        a, b = even[:, 128 * t : 128 * t + 128], odd[:, 128 * t : 128 * t + 128]
        store(2 * t, jnp.where(low, a, pltpu.roll(b, 64, 1)))
        store(2 * t + 1, jnp.where(low, pltpu.roll(a, 64, 1), b))


def unpack_planes(load):
    low = lax.broadcasted_iota(jnp.int32, (PER_DEV, 128), 1) < 64
    even, odd = [], []
    for t in range(4):
        a, b = load(2 * t), load(2 * t + 1)
        even.append(jnp.where(low, a, pltpu.roll(b, 64, 1)))
        odd.append(jnp.where(low, pltpu.roll(a, 64, 1), b))
    return jnp.concatenate(even, axis=1), jnp.concatenate(odd, axis=1)


def cot_kernel(x_ref, out_ref):
    for v in range(VARS):
        planes = planes_of(x_ref, v)
        for r in range(4):

            def store(d, value, t=v * 4 + r):
                out_ref[d, t] = value

            pack_planes(planes[2 * r], planes[2 * r + 1], store)


def load_state(s_ref, x_ref, top_ref, bot_ref):
    for v in range(VARS):
        s_ref[v, HALO : HALO + ROWS] = planes_of(x_ref, v)
        for r in range(HALO):
            s_ref[v, r] = top_ref[v * HALO + r]
            s_ref[v, HALO + ROWS + r] = bot_ref[v * HALO + r]


def forward_kernel(x_ref, top_ref, bot_ref, sel_ref, cot_ref, out_ref, mid_ref, s_ref, fore_ref):
    for d in range(8):
        out_ref[d, 28:] = cot_ref[d]
    load_state(s_ref, x_ref, top_ref, bot_ref)

    def middle(i, carry):
        rates = tendency(s_ref, i + 2)
        for v in range(VARS):
            mid_ref[v, i] = s_ref[v, i + 2] + time_step * rates[v]
        return carry

    lax.fori_loop(0, 12, middle, 0, unroll=4)

    def finish(i, carry):
        rates = tendency(mid_ref, i + 2)
        for v in range(VARS):
            fore_ref[v, i] = 0.5 * (s_ref[v, i + HALO] + mid_ref[v, i + 2]) + 0.5 * time_step * rates[v]
        return carry

    lax.fori_loop(0, ROWS, finish, 0, unroll=4)

    def pack(v, carry):
        for r in range(4):

            def store(d, value, r=r):
                out_ref[d, v * 4 + r] = value

            pack_planes(fore_ref[v, 2 * r], fore_ref[v, 2 * r + 1], store)
        return carry

    lax.fori_loop(0, VARS, pack, 0, unroll=2)

    for o in range(4):
        chosen = jnp.broadcast_to(sel_ref[o : o + 1, :], (PER_DEV, COLS))

        def pick(v, acc, chosen=chosen):
            for r in range(ROWS):
                acc = jnp.where(chosen == v * ROWS + r, fore_ref[v, r], acc)
            return acc

        seen = lax.fori_loop(0, VARS, pick, jnp.zeros((PER_DEV, COLS), f32), unroll=2)
        for d in range(8):
            out_ref[d, 24 + o] = lane_shift(seen, 8 - 64 * d)[:, :128]


def place_kernel(got_ref, out_ref):
    for v in range(VARS):
        planes = []
        for r in range(4):
            planes.extend(unpack_planes(lambda d: got_ref[d, 28 + v * 4 + r]))
        out_ref[:, v] = jnp.swapaxes(jnp.stack(planes), 0, 1)


def pull_products(s_ref, s_at, g_ref, prod_ref, prod_at, count):
    def body(i, carry):
        for l in range(2):
            u = s_ref[l, i + s_at]
            gu, gv, gb = g_ref[l, i], g_ref[2 + l, i], g_ref[4 + l, i]
            prod_ref[l, i + prod_at] = u * gu + gb
            prod_ref[2 + l, i + prod_at] = u * gv
            prod_ref[4 + l, i + prod_at] = u * gb + gu
        return carry

    lax.fori_loop(0, count, body, 0, unroll=2)


def pull_row(s_ref, s_at, g_ref, g_at, prod_ref, prod_at):
    out = [None] * VARS
    for l in range(2):
        u, v, b = (s_ref[k + l, s_at] for k in (0, 2, 4))
        gu, gv, gb = (g_ref[k + l, g_at] for k in (0, 2, 4))
        ru, rv, rb = (row_diff(s_ref, k + l, s_at) for k in (0, 2, 4))
        cu, cv, cb = col_diff(u), col_diff(v), col_diff(b)
        pu, pv, pb = (row_diff(prod_ref, k + l, prod_at) for k in (0, 2, 4))
        out[l] = (
            pu + col_diff(v * gu)
            - (gu * ru + gv * rv + gb * rb) - 0.5 * gv + 0.3 * (g_ref[1 - l, g_at] - gu)
        )
        out[2 + l] = (
            pv + col_diff(v * gv + gb)
            - (gu * cu + gv * cv + gb * cb) + 0.5 * gu + 0.3 * (g_ref[3 - l, g_at] - gv)
        )
        out[4 + l] = pb + col_diff(v * gb + gv) + 0.3 * (g_ref[5 - l, g_at] - gb)
    return out


def collect_kernel(got_ref, sel_ref, mid_ref, g_ref, prod_ref, edge_ref, first_ref, last_ref):
    lane = lax.broadcasted_iota(jnp.int32, (PER_DEV, 128), 1)
    sums, chosen = [], []
    for o in range(4):
        total = jnp.zeros((PER_DEV, COLS), f32)
        for d in range(8):
            piece = jnp.where(lane < WINDOW, got_ref[d, 24 + o], 0.0)
            wide = jnp.concatenate([piece, jnp.zeros((PER_DEV, COLS - 128), f32)], axis=1)
            total = total + lane_shift(wide, 64 * d - 8)
        sums.append(total)
        chosen.append(jnp.broadcast_to(sel_ref[o : o + 1, :], (PER_DEV, COLS)))

    for v in range(VARS):
        for r in range(4):
            pair = unpack_planes(lambda d: got_ref[d, v * 4 + r])
            for k in range(2):
                row = 2 * r + k
                value = pair[k]
                for o in range(4):
                    value = value + jnp.where(chosen[o] == v * ROWS + row, sums[o], 0.0)
                g_ref[v, row] = value

    for v in range(VARS):
        for r in (0, 1, 10, 11):
            prod_ref[v, r] = jnp.zeros((PER_DEV, COLS), f32)
    pull_products(mid_ref, 2, g_ref, prod_ref, 2, ROWS)
    for n, r in enumerate((0, 1, 6, 7)):
        got = pull_row(mid_ref, r + 2, g_ref, r, prod_ref, r + 2)
        to_ref = first_ref if r < 2 else last_ref
        for v in range(VARS):
            pulled = HALF_STEP * got[v]
            edge_ref[v, n] = pulled
            to_ref[2 * v + n % 2] = HALF_STEP * g_ref[v, r] + time_step * pulled
            to_ref[12 + 2 * v + n % 2] = prod_ref[v, r + 2]


def inner_kernel(mid_ref, g_ref, prod_ref, out_ref):
    for r in range(2, 6):
        got = pull_row(mid_ref, r + 2, g_ref, r, prod_ref, r + 2)
        for v in range(VARS):
            out_ref[v, r - 2] = HALF_STEP * got[v]


def backward_kernel(
    x_ref, top_ref, bot_ref, g_ref, prod_ref, edge_ref, inner_ref, from_top_ref, from_bot_ref,
    out_ref, s_ref, h_ref, prod2_ref, total_ref,
):
    load_state(s_ref, x_ref, top_ref, bot_ref)
    near, far = 8.0 / 12.0, 1.0 / 12.0
    for v in range(VARS):
        p = [prod_ref[v, 2 + r] for r in (0, 1, 6, 7)]
        t = [from_top_ref[12 + 2 * v + k] for k in range(2)]
        b = [from_bot_ref[12 + 2 * v + k] for k in range(2)]
        step = time_step * HALF_STEP
        h_ref[v, 0] = from_top_ref[2 * v] - (step * far) * p[0]
        h_ref[v, 1] = from_top_ref[2 * v + 1] + step * (near * p[0] - far * p[1])
        h_ref[v, 10] = from_bot_ref[2 * v] + step * (far * p[2] - near * p[3])
        h_ref[v, 11] = from_bot_ref[2 * v + 1] + (step * far) * p[3]
        pulled = [
            edge_ref[v, 0] + HALF_STEP * (far * t[0] - near * t[1]),
            edge_ref[v, 1] + (HALF_STEP * far) * t[1],
            *(inner_ref[v, k] for k in range(4)),
            edge_ref[v, 2] - (HALF_STEP * far) * b[0],
            edge_ref[v, 3] + HALF_STEP * (near * b[0] - far * b[1]),
        ]
        for r in range(ROWS):
            g = g_ref[v, r]
            h_ref[v, 2 + r] = HALF_STEP * g + time_step * pulled[r]
            total_ref[v, r] = g + pulled[r]

    pull_products(s_ref, HALO - 2, h_ref, prod2_ref, 0, ROWS + 4)

    def first(i, carry):
        got = pull_row(s_ref, i + HALO, h_ref, i + 2, prod2_ref, i + 2)
        for v in range(VARS):
            total_ref[v, i] = total_ref[v, i] + got[v]
        return carry

    lax.fori_loop(0, ROWS, first, 0, unroll=4)
    for v in range(VARS):
        out_ref[:, v] = jnp.swapaxes(total_ref[v], 0, 1)


def halves(x):
    high = x.astype(bf16)
    return high, (x - high.astype(f32)).astype(bf16)


def dot(a, b):
    return lax.dot_general(a, b, (((1,), (0,)), ((), ())), preferred_element_type=f32)


def dot_first(a, b):
    return lax.dot_general(a, b, (((0,), (0,)), ((), ())), preferred_element_type=f32)


def times(left, right, more_left=None, more_right=None):
    n = left[0].shape[0]
    out = []
    for p in range(2):
        at = slice(128 * p, 128 * p + 128)
        rows = [x[:, at] for x in left]
        weights = right[p]
        if more_left is not None:
            rows = [jnp.concatenate([r, x[:, at]], axis=1) for r, x in zip(rows, more_left)]
            weights = jnp.concatenate([weights, more_right[p]], axis=0)
        if more_left is None:
            zero = jnp.zeros((128, 128), bf16)
            deep = jnp.concatenate([weights[:, :128], zero], axis=1)
            both = dot(jnp.concatenate(rows, axis=1), jnp.concatenate([weights, deep], axis=0))
            out.append(both[:, :128] + both[:, 128:])
            continue
        both = dot(jnp.concatenate(rows, axis=0), weights)
        high, low = both[:n], both[n:, :128]
        out.append(high[:, :128] + (high[:, 128:] + low))
    return jnp.concatenate(out, axis=1)


def in_step(jobs):
    results = [None] * len(jobs)
    left = list(range(len(jobs)))
    while left:
        for n in list(left):
            try:
                next(jobs[n])
            except StopIteration as done:
                results[n] = done.value
                left.remove(n)
    return results


def stack(*parts):
    return tuple(jnp.concatenate(p, axis=0) for p in zip(*parts))


def analysis_kernel(
    got_ref, list_ref, meta_ref, out_ref, x_ref, c_ref, y_ref, d_ref, go_ref, block_ref
):
    width = 4 * MEMBERS
    block_row = lax.broadcasted_iota(jnp.int32, (width, 128), 0) // MEMBERS % 2
    block_col = lax.broadcasted_iota(jnp.int32, (width, 128), 1) // MEMBERS
    block_ref[...] = jnp.where(block_row == block_col, 1.0, 0.0).astype(bf16)

    top_half = lax.broadcasted_iota(jnp.int32, (8, 128), 0) < 4

    for first, dst in ((0, x_ref), (28, c_ref)):

        def turn(v, carry, first=first, dst=dst):
            for h in range(2):
                tall = [got_ref[s, first + v * 4 + 2 * h + k] for k in range(2) for s in range(8)]
                tall = jnp.concatenate(tall, axis=0).T
                for p in range(QUADS // 2):
                    upper, lower = tall[8 * p : 8 * p + 8], tall[64 + 8 * p : 72 + 8 * p]
                    at = slice(128 * h, 128 * h + 128)
                    dst[v, 2 * p, :, at] = jnp.where(top_half, upper, pltpu.roll(lower, 4, 0))
                    dst[v, 2 * p + 1, :, at] = jnp.where(top_half, pltpu.roll(upper, 4, 0), lower)
            return carry

        lax.fori_loop(0, VARS, turn, 0, unroll=6)

    for o in range(4):
        tall = [got_ref[s, 24 + o] for s in range(8)]
        seen = jnp.concatenate(tall + tall, axis=0).T[:WINDOW]
        mean = jnp.sum(seen, axis=1, keepdims=True) * (1.0 / 128.0)
        spread = seen - mean
        at = pl.ds(o, WINDOW, stride=4)
        y_ref[at, :] = spread
        d_ref[at, :] = meta_ref[0, at, :] - mean
    go_ref[...] = jnp.zeros(go_ref.shape, f32)

    def block_of(pair):
        mask = block_ref[:128]
        out = []
        for p in range(2):
            parts = [x[:, 128 * p : 128 * p + 128] for x in pair]
            parts = [jnp.concatenate([x, x], axis=0) * mask for x in parts]
            out.append(jnp.concatenate(parts, axis=1))
        return out

    def block_sum(x):
        parts = halves(x)
        out = []
        for p in range(2):
            wide = jnp.concatenate([x[:, 128 * p : 128 * p + 128] for x in parts], axis=1)
            out.append(dot(wide, block_ref[...]))
        return jnp.concatenate(out, axis=1)

    def row_sum(x):
        return block_sum(jnp.broadcast_to(jnp.sum(x, axis=0, keepdims=True), (8, width)))

    lane = lax.broadcasted_iota(jnp.int32, (MEMBERS, width), 1)
    sub = lax.broadcasted_iota(jnp.int32, (MEMBERS, width), 0)
    identity = jnp.where(lane % MEMBERS == sub, 1.0, 0.0)
    entry = lax.broadcasted_iota(jnp.int32, (WINDOW, width), 0)
    patch_row = (lax.broadcasted_iota(jnp.int32, (WINDOW, width), 1) // MEMBERS).astype(f32)
    col_gap = (entry // 4).astype(f32) - 9.5
    col_gap_sq = col_gap * col_gap
    row8 = lax.broadcasted_iota(jnp.int32, (8, width), 0)
    row16 = lax.broadcasted_iota(jnp.int32, (16, width), 0)

    def hits_of(quad):
        lists = list_ref[pl.ds(quad, 1), :]
        return jnp.where(jnp.broadcast_to(lists, (WINDOW, width)) == entry, 1.0, 0.0).astype(bf16)

    def solve(quad, count):
        at = pl.ds(pl.multiple_of(16 * quad, 16), WINDOW)
        obs_row = jnp.concatenate([meta_ref[1, at, :]] * 2, axis=1)
        error = jnp.concatenate([meta_ref[2, at, :]] * 2, axis=1)
        row_gap = obs_row - 2.0 * patch_row - 0.5
        weight = count * jnp.exp((row_gap * row_gap + col_gap_sq) * (-1.0 / (2.0 * LOC_R * LOC_R))) / error
        y = y_ref[at, :]
        scaled = weight * jnp.concatenate([y, y], axis=1)
        d = d_ref[at, :]
        gain = weight * jnp.concatenate([d, d], axis=1)
        scaled_pair = halves(scaled)
        yh, yl = halves(y[:, :MEMBERS])
        sh, sl = scaled_pair
        gram = dot_first(jnp.concatenate([yh, yl, yh], axis=0), jnp.concatenate([sh, sh, sl], axis=0))
        gram = gram + (MEMBERS - 1.0) * identity
        yield
        inv = lax.rsqrt(row_sum(gram * gram))
        yield
        t0 = gram * inv[:1]
        forcing = jnp.sum(scaled * jnp.concatenate([d, d], axis=1), axis=0, keepdims=True)

        m0 = 1.5 * identity - 0.5 * t0
        z1 = halves(m0)
        r0 = block_of(z1)
        t0p = halves(t0)
        u0 = halves(times(t0p, r0))
        yield
        t1f = times(u0, r0)
        yield
        t1 = halves(t1f)
        r1 = block_of(halves(1.5 * identity - 0.5 * t1f))
        both = times(stack(z1, t1), r1)
        yield
        z2, u1 = halves(both[:MEMBERS]), halves(both[MEMBERS:])
        t2f = times(u1, r1)
        yield
        t2 = halves(t2f)
        r2 = block_of(halves(1.5 * identity - 0.5 * t2f))
        both = times(stack(z2, t2), r2)
        yield
        z3, u2 = halves(both[:MEMBERS]), halves(both[MEMBERS:])
        t3f = times(u2, r2)
        yield
        r3 = block_of(halves(1.5 * identity - 0.5 * t3f))
        z4 = block_of(halves(times(z3, r3)))
        yield
        state = (t0, t0p, u0, t1, u1, t2, u2, z1, z2, z3, r0, r1, r2, r3)
        return at, inv, z4, forcing, scaled, scaled_pair, gain, state

    def pull_root(e, state):
        t0, t0p, u0, t1, u1, t2, u2, z1, z2, z3, r0, r1, r2, r3 = state
        dt0 = halves(e)
        dm = halves(-0.5 * e)
        s0 = block_of(dm)
        du0 = halves(times(dt0, r0, t0p, s0))
        yield
        dt1f = times(du0, r0, u0, s0)
        yield
        dt1 = halves(dt1f)
        s1 = block_of(halves(-0.5 * dt1f))
        both = times(stack(dm, dt1), r1, stack(z1, t1), s1)
        yield
        dz2, du1 = halves(both[:MEMBERS]), halves(both[MEMBERS:])
        dt2f = times(du1, r1, u1, s1)
        yield
        dt2 = halves(dt2f)
        s2 = block_of(halves(-0.5 * dt2f))
        both = times(stack(dz2, dt2), r2, stack(z2, t2), s2)
        yield
        dz3, du2 = halves(both[:MEMBERS]), halves(both[MEMBERS:])
        dt3f = times(du2, r2, u2, s2)
        yield
        s3 = block_of(halves(-0.5 * dt3f))
        got = times(dz3, r3, z3, s3)
        yield
        return got

    def fold(x):
        x = x[:, :128] + x[:, 128:]
        return x + pltpu.roll(x, 64, 1)

    def one_quad(quad, count, x, c, centre, c_sum):
        a = x - centre
        g_mean = jnp.sum(a * c_sum, axis=0, keepdims=True)
        at, inv, z4, forcing, scaled, scaled_pair, gain, state = yield from solve(quad, count)
        inv = inv[:1]
        alpha = math.sqrt(MEMBERS - 1.0) * jnp.sqrt(inv)
        few = jnp.where(row16 == 0, forcing, jnp.where(row16 == 1, g_mean, 0.0))
        both = times(halves(jnp.concatenate([a, c, few], axis=0)), z4)
        yield
        few = both[2 * CELLS :]
        half_way, g_half = few[:1], few[1:2] * inv
        few = times(halves(few * jnp.where(row16 == 1, inv, 1.0)), z4)
        yield
        mean_weight, g_forcing = few[:1] * inv, few[1:2]
        moved = alpha * both[:CELLS]
        update = centre + moved + block_sum(a * mean_weight)
        for v in range(VARS):
            x_ref[v, quad] = update[8 * v : 8 * v + 8]
        yield
        pull = alpha * both[CELLS : 2 * CELLS] + c_sum * mean_weight
        left = jnp.where(row8 == 0, g_mean * inv, jnp.where(row8 == 1, g_half, 0.0))
        right = jnp.where(row8 == 0, half_way, jnp.where(row8 == 1, forcing, 0.0))
        scaled_a = a * alpha
        lhs = halves(jnp.concatenate([scaled_a, c, left, right], axis=0))
        rhs = halves(jnp.concatenate([c, scaled_a, right, left], axis=0))
        e = []
        for p in range(2):
            part = slice(128 * p, 128 * p + 128)
            tall = jnp.concatenate([x[:, part] for x in lhs], axis=1)
            wide = jnp.concatenate([x[:, part] for x in rhs], axis=1)
            full = dot_first(tall, wide)
            full = full[:128, :128] + (full[:128, 128:] + full[128:, :128])
            e.append(jnp.where(lane[:, :128] < MEMBERS, full[:64], full[64:]))
        e = jnp.concatenate(e, axis=1) * 0.5
        yield
        g_root = yield from pull_root(e, state)
        t0 = state[0]
        loss = jnp.sum(c * moved, axis=0, keepdims=True) * 0.5
        loss = loss + g_mean * mean_weight + jnp.sum(g_root * t0, axis=0, keepdims=True)
        loss = block_sum(jnp.broadcast_to(loss, (8, width)))
        yield
        g_gram = (g_root - loss[:1] * t0) * inv
        g_y = 2.0 * times(scaled_pair, block_of(halves(g_gram))) + gain * g_forcing
        yield
        g_d = scaled * g_forcing
        low = lax.broadcasted_iota(jnp.int32, (WINDOW, 128), 1) < 64
        go_ref[at, :] += jnp.where(low, fold(g_y), fold(g_d))
        return pull

    def group(g, carry):
        quads = [TOGETHER * g + k for k in range(TOGETHER)]
        hits = jnp.concatenate([hits_of(q) for q in quads], axis=0)
        counts = [dot(hits[:, 128 * p : 128 * p + 128], block_ref[:128]) for p in range(2)]
        counts = jnp.concatenate(counts, axis=1)
        cells = [ref[v, q] for q in quads for ref in (x_ref, c_ref) for v in range(VARS)]
        cells = jnp.concatenate(cells, axis=0)
        sums = block_sum(cells)
        jobs, c_sums = [], []
        for k, q in enumerate(quads):
            low, mid, high = (CELLS * n for n in (2 * k, 2 * k + 1, 2 * k + 2))
            count = counts[WINDOW * k : WINDOW * k + WINDOW]
            centre, c_sum = sums[low:mid] * (1.0 / MEMBERS), sums[mid:high]
            jobs.append(one_quad(q, count, cells[low:mid], cells[mid:high], centre, c_sum))
            c_sums.append(c_sum)
        pulls = jnp.concatenate(in_step(jobs), axis=0)
        pulls = pulls + (jnp.concatenate(c_sums, axis=0) - block_sum(pulls)) * (1.0 / MEMBERS)
        for k, q in enumerate(quads):
            for v in range(VARS):
                c_ref[v, q] = pulls[CELLS * k + 8 * v : CELLS * k + 8 * v + 8]
        return carry

    lax.fori_loop(0, QUADS // TOGETHER, group, 0)

    for src, first in ((x_ref, 28), (c_ref, 0)):

        def turn_back(v, carry, src=src, first=first):
            for h in range(2):
                upper, lower = [], []
                for p in range(QUADS // 2):
                    a, b = (src[v, 2 * p + k, :, 128 * h : 128 * h + 128] for k in range(2))
                    upper.append(jnp.where(top_half, a, pltpu.roll(b, 4, 0)))
                    lower.append(jnp.where(top_half, pltpu.roll(a, 4, 0), b))
                tall = jnp.concatenate(upper + lower, axis=0).T
                for k in range(2):
                    for s in range(8):
                        at = 64 * k + 8 * s
                        out_ref[s, first + v * 4 + 2 * h + k] = tall[at : at + 8]
            return carry

        lax.fori_loop(0, VARS, turn_back, 0, unroll=6)

    for o in range(4):
        got = go_ref[pl.ds(o, WINDOW, stride=4), :]
        got = got - jnp.sum(got, axis=1, keepdims=True) * (1.0 / MEMBERS)
        tall = jnp.concatenate([got, jnp.zeros((128 - WINDOW, 128), f32)], axis=0).T
        for s in range(8):
            out_ref[s, 24 + o] = tall[8 * s : 8 * s + 8]


def ring(value, up):
    count = lax.axis_size("space")
    if up:
        pairs = [((i + 1) % count, i) for i in range(count)]
    else:
        pairs = [(i, (i + 1) % count) for i in range(count)]
    return lax.ppermute(value, "space", pairs)


def swap(value):
    return lax.all_to_all(value, "member", split_axis=0, concat_axis=0, tiled=True)


def plane_scratch(rows):
    return pltpu.VMEM((VARS, rows, PER_DEV, COLS), f32)


def shards(initial_ensemble, obs_value, obs_error, obs_location, patch_obs, cotangent):
    shape = initial_ensemble.shape
    edge = (VARS * HALO, PER_DEV, COLS)
    half = (VARS * 4, PER_DEV, COLS)
    size = 4 * PER_DEV * STRIDE * COLS

    state = initial_ensemble
    first, last = call(edge_kernel, [edge, edge], [], 1000, 2 * size, state)
    bot = ring(first, True)
    top = ring(last, False)

    position = lax.axis_index("member") * (NOBS // 8)
    plane = obs_location[0] // COLS
    chosen = plane.reshape(COLS, 4).T
    meta = jnp.stack([obs_value[0], (plane % ROWS).astype(f32), obs_error[0]])
    meta = jnp.concatenate([meta[:, -32:], meta, meta[:, :32]], axis=1)
    meta = lax.dynamic_slice_in_dim(meta, position, LOCAL_OBS, axis=1)
    meta = jnp.broadcast_to(meta[:, :, None], (3, LOCAL_OBS, 128))
    lists = (patch_obs[0] - position + 32) % NOBS
    lists = lists.reshape(QUADS, 256) - 16 * jnp.arange(QUADS, dtype=jnp.int32)[:, None]
    chosen, meta, lists, cotangent = lax.optimization_barrier((chosen, meta, lists, cotangent))
    (cot_sent,) = call(cot_kernel, [(8, 24, PER_DEV, 128)], [], 1000, 2 * size, cotangent)

    sent, mid = call(
        forward_kernel,
        [(8, 52, PER_DEV, 128), (VARS, 12, PER_DEV, COLS)],
        [plane_scratch(ROWS + 2 * HALO), plane_scratch(ROWS)],
        10**7, 6 * size, state, top, bot, chosen, cot_sent,
    )
    owned = swap(sent)

    cells = pltpu.VMEM((VARS, QUADS, 8, 256), f32)
    (returned,) = call(
        analysis_kernel,
        [(8, 52, PER_DEV, 128)],
        [
            cells, cells, pltpu.VMEM((LOCAL_OBS, 128), f32), pltpu.VMEM((LOCAL_OBS, 128), f32),
            pltpu.VMEM((LOCAL_OBS, 128), f32), pltpu.VMEM((256, 128), bf16),
        ],
        10**10, 5 * size, owned, lists, meta,
    )
    got = swap(returned)

    planes = lambda rows: (VARS, rows, PER_DEV, COLS)
    g, prod, outer, g_first, g_last = call(
        collect_kernel,
        [planes(ROWS), planes(12), planes(4), half, half],
        [], 10**6, 4 * size, got, chosen, mid,
    )
    g_bot = ring(g_first, True)
    g_top = ring(g_last, False)
    (inner,) = call(inner_kernel, [planes(4)], [], 10**6, 3 * size, mid, g, prod)
    (analysis,) = call(place_kernel, [shape], [], 1000, 2 * size, got)
    (gradient,) = call(
        backward_kernel,
        [shape],
        [plane_scratch(ROWS + 2 * HALO), plane_scratch(12), plane_scratch(12), plane_scratch(ROWS)],
        10**7, 6 * size, state, top, bot, g, prod, outer, inner, g_top, g_bot,
    )
    return analysis, gradient


def solution(mesh):
    placed = (
        P("member", None, "space", None),
        P("space", None),
        P("space", None),
        P("space", None),
        P("space", "member", None),
        P("member", None, "space", None),
    )
    return jax.shard_map(
        shards,
        mesh=mesh,
        in_specs=placed,
        out_specs=(P("member", None, "space", None), P("member", None, "space", None)),
        check_vma=False,
    )
```

```python
import functools
import math

import jax
import jax.numpy as jnp
from jax import lax
from jax.experimental import pallas as pl
from jax.experimental.pallas import tpu as pltpu
from jax.sharding import PartitionSpec as P

VARS = 6
ROWS = 8
COLS = 512
MEMBERS = 64
PER_DEV = 8
STRIDE = VARS * ROWS
NOBS = 2048
WINDOW = 80
LOCAL_OBS = 320
QUADS = 16
HALO = 4
TOGETHER = 8
CELLS = 48
LOC_R = 8

time_step = 0.2
HALF_STEP = 0.1
f32 = jnp.float32
bf16 = jnp.bfloat16
VMEM_LIMIT = 32 * 1024 * 1024


def call(kernel, outs, scratch, flops, moved, *args):
    spec = pl.BlockSpec(memory_space=pltpu.VMEM)
    return pl.pallas_call(
        kernel,
        out_shape=[jax.ShapeDtypeStruct(s, f32) for s in outs],
        in_specs=[spec] * len(args),
        out_specs=[spec] * len(outs),
        scratch_shapes=scratch,
        compiler_params=pltpu.CompilerParams(vmem_limit_bytes=VMEM_LIMIT),
        cost_estimate=pl.CostEstimate(flops=flops, bytes_accessed=moved, transcendentals=0),
    )(*args)


def lane_shift(q, by):
    return pltpu.roll(q, by % COLS, 1)


def col_diff(q):
    near = lane_shift(q, -1) - lane_shift(q, 1)
    far = lane_shift(q, -2) - lane_shift(q, 2)
    return near * (8.0 / 12.0) - far * (1.0 / 12.0)


def row_diff(ref, v, i):
    near = ref[v, i + 1] - ref[v, i - 1]
    far = ref[v, i + 2] - ref[v, i - 2]
    return near * (8.0 / 12.0) - far * (1.0 / 12.0)


def tendency(ref, i):
    rates = [None] * VARS
    for l in range(2):
        u, v, b = ref[l, i], ref[2 + l, i], ref[4 + l, i]
        ru, rv, rb = (row_diff(ref, k + l, i) for k in (0, 2, 4))
        cu, cv, cb = col_diff(u), col_diff(v), col_diff(b)
        rates[l] = 0.5 * v - (u * ru + v * cu) - rb + 0.3 * (ref[1 - l, i] - u)
        rates[2 + l] = -0.5 * u - (u * rv + v * cv) - cb + 0.3 * (ref[3 - l, i] - v)
        rates[4 + l] = -(u * rb + v * cb) - (ru + cv) + 0.3 * (ref[5 - l, i] - b)
    return rates


def planes_of(x_ref, v):
    return jnp.swapaxes(x_ref[:, v], 0, 1)


def edge_kernel(x_ref, first_ref, last_ref):
    for v in range(VARS):
        planes = planes_of(x_ref, v)
        first_ref[HALO * v : HALO * v + HALO] = planes[:HALO]
        last_ref[HALO * v : HALO * v + HALO] = planes[ROWS - HALO :]


def pack_planes(even, odd, store):
    low = lax.broadcasted_iota(jnp.int32, (PER_DEV, 128), 1) < 64
    for t in range(4):
        a, b = even[:, 128 * t : 128 * t + 128], odd[:, 128 * t : 128 * t + 128]
        store(2 * t, jnp.where(low, a, pltpu.roll(b, 64, 1)))
        store(2 * t + 1, jnp.where(low, pltpu.roll(a, 64, 1), b))


def unpack_planes(load):
    low = lax.broadcasted_iota(jnp.int32, (PER_DEV, 128), 1) < 64
    even, odd = [], []
    for t in range(4):
        a, b = load(2 * t), load(2 * t + 1)
        even.append(jnp.where(low, a, pltpu.roll(b, 64, 1)))
        odd.append(jnp.where(low, pltpu.roll(a, 64, 1), b))
    return jnp.concatenate(even, axis=1), jnp.concatenate(odd, axis=1)


def cot_kernel(x_ref, out_ref):
    for v in range(VARS):
        planes = planes_of(x_ref, v)
        for r in range(4):

            def store(d, value, t=v * 4 + r):
                out_ref[d, t] = value

            pack_planes(planes[2 * r], planes[2 * r + 1], store)


def load_state(s_ref, x_ref, top_ref, bot_ref):
    for v in range(VARS):
        s_ref[v, HALO : HALO + ROWS] = planes_of(x_ref, v)
        for r in range(HALO):
            s_ref[v, r] = top_ref[v * HALO + r]
            s_ref[v, HALO + ROWS + r] = bot_ref[v * HALO + r]


def forward_kernel(x_ref, top_ref, bot_ref, sel_ref, cot_ref, out_ref, mid_ref, s_ref, fore_ref):
    for d in range(8):
        out_ref[d, 28:] = cot_ref[d]
    load_state(s_ref, x_ref, top_ref, bot_ref)

    def middle(i, carry):
        rates = tendency(s_ref, i + 2)
        for v in range(VARS):
            mid_ref[v, i] = s_ref[v, i + 2] + time_step * rates[v]
        return carry

    lax.fori_loop(0, 12, middle, 0, unroll=4)

    def finish(i, carry):
        rates = tendency(mid_ref, i + 2)
        for v in range(VARS):
            fore_ref[v, i] = 0.5 * (s_ref[v, i + HALO] + mid_ref[v, i + 2]) + 0.5 * time_step * rates[v]
        return carry

    lax.fori_loop(0, ROWS, finish, 0, unroll=4)

    def pack(v, carry):
        for r in range(4):

            def store(d, value, r=r):
                out_ref[d, v * 4 + r] = value

            pack_planes(fore_ref[v, 2 * r], fore_ref[v, 2 * r + 1], store)
        return carry

    lax.fori_loop(0, VARS, pack, 0, unroll=2)

    for o in range(4):
        chosen = jnp.broadcast_to(sel_ref[o : o + 1, :], (PER_DEV, COLS))

        def pick(v, acc, chosen=chosen):
            for r in range(ROWS):
                acc = jnp.where(chosen == v * ROWS + r, fore_ref[v, r], acc)
            return acc

        seen = lax.fori_loop(0, VARS, pick, jnp.zeros((PER_DEV, COLS), f32), unroll=2)
        for d in range(8):
            out_ref[d, 24 + o] = lane_shift(seen, 8 - 64 * d)[:, :128]


def place_kernel(got_ref, out_ref):
    for v in range(VARS):
        planes = []
        for r in range(4):
            planes.extend(unpack_planes(lambda d: got_ref[d, 28 + v * 4 + r]))
        out_ref[:, v] = jnp.swapaxes(jnp.stack(planes), 0, 1)


def pull_products(s_ref, s_at, g_ref, prod_ref, prod_at, count):
    def body(i, carry):
        for l in range(2):
            u = s_ref[l, i + s_at]
            gu, gv, gb = g_ref[l, i], g_ref[2 + l, i], g_ref[4 + l, i]
            prod_ref[l, i + prod_at] = u * gu + gb
            prod_ref[2 + l, i + prod_at] = u * gv
            prod_ref[4 + l, i + prod_at] = u * gb + gu
        return carry

    lax.fori_loop(0, count, body, 0, unroll=2)


def pull_row(s_ref, s_at, g_ref, g_at, prod_ref, prod_at):
    out = [None] * VARS
    for l in range(2):
        u, v, b = (s_ref[k + l, s_at] for k in (0, 2, 4))
        gu, gv, gb = (g_ref[k + l, g_at] for k in (0, 2, 4))
        ru, rv, rb = (row_diff(s_ref, k + l, s_at) for k in (0, 2, 4))
        cu, cv, cb = col_diff(u), col_diff(v), col_diff(b)
        pu, pv, pb = (row_diff(prod_ref, k + l, prod_at) for k in (0, 2, 4))
        out[l] = (
            pu + col_diff(v * gu)
            - (gu * ru + gv * rv + gb * rb) - 0.5 * gv + 0.3 * (g_ref[1 - l, g_at] - gu)
        )
        out[2 + l] = (
            pv + col_diff(v * gv + gb)
            - (gu * cu + gv * cv + gb * cb) + 0.5 * gu + 0.3 * (g_ref[3 - l, g_at] - gv)
        )
        out[4 + l] = pb + col_diff(v * gb + gv) + 0.3 * (g_ref[5 - l, g_at] - gb)
    return out


def collect_kernel(got_ref, sel_ref, mid_ref, g_ref, prod_ref, edge_ref, first_ref, last_ref):
    lane = lax.broadcasted_iota(jnp.int32, (PER_DEV, 128), 1)
    sums, chosen = [], []
    for o in range(4):
        total = jnp.zeros((PER_DEV, COLS), f32)
        for d in range(8):
            piece = jnp.where(lane < WINDOW, got_ref[d, 24 + o], 0.0)
            wide = jnp.concatenate([piece, jnp.zeros((PER_DEV, COLS - 128), f32)], axis=1)
            total = total + lane_shift(wide, 64 * d - 8)
        sums.append(total)
        chosen.append(jnp.broadcast_to(sel_ref[o : o + 1, :], (PER_DEV, COLS)))

    for v in range(VARS):
        for r in range(4):
            pair = unpack_planes(lambda d: got_ref[d, v * 4 + r])
            for k in range(2):
                row = 2 * r + k
                value = pair[k]
                for o in range(4):
                    value = value + jnp.where(chosen[o] == v * ROWS + row, sums[o], 0.0)
                g_ref[v, row] = value

    for v in range(VARS):
        for r in (0, 1, 10, 11):
            prod_ref[v, r] = jnp.zeros((PER_DEV, COLS), f32)
    pull_products(mid_ref, 2, g_ref, prod_ref, 2, ROWS)
    for n, r in enumerate((0, 1, 6, 7)):
        got = pull_row(mid_ref, r + 2, g_ref, r, prod_ref, r + 2)
        to_ref = first_ref if r < 2 else last_ref
        for v in range(VARS):
            pulled = HALF_STEP * got[v]
            edge_ref[v, n] = pulled
            to_ref[2 * v + n % 2] = HALF_STEP * g_ref[v, r] + time_step * pulled
            to_ref[12 + 2 * v + n % 2] = prod_ref[v, r + 2]


def inner_kernel(mid_ref, g_ref, prod_ref, out_ref):
    for r in range(2, 6):
        got = pull_row(mid_ref, r + 2, g_ref, r, prod_ref, r + 2)
        for v in range(VARS):
            out_ref[v, r - 2] = HALF_STEP * got[v]


def backward_kernel(
    x_ref, top_ref, bot_ref, g_ref, prod_ref, edge_ref, inner_ref, from_top_ref, from_bot_ref,
    out_ref, s_ref, h_ref, prod2_ref, total_ref,
):
    load_state(s_ref, x_ref, top_ref, bot_ref)
    near, far = 8.0 / 12.0, 1.0 / 12.0
    for v in range(VARS):
        p = [prod_ref[v, 2 + r] for r in (0, 1, 6, 7)]
        t = [from_top_ref[12 + 2 * v + k] for k in range(2)]
        b = [from_bot_ref[12 + 2 * v + k] for k in range(2)]
        step = time_step * HALF_STEP
        h_ref[v, 0] = from_top_ref[2 * v] - (step * far) * p[0]
        h_ref[v, 1] = from_top_ref[2 * v + 1] + step * (near * p[0] - far * p[1])
        h_ref[v, 10] = from_bot_ref[2 * v] + step * (far * p[2] - near * p[3])
        h_ref[v, 11] = from_bot_ref[2 * v + 1] + (step * far) * p[3]
        pulled = [
            edge_ref[v, 0] + HALF_STEP * (far * t[0] - near * t[1]),
            edge_ref[v, 1] + (HALF_STEP * far) * t[1],
            *(inner_ref[v, k] for k in range(4)),
            edge_ref[v, 2] - (HALF_STEP * far) * b[0],
            edge_ref[v, 3] + HALF_STEP * (near * b[0] - far * b[1]),
        ]
        for r in range(ROWS):
            g = g_ref[v, r]
            h_ref[v, 2 + r] = HALF_STEP * g + time_step * pulled[r]
            total_ref[v, r] = g + pulled[r]

    pull_products(s_ref, HALO - 2, h_ref, prod2_ref, 0, ROWS + 4)

    def first(i, carry):
        got = pull_row(s_ref, i + HALO, h_ref, i + 2, prod2_ref, i + 2)
        for v in range(VARS):
            total_ref[v, i] = total_ref[v, i] + got[v]
        return carry

    lax.fori_loop(0, ROWS, first, 0, unroll=4)
    for v in range(VARS):
        out_ref[:, v] = jnp.swapaxes(total_ref[v], 0, 1)


def halves(x):
    high = x.astype(bf16)
    return high, (x - high.astype(f32)).astype(bf16)


def dot(a, b):
    return lax.dot_general(a, b, (((1,), (0,)), ((), ())), preferred_element_type=f32)


def dot_first(a, b):
    return lax.dot_general(a, b, (((0,), (0,)), ((), ())), preferred_element_type=f32)


def times(left, right, more_left=None, more_right=None):
    n = left[0].shape[0]
    out = []
    for p in range(2):
        at = slice(128 * p, 128 * p + 128)
        rows = [x[:, at] for x in left]
        weights = right[p]
        if more_left is not None:
            rows = [jnp.concatenate([r, x[:, at]], axis=1) for r, x in zip(rows, more_left)]
            weights = jnp.concatenate([weights, more_right[p]], axis=0)
        if more_left is None:
            zero = jnp.zeros((128, 128), bf16)
            deep = jnp.concatenate([weights[:, :128], zero], axis=1)
            both = dot(jnp.concatenate(rows, axis=1), jnp.concatenate([weights, deep], axis=0))
            out.append(both[:, :128] + both[:, 128:])
            continue
        both = dot(jnp.concatenate(rows, axis=0), weights)
        high, low = both[:n], both[n:, :128]
        out.append(high[:, :128] + (high[:, 128:] + low))
    return jnp.concatenate(out, axis=1)


def in_step(jobs):
    results = [None] * len(jobs)
    left = list(range(len(jobs)))
    while left:
        for n in list(left):
            try:
                next(jobs[n])
            except StopIteration as done:
                results[n] = done.value
                left.remove(n)
    return results


def stack(*parts):
    return tuple(jnp.concatenate(p, axis=0) for p in zip(*parts))


def analysis_kernel(
    got_ref, list_ref, meta_ref, out_ref, x_ref, c_ref, y_ref, d_ref, go_ref, block_ref, near_ref
):
    width = 4 * MEMBERS
    block_row = lax.broadcasted_iota(jnp.int32, (width, 128), 0) // MEMBERS % 2
    block_col = lax.broadcasted_iota(jnp.int32, (width, 128), 1) // MEMBERS
    block_ref[...] = jnp.where(block_row == block_col, 1.0, 0.0).astype(bf16)

    top_half = lax.broadcasted_iota(jnp.int32, (8, 128), 0) < 4

    for first, dst in ((0, x_ref), (28, c_ref)):

        def turn(v, carry, first=first, dst=dst):
            for h in range(2):
                tall = [got_ref[s, first + v * 4 + 2 * h + k] for k in range(2) for s in range(8)]
                tall = jnp.concatenate(tall, axis=0).T
                for p in range(QUADS // 2):
                    upper, lower = tall[8 * p : 8 * p + 8], tall[64 + 8 * p : 72 + 8 * p]
                    at = slice(128 * h, 128 * h + 128)
                    dst[v, 2 * p, :, at] = jnp.where(top_half, upper, pltpu.roll(lower, 4, 0))
                    dst[v, 2 * p + 1, :, at] = jnp.where(top_half, pltpu.roll(upper, 4, 0), lower)
            return carry

        lax.fori_loop(0, VARS, turn, 0, unroll=6)

    for o in range(4):
        tall = [got_ref[s, 24 + o] for s in range(8)]
        seen = jnp.concatenate(tall + tall, axis=0).T[:WINDOW]
        mean = jnp.sum(seen, axis=1, keepdims=True) * (1.0 / 128.0)
        spread = seen - mean
        at = pl.ds(o, WINDOW, stride=4)
        y_ref[at, :] = spread
        d_ref[at, :] = meta_ref[0, at, :] - mean
    go_ref[...] = jnp.zeros(go_ref.shape, f32)

    def block_of(pair):
        mask = block_ref[:128]
        out = []
        for p in range(2):
            parts = [x[:, 128 * p : 128 * p + 128] for x in pair]
            parts = [jnp.concatenate([x, x], axis=0) * mask for x in parts]
            out.append(jnp.concatenate(parts, axis=1))
        return out

    def block_sum(x):
        parts = halves(x)
        out = []
        for p in range(2):
            wide = jnp.concatenate([x[:, 128 * p : 128 * p + 128] for x in parts], axis=1)
            out.append(dot(wide, block_ref[...]))
        return jnp.concatenate(out, axis=1)

    def row_sum(x):
        return block_sum(jnp.broadcast_to(jnp.sum(x, axis=0, keepdims=True), (8, width)))

    lane = lax.broadcasted_iota(jnp.int32, (MEMBERS, width), 1)
    sub = lax.broadcasted_iota(jnp.int32, (MEMBERS, width), 0)
    identity = jnp.where(lane % MEMBERS == sub, 1.0, 0.0)
    entry = lax.broadcasted_iota(jnp.int32, (WINDOW, width), 0)
    patch_row = (lax.broadcasted_iota(jnp.int32, (WINDOW, width), 1) // MEMBERS).astype(f32)
    col_gap = (entry // 4).astype(f32) - 9.5
    spread_sq = 2.0 * LOC_R * LOC_R
    near_col = jnp.exp(col_gap * col_gap * (-1.0 / spread_sq))
    for n in range(LOCAL_OBS // WINDOW):
        at = pl.ds(WINDOW * n, WINDOW)
        row_gap = jnp.concatenate([meta_ref[1, at, :]] * 2, axis=1) - 2.0 * patch_row - 0.5
        error = jnp.concatenate([meta_ref[2, at, :]] * 2, axis=1)
        near_ref[at, :] = jnp.exp(row_gap * row_gap * (-1.0 / spread_sq)) / error
    row8 = lax.broadcasted_iota(jnp.int32, (8, width), 0)
    row16 = lax.broadcasted_iota(jnp.int32, (16, width), 0)

    def hits_of(quad):
        lists = list_ref[pl.ds(quad, 1), :]
        return jnp.where(jnp.broadcast_to(lists, (WINDOW, width)) == entry, 1.0, 0.0).astype(bf16)

    def solve(quad, count):
        at = pl.ds(pl.multiple_of(16 * quad, 16), WINDOW)
        weight = count * (near_ref[at, :] * near_col)
        y = y_ref[at, :]
        scaled = weight * jnp.concatenate([y, y], axis=1)
        d = d_ref[at, :]
        gain = weight * jnp.concatenate([d, d], axis=1)
        scaled_pair = halves(scaled)
        yh, yl = halves(y[:, :MEMBERS])
        sh, sl = scaled_pair
        gram = dot_first(jnp.concatenate([yh, yl, yh], axis=0), jnp.concatenate([sh, sh, sl], axis=0))
        gram = gram + (MEMBERS - 1.0) * identity
        yield
        inv = lax.rsqrt(row_sum(gram * gram))
        yield
        t0 = gram * inv[:1]
        forcing = jnp.sum(scaled * jnp.concatenate([d, d], axis=1), axis=0, keepdims=True)

        m0 = 1.5 * identity - 0.5 * t0
        z1 = halves(m0)
        r0 = block_of(z1)
        t0p = halves(t0)
        u0 = halves(times(t0p, r0))
        yield
        t1f = times(u0, r0)
        yield
        t1 = halves(t1f)
        r1 = block_of(halves(1.5 * identity - 0.5 * t1f))
        both = times(stack(z1, t1), r1)
        yield
        z2, u1 = halves(both[:MEMBERS]), halves(both[MEMBERS:])
        t2f = times(u1, r1)
        yield
        t2 = halves(t2f)
        r2 = block_of(halves(1.5 * identity - 0.5 * t2f))
        both = times(stack(z2, t2), r2)
        yield
        z3, u2 = halves(both[:MEMBERS]), halves(both[MEMBERS:])
        t3f = times(u2, r2)
        yield
        r3 = block_of(halves(1.5 * identity - 0.5 * t3f))
        z4 = block_of(halves(times(z3, r3)))
        yield
        state = (t0, t0p, u0, t1, u1, t2, u2, z1, z2, z3, r0, r1, r2, r3)
        return at, inv, z4, forcing, scaled, scaled_pair, gain, state

    def pull_root(e, state):
        t0, t0p, u0, t1, u1, t2, u2, z1, z2, z3, r0, r1, r2, r3 = state
        dt0 = halves(e)
        dm = halves(-0.5 * e)
        s0 = block_of(dm)
        du0 = halves(times(dt0, r0, t0p, s0))
        yield
        dt1f = times(du0, r0, u0, s0)
        yield
        dt1 = halves(dt1f)
        s1 = block_of(halves(-0.5 * dt1f))
        both = times(stack(dm, dt1), r1, stack(z1, t1), s1)
        yield
        dz2, du1 = halves(both[:MEMBERS]), halves(both[MEMBERS:])
        dt2f = times(du1, r1, u1, s1)
        yield
        dt2 = halves(dt2f)
        s2 = block_of(halves(-0.5 * dt2f))
        both = times(stack(dz2, dt2), r2, stack(z2, t2), s2)
        yield
        dz3, du2 = halves(both[:MEMBERS]), halves(both[MEMBERS:])
        dt3f = times(du2, r2, u2, s2)
        yield
        s3 = block_of(halves(-0.5 * dt3f))
        got = times(dz3, r3, z3, s3)
        yield
        return got

    def fold(x):
        x = x[:, :128] + x[:, 128:]
        return x + pltpu.roll(x, 64, 1)

    def one_quad(quad, count, x, c, centre, c_sum):
        a = x - centre
        g_mean = jnp.sum(a * c_sum, axis=0, keepdims=True)
        at, inv, z4, forcing, scaled, scaled_pair, gain, state = yield from solve(quad, count)
        inv = inv[:1]
        alpha = math.sqrt(MEMBERS - 1.0) * jnp.sqrt(inv)
        few = jnp.where(row16 == 0, forcing, jnp.where(row16 == 1, g_mean, 0.0))
        both = times(halves(jnp.concatenate([a, c, few], axis=0)), z4)
        yield
        few = both[2 * CELLS :]
        half_way, g_half = few[:1], few[1:2] * inv
        few = times(halves(few * jnp.where(row16 == 1, inv, 1.0)), z4)
        yield
        mean_weight, g_forcing = few[:1] * inv, few[1:2]
        moved = alpha * both[:CELLS]
        update = centre + moved + block_sum(a * mean_weight)
        for v in range(VARS):
            x_ref[v, quad] = update[8 * v : 8 * v + 8]
        yield
        pull = alpha * both[CELLS : 2 * CELLS] + c_sum * mean_weight
        left = jnp.where(row8 == 0, g_mean * inv, jnp.where(row8 == 1, g_half, 0.0))
        right = jnp.where(row8 == 0, half_way, jnp.where(row8 == 1, forcing, 0.0))
        scaled_a = a * alpha
        lhs = halves(jnp.concatenate([scaled_a, c, left, right], axis=0))
        rhs = halves(jnp.concatenate([c, scaled_a, right, left], axis=0))
        e = []
        for p in range(2):
            part = slice(128 * p, 128 * p + 128)
            tall = jnp.concatenate([x[:, part] for x in lhs], axis=1)
            wide = jnp.concatenate([x[:, part] for x in rhs], axis=1)
            full = dot_first(tall, wide)
            full = full[:128, :128] + (full[:128, 128:] + full[128:, :128])
            e.append(jnp.where(lane[:, :128] < MEMBERS, full[:64], full[64:]))
        e = jnp.concatenate(e, axis=1) * 0.5
        yield
        g_root = yield from pull_root(e, state)
        t0 = state[0]
        loss = jnp.sum(c * moved, axis=0, keepdims=True) * 0.5
        loss = loss + g_mean * mean_weight + jnp.sum(g_root * t0, axis=0, keepdims=True)
        loss = block_sum(jnp.broadcast_to(loss, (8, width)))
        yield
        g_gram = (g_root - loss[:1] * t0) * inv
        g_y = 2.0 * times(scaled_pair, block_of(halves(g_gram))) + gain * g_forcing
        yield
        g_d = scaled * g_forcing
        low = lax.broadcasted_iota(jnp.int32, (WINDOW, 128), 1) < 64
        go_ref[at, :] += jnp.where(low, fold(g_y), fold(g_d))
        return pull

    def group(g, carry):
        quads = [TOGETHER * g + k for k in range(TOGETHER)]
        hits = jnp.concatenate([hits_of(q) for q in quads], axis=0)
        counts = [dot(hits[:, 128 * p : 128 * p + 128], block_ref[:128]) for p in range(2)]
        counts = jnp.concatenate(counts, axis=1)
        cells = [ref[v, q] for q in quads for ref in (x_ref, c_ref) for v in range(VARS)]
        cells = jnp.concatenate(cells, axis=0)
        sums = block_sum(cells)
        jobs, c_sums = [], []
        for k, q in enumerate(quads):
            low, mid, high = (CELLS * n for n in (2 * k, 2 * k + 1, 2 * k + 2))
            count = counts[WINDOW * k : WINDOW * k + WINDOW]
            centre, c_sum = sums[low:mid] * (1.0 / MEMBERS), sums[mid:high]
            jobs.append(one_quad(q, count, cells[low:mid], cells[mid:high], centre, c_sum))
            c_sums.append(c_sum)
        pulls = jnp.concatenate(in_step(jobs), axis=0)
        pulls = pulls + (jnp.concatenate(c_sums, axis=0) - block_sum(pulls)) * (1.0 / MEMBERS)
        for k, q in enumerate(quads):
            for v in range(VARS):
                c_ref[v, q] = pulls[CELLS * k + 8 * v : CELLS * k + 8 * v + 8]
        return carry

    lax.fori_loop(0, QUADS // TOGETHER, group, 0)

    for src, first in ((x_ref, 28), (c_ref, 0)):

        def turn_back(v, carry, src=src, first=first):
            for h in range(2):
                upper, lower = [], []
                for p in range(QUADS // 2):
                    a, b = (src[v, 2 * p + k, :, 128 * h : 128 * h + 128] for k in range(2))
                    upper.append(jnp.where(top_half, a, pltpu.roll(b, 4, 0)))
                    lower.append(jnp.where(top_half, pltpu.roll(a, 4, 0), b))
                tall = jnp.concatenate(upper + lower, axis=0).T
                for k in range(2):
                    for s in range(8):
                        at = 64 * k + 8 * s
                        out_ref[s, first + v * 4 + 2 * h + k] = tall[at : at + 8]
            return carry

        lax.fori_loop(0, VARS, turn_back, 0, unroll=6)

    for o in range(4):
        got = go_ref[pl.ds(o, WINDOW, stride=4), :]
        got = got - jnp.sum(got, axis=1, keepdims=True) * (1.0 / MEMBERS)
        tall = jnp.concatenate([got, jnp.zeros((128 - WINDOW, 128), f32)], axis=0).T
        for s in range(8):
            out_ref[s, 24 + o] = tall[8 * s : 8 * s + 8]


def ring(value, up):
    count = lax.axis_size("space")
    if up:
        pairs = [((i + 1) % count, i) for i in range(count)]
    else:
        pairs = [(i, (i + 1) % count) for i in range(count)]
    return lax.ppermute(value, "space", pairs)


def swap(value):
    return lax.all_to_all(value, "member", split_axis=0, concat_axis=0, tiled=True)


def plane_scratch(rows):
    return pltpu.VMEM((VARS, rows, PER_DEV, COLS), f32)


def shards(initial_ensemble, obs_value, obs_error, obs_location, patch_obs, cotangent):
    shape = initial_ensemble.shape
    edge = (VARS * HALO, PER_DEV, COLS)
    half = (VARS * 4, PER_DEV, COLS)
    size = 4 * PER_DEV * STRIDE * COLS

    state = initial_ensemble
    first, last = call(edge_kernel, [edge, edge], [], 1000, 2 * size, state)
    bot = ring(first, True)
    top = ring(last, False)

    position = lax.axis_index("member") * (NOBS // 8)
    plane = obs_location[0] // COLS
    chosen = plane.reshape(COLS, 4).T
    meta = jnp.stack([obs_value[0], (plane % ROWS).astype(f32), obs_error[0]])
    meta = jnp.concatenate([meta[:, -32:], meta, meta[:, :32]], axis=1)
    meta = lax.dynamic_slice_in_dim(meta, position, LOCAL_OBS, axis=1)
    meta = jnp.broadcast_to(meta[:, :, None], (3, LOCAL_OBS, 128))
    lists = (patch_obs[0] - position + 32) % NOBS
    lists = lists.reshape(QUADS, 256) - 16 * jnp.arange(QUADS, dtype=jnp.int32)[:, None]
    chosen, meta, lists, cotangent = lax.optimization_barrier((chosen, meta, lists, cotangent))
    (cot_sent,) = call(cot_kernel, [(8, 24, PER_DEV, 128)], [], 1000, 2 * size, cotangent)

    sent, mid = call(
        forward_kernel,
        [(8, 52, PER_DEV, 128), (VARS, 12, PER_DEV, COLS)],
        [plane_scratch(ROWS + 2 * HALO), plane_scratch(ROWS)],
        10**7, 6 * size, state, top, bot, chosen, cot_sent,
    )
    owned = swap(sent)

    cells = pltpu.VMEM((VARS, QUADS, 8, 256), f32)
    (returned,) = call(
        analysis_kernel,
        [(8, 52, PER_DEV, 128)],
        [
            cells, cells, pltpu.VMEM((LOCAL_OBS, 128), f32), pltpu.VMEM((LOCAL_OBS, 128), f32),
            pltpu.VMEM((LOCAL_OBS, 128), f32), pltpu.VMEM((256, 128), bf16),
            pltpu.VMEM((LOCAL_OBS, 256), f32),
        ],
        10**10, 5 * size, owned, lists, meta,
    )
    got = swap(returned)

    planes = lambda rows: (VARS, rows, PER_DEV, COLS)
    g, prod, outer, g_first, g_last = call(
        collect_kernel,
        [planes(ROWS), planes(12), planes(4), half, half],
        [], 10**6, 4 * size, got, chosen, mid,
    )
    g_bot = ring(g_first, True)
    g_top = ring(g_last, False)
    (inner,) = call(inner_kernel, [planes(4)], [], 10**6, 3 * size, mid, g, prod)
    (analysis,) = call(place_kernel, [shape], [], 1000, 2 * size, got)
    (gradient,) = call(
        backward_kernel,
        [shape],
        [plane_scratch(ROWS + 2 * HALO), plane_scratch(12), plane_scratch(12), plane_scratch(ROWS)],
        10**7, 6 * size, state, top, bot, g, prod, outer, inner, g_top, g_bot,
    )
    return analysis, gradient


def solution(mesh):
    placed = (
        P("member", None, "space", None),
        P("space", None),
        P("space", None),
        P("space", None),
        P("space", "member", None),
        P("member", None, "space", None),
    )
    return jax.shard_map(
        shards,
        mesh=mesh,
        in_specs=placed,
        out_specs=(P("member", None, "space", None), P("member", None, "space", None)),
        check_vma=False,
    )
```
